32 devices in a mesh: groups: 2 (over y), frame: 4 (over z), map: 2 (over x), psf: 2 (over core).
Axes of the slice: x: 2, y: 2, z: 4, core: 2. Of those that a mesh axis runs over, the one named last changes fastest.
Arguments:
- observed: float32 [8, 128, 512], P(('groups', 'frame'), ('map', 'psf')), parts along dimension 0, may hold values from -6 to 6
- pixel_mask: int32 [8, 128, 512], P(('groups', 'frame'), ('map', 'psf')), parts along dimension 0, may hold values 0 or 1
- ramp_counts: int32 [8, 128, 512], P(('groups', 'frame'), ('map', 'psf')), parts along dimension 0, may hold values from 1 to 16
- flat_map: float32 [8, 32, 512], P(('groups', 'map', 'psf'), 'frame'), parts along dimension 0, may hold values from 0.5 to 1.5
- bfe_map: float32 [8, 32, 512], P(('groups', 'map', 'psf'), 'frame'), parts along dimension 0, may hold values from 0.005 to 0.05
- ipc_kernel: float32 [6, 3], P('groups'), parts along dimension 0, may hold values from 0 to 0.04
- zernike: float32 [42], P('groups'), parts along dimension 0, may hold values from -2.5 to 2.5
- jitter: float32 [8], P(('groups', 'frame')), parts along dimension 0, may hold values from 4 to 20
- sky_level: float32 [8], P(('groups', 'frame')), parts along dimension 0, may hold values from 0.5 to 2
- dither: int32 [8, 2], P(('groups', 'frame')), parts along dimension 0, may hold values from -56 to 55
Outputs:
- grad_flat: float32 [8, 32, 512], P(('groups', 'map', 'psf'), 'frame'), parts along dimension 0
- grad_bfe: float32 [8, 32, 512], P(('groups', 'map', 'psf'), 'frame'), parts along dimension 0
- grad_ipc: float32 [6, 3], P('groups'), parts along dimension 0
- grad_zernike: float32 [42], P('groups'), parts along dimension 0
- grad_jitter: float32 [8], P(('groups', 'frame')), parts along dimension 0
The draws below stay inside these ranges and needn't reach their ends.
There are 2 independent parts, one for each index of `groups`. The reference program is written for one: setup_inputs(seed, part) draws one part's arguments, and reference() takes and returns one part's arrays. A program takes and returns all parts, laid end to end along the dimension named above; each array names one. Nothing has to cross between parts.
All inputs are finite; a program needn't handle non-finite values. No bound on the sum of `pixel_mask` on one device may be relied on, other than what follows from the above.
Results may differ from the reference program's by a relative error of at most 0.0003.
Values sent between devices are 32-bit elements; how exact they have to be, the bound alone decides.
No kernel may reach another device: no remote copies, remote signals or barrier semaphores. Data moves between devices by JAX's collectives and lax.ppermute only.
A program may use at most 64 MiB of HBM per device.

```python
import math
import jax
import jax.numpy as jnp
import numpy as np
from jax import lax

W = 512
NP = 256
NZ = 21
NR = 16
RD = 32
NB = 4
R = 128
NF = 4


def place_ends(result, key, smallest, top_value):
    longest = result.shape.index(max(result.shape))
    spots = []
    for shift in (0, 1):
        where = [jax.random.randint(jax.random.fold_in(key, axis), (), 0, length) for axis, length in enumerate(result.shape)]
        where[longest] = (where[longest] + shift) % result.shape[longest]
        spots.append(tuple(where))
    return result.at[spots[0]].set(smallest).at[spots[1]].set(top_value)


def shard_levels(own_key, extent, pieces, low, largest):
    loudness, own = 1.0, jax.random.fold_in(own_key, 6)
    for position, blocks in pieces:
        steps = jnp.exp(jax.random.uniform(jax.random.fold_in(own, position), (blocks,), jnp.float32, low / len(pieces), largest / len(pieces)))
        loudness = loudness * jnp.repeat(steps, extent[position] // blocks).reshape([-1 if axis == position else 1 for axis in range(len(extent))])
    return loudness


def gaussian(key, dims, width, most, cuts=(), held_as=jnp.bfloat16):
    loudness = shard_levels(key, dims, cuts, -0.22, 0.18) if cuts else 1.0
    result = jax.random.normal(key, dims, jnp.float32) * width * loudness
    return jnp.minimum(jnp.maximum(result, -most), most).astype(held_as)


def setup_inputs(seed: int = 0, part: int = 0) -> dict:
    key_list = jax.random.split(jax.random.key(seed), 11)
    part_keys = jax.random.split(jax.random.fold_in(key_list[10], part), 11)
    observed = gaussian(part_keys[0], (NF, R, W), 1.0, 6.0, ((0, 4), (1, 4)), jnp.float32)
    pixel_mask = place_ends((jax.random.randint(part_keys[1], (NF, R, W), 0, 16) < 15).astype(jnp.int32), jax.random.fold_in(part_keys[1], 1), 0, 1)
    ramp_counts = place_ends(jax.random.randint(part_keys[2], (NF, R, W), 1, NR + 1), jax.random.fold_in(part_keys[2], 1), 1, NR).astype(jnp.int32)
    flat_map = jnp.clip(1.0 + 0.1 * jax.random.normal(part_keys[3], (NB, RD, W), jnp.float32), 0.5, 1.5)
    bfe_map = jnp.clip(jnp.exp(math.log(0.05) - 2.3025851 * jax.random.uniform(part_keys[4], (NB, RD, W), jnp.float32) ** shard_levels(part_keys[4], (NB, RD, W), ((0, 4), (1, 4)), -0.2, 0.2)), 0.005, 0.05)
    ipc_kernel = jnp.clip(jax.random.uniform(part_keys[5], (3, 3), jnp.float32, 0.0, 0.04), 0.0, 0.04)
    zernike = gaussian(part_keys[6], (NZ,), 0.4, 2.5, (), jnp.float32)
    jitter = jnp.clip(jnp.exp(math.log(20.0) - 1.609438 * jax.random.uniform(part_keys[7], (NF,), jnp.float32) ** shard_levels(part_keys[7], (NF,), ((0, 4),), -0.2, 0.2)), 4.0, 20.0)
    sky_level = jnp.clip(0.5 + 1.5 * jax.random.uniform(part_keys[8], (NF,), jnp.float32) ** shard_levels(part_keys[8], (NF,), ((0, 4),), -0.2, 0.2), 0.5, 2.0)
    dither = place_ends(jax.random.randint(part_keys[9], (NF, 2), 8 - min(R, W) // 2, min(R, W) // 2 - 8), jax.random.fold_in(part_keys[9], 1), 8 - min(R, W) // 2, (min(R, W) // 2 - 8) - 1).astype(jnp.int32)
    return {"observed": observed, "pixel_mask": pixel_mask, "ramp_counts": ramp_counts, "flat_map": flat_map, "bfe_map": bfe_map, "ipc_kernel": ipc_kernel, "zernike": zernike, "jitter": jitter, "sky_level": sky_level, "dither": dither}


HIGHEST_PRECISION = lax.Precision.HIGHEST
OVERSAMPLE = 32.0
AMPLITUDE = 2.0
IPC_CENTER = 0.8

def bfe_table():
    table_values = np.zeros((5, 5))
    for i in range(5):
        for j in range(5):
            distance = (i - 2) ** 2 + (j - 2) ** 2
            if distance > 0:
                table_values[i, j] = 1.0 / distance
    table_values[2, 2] = -table_values.sum()
    return table_values / -table_values[2, 2]

def center_table():
    table_values = np.zeros((3, 3))
    table_values[1, 1] = IPC_CENTER
    return table_values

def correlate(padded, kernel):
    kernel_size = kernel.shape[0]
    half_size = kernel_size // 2
    out_rows = padded.shape[-2] - 2 * half_size
    columns = padded.shape[-1]
    extended = jnp.pad(padded, [(0, 0)] * (padded.ndim - 1) + [(half_size, half_size)])
    accum_sum = jnp.zeros(padded.shape[:-2] + (out_rows, columns), padded.dtype)
    for i in range(kernel_size):
        for j in range(kernel_size):
            accum_sum = accum_sum + kernel[i, j] * extended[..., i:i + out_rows, j:j + columns]
    return accum_sum

def pupil_modes(coords):
    mode_list = []
    for degree in range(6):
        for power in range(degree + 1):
            mode_list.append(jnp.outer(coords ** power, coords ** (degree - power)))
    return jnp.stack(mode_list, 0)

def frame_image(zernike, jitter_width, sky_value, shift_row, shift_col, row_pos, total_rows, npupil, columns):
    coords = (2.0 * jnp.arange(npupil, dtype=jnp.float32) + 1.0) / npupil - 1.0
    pupil_phase = jnp.tensordot(zernike, pupil_modes(coords), axes=1, precision=HIGHEST_PRECISION)
    radius = coords[:, None] ** 2 + coords[None, :] ** 2
    aperture = jnp.where((radius <= 1.0) & (radius >= 0.09), 1.0, 0.0).astype(jnp.float32)
    pupil_real = aperture * jnp.cos(pupil_phase)
    pupil_imag = aperture * jnp.sin(pupil_phase)
    rho = total_rows / 2.0 + shift_row.astype(jnp.float32)
    chi = columns / 2.0 + shift_col.astype(jnp.float32)
    col_pos = jnp.arange(columns, dtype=jnp.float32)
    left_angle = -math.pi * (row_pos - rho)[:, None] * coords[None, :] / OVERSAMPLE
    right_angle = -math.pi * coords[:, None] * (col_pos - chi)[None, :] / OVERSAMPLE
    left_real, left_imag = (jnp.cos(left_angle), jnp.sin(left_angle))
    right_real, right_imag = (jnp.cos(right_angle), jnp.sin(right_angle))
    mid_real = jnp.dot(left_real, pupil_real, precision=HIGHEST_PRECISION) - jnp.dot(left_imag, pupil_imag, precision=HIGHEST_PRECISION)
    mid_imag = jnp.dot(left_real, pupil_imag, precision=HIGHEST_PRECISION) + jnp.dot(left_imag, pupil_real, precision=HIGHEST_PRECISION)
    field_real = jnp.dot(mid_real, right_real, precision=HIGHEST_PRECISION) - jnp.dot(mid_imag, right_imag, precision=HIGHEST_PRECISION)
    field_imag = jnp.dot(mid_real, right_imag, precision=HIGHEST_PRECISION) + jnp.dot(mid_imag, right_real, precision=HIGHEST_PRECISION)
    intensity = (field_real * field_real + field_imag * field_imag) * (AMPLITUDE / npupil ** 2) ** 2
    offsets = col_pos[:, None] - col_pos[None, :]
    blur = jnp.exp(-offsets * offsets / (2.0 * jitter_width * jitter_width))
    blur = blur / lax.optimization_barrier(jnp.sum(blur, axis=0, keepdims=True))
    return jnp.dot(intensity, blur, precision=HIGHEST_PRECISION) + sky_value

def reference(observed, pixel_mask, ramp_counts, flat_map, bfe_map, ipc_kernel, zernike, jitter, sky_level, dither):
    frames, total_rows, columns = observed.shape
    flat_gain = flat_map.reshape(total_rows, columns)
    bfe_gain = bfe_map.reshape(total_rows, columns)
    weights = pixel_mask.astype(jnp.float32) * ramp_counts.astype(jnp.float32) / NR / math.sqrt(frames)
    row_pos = jnp.arange(total_rows, dtype=jnp.float32)
    bfe_kernel = jnp.asarray(bfe_table(), jnp.float32)
    center_kernel = jnp.asarray(center_table(), jnp.float32)

    def frame_loss(flat_gain, bfe_gain, ipc_kernel, zernike, jitter_width, sky_value, shift, observed_frame, frame_weights):
        psf_image = frame_image(zernike, jitter_width, sky_value, shift[0], shift[1], row_pos, total_rows, NP, columns)
        charge = flat_gain * psf_image
        curvature = correlate(jnp.pad(charge, ((2, 2), (0, 0))), bfe_kernel)
        spread = charge * (1.0 + bfe_gain * curvature)
        detected = correlate(jnp.pad(spread, ((1, 1), (0, 0))), ipc_kernel + center_kernel)
        residual = detected - observed_frame
        return 0.5 * jnp.sum(frame_weights * residual * residual)
    gradient_fn = jax.grad(frame_loss, argnums=(0, 1, 2, 3, 4))

    def frame_step(running, inputs):
        jitter_width, sky_value, shift, observed_frame, frame_weights = inputs
        grad_flat, grad_bfe, grad_ipc, grad_zern, grad_width = gradient_fn(flat_gain, bfe_gain, ipc_kernel, zernike, jitter_width, sky_value, shift, observed_frame, frame_weights)
        return ((running[0] + grad_flat, running[1] + grad_bfe, running[2] + grad_ipc, running[3] + grad_zern), grad_width)
    start_sums = (jnp.zeros((total_rows, columns), jnp.float32), jnp.zeros((total_rows, columns), jnp.float32), jnp.zeros((3, 3), jnp.float32), jnp.zeros(zernike.shape, jnp.float32))
    sums_out, grad_widths = lax.scan(frame_step, start_sums, (jitter, sky_level, dither, observed, weights))
    return (sums_out[0].reshape(flat_map.shape), sums_out[1].reshape(bfe_map.shape), sums_out[2], sums_out[3], grad_widths)
```

```python
import math

import jax
import jax.numpy as jnp
import numpy as np
from jax import lax
from jax.experimental import pallas as pl
from jax.experimental.pallas import tpu as pltpu
from jax.sharding import PartitionSpec as P

NP = 256
HALF = NP // 2
NR = 16
OVERSAMPLE = 32
AMPLITUDE = 2.0
IPC_CENTER = 0.8
TURN = 2 * NP * OVERSAMPLE
FIELD_SCALE = (AMPLITUDE / NP**2) ** 2
GUARD = 8
ZERN_LANE, IPC_LANE, JITTER_LANE = 0, 32, 48
JITTER, SKY, ROW_START, COLUMN, KAPPA = range(5)

f32, bf16 = jnp.float32, jnp.bfloat16
MODES = [(p, d - p) for d in range(6) for p in range(d + 1)]


def sine_table():
    nodes = 0.125 + 0.125 * np.cos(np.pi * (np.arange(200) + 0.5) / 200)
    powers = np.stack([nodes ** (2 * k + 1) for k in range(5)], 1)
    return [float(c) for c in np.linalg.lstsq(powers, np.sin(2 * np.pi * nodes), rcond=None)[0]]


SINE = sine_table()


def sin_quarter(y):
    t = y * y
    poly = SINE[4]
    for c in SINE[3::-1]:
        poly = poly * t + c
    return poly * y


def cos_turn(x):
    return sin_quarter(0.25 - jnp.abs(x))


def sin_turn(x):
    return sin_quarter(jnp.minimum(jnp.maximum(x, -0.5 - x), 0.5 - x))


def turn_fraction(k):
    return (((k + TURN // 2) & (TURN - 1)) - TURN // 2).astype(f32) * (1.0 / TURN)


def iota(shape, axis):
    return lax.broadcasted_iota(jnp.int32, shape, axis)


def mm(a, b):
    return jnp.dot(a, b, preferred_element_type=f32)


def mm_nt(a, b):
    return lax.dot_general(a, b, (((1,), (1,)), ((), ())), preferred_element_type=f32)


def halves(x):
    high = x.astype(bf16)
    return high, (x - high.astype(f32)).astype(bf16)


def dot_blur(x, high, low):
    half = high.shape[0]
    left, right = x[:, :half], x[:, half:]
    rows = x.shape[0]
    both = dot_split(jnp.concatenate([left, right], 0), high[:, half : 2 * half], low[:, half : 2 * half])
    first = both[:rows] + dot_split(right, high[:, :half], low[:, :half])
    last = both[rows:] + dot_split(left, high[:, 2 * half :], low[:, 2 * half :])
    return jnp.concatenate([first, last], 1)


def dot_split(x, high, low, product=mm):
    rows = x.shape[0]
    top = x.astype(bf16)
    both = jnp.concatenate([top.astype(f32), x - top.astype(f32)], 0).astype(bf16)
    first = product(both, high)
    return first[:rows] + first[rows:] + product(top, low)


def pupil_kernel(
    zern_ref,
    level_ref,
    dither_ref,
    ipc_ref,
    scalar_ref,
    turned_ref,
    pupil_ref,
    fold_hi,
    fold_lo,
    *,
    rows,
    columns,
):
    spread_rows = rows + GUARD
    blocks = lax.axis_size(("map", "psf"))
    row_start = lax.axis_index(("map", "psf")) * rows - rows * blocks // 2 - dither_ref[0, 0]
    column = columns // 2 + dither_ref[0, 1]
    values = [level_ref[0, 0], level_ref[0, 1], row_start.astype(f32), column.astype(f32)]
    values += [
        ipc_ref[i, j] + (IPC_CENTER if i == j == 1 else 0.0) for i in range(3) for j in range(3)
    ]
    for k, value in enumerate(values):
        scalar_ref[k : k + 1, :] = jnp.full((1, columns), value, f32)
    z = {mode: zern_ref[k] for k, mode in enumerate(MODES)}

    def pupil_step(step, carry):
        at = pl.multiple_of(step * 16, 16)
        j = iota((16, HALF), 0) + at
        l = iota((16, HALF), 1)
        u = (2 * j + 1).astype(f32) * (1.0 / NP)
        v = (2 * l + 1).astype(f32) * (1.0 / NP)
        uu, vv = u * u, v * v
        ee = (
            z[0, 0]
            + vv * (z[0, 2] + vv * z[0, 4])
            + uu * (z[2, 0] + vv * z[2, 2] + uu * z[4, 0])
        )
        oe = u * (
            z[1, 0]
            + vv * (z[1, 2] + vv * z[1, 4])
            + uu * (z[3, 0] + vv * z[3, 2] + uu * z[5, 0])
        )
        eo = v * (
            z[0, 1]
            + vv * (z[0, 3] + vv * z[0, 5])
            + uu * (z[2, 1] + vv * z[2, 3] + uu * z[4, 1])
        )
        oo = u * v * (z[1, 1] + vv * z[1, 3] + uu * z[3, 1])
        radius = uu + vv
        open_ = jnp.where((radius <= 1.0) & (radius >= 0.09), 1.0, 0.0).astype(f32)
        even, odd = (ee + eo, oe + oo), (ee - eo, oe - oo)
        phases = (even[0] + even[1], even[0] - even[1], odd[0] + odd[1], odd[0] - odd[1])
        real, imag = [], []
        for quadrant, phase in enumerate(phases):
            turns = phase * (0.5 / math.pi)
            turns = turns - jnp.floor(turns + 0.5)
            real.append(open_ * cos_turn(turns))
            imag.append(open_ * sin_turn(turns))
            pupil_ref[quadrant, pl.ds(at, 16), :] = real[-1]
            pupil_ref[4 + quadrant, pl.ds(at, 16), :] = imag[-1]

        def folds(x):
            a, b, c, d = x[0] + x[1], x[0] - x[1], x[2] + x[3], x[2] - x[3]
            return a + c, a - c, b + d, b - d

        ree, reo, roe, roo = folds(real)
        iee, ieo, ioe, ioo = folds(imag)
        for first, parts in ((0, (ree, iee, reo, ieo)), (HALF, (ioe, -roe, ioo, -roo))):
            for k, part in enumerate(parts):
                high, low = halves(part)
                fold_hi[pl.ds(first + at, 16), k * HALF : (k + 1) * HALF] = high
                fold_lo[pl.ds(first + at, 16), k * HALF : (k + 1) * HALF] = low
        return carry

    lax.fori_loop(0, HALF // 16, pupil_step, 0)

    at = iota((HALF, HALF), 1)
    part = (at >= spread_rows).astype(jnp.int32) + (at >= 2 * spread_rows).astype(jnp.int32)
    i = at - part * spread_rows
    i = jnp.where(i < rows + 4, i, i - spread_rows)
    x = turn_fraction((2 * iota((HALF, HALF), 0) + 1) * (i + row_start))
    for first, value in ((0, cos_turn(x)), (HALF, sin_turn(x))):
        high = value.astype(bf16).astype(f32)
        value = jnp.where(part == 1, value - high, high)
        turned_ref[first : first + HALF, :] = value.astype(bf16)


def table_kernel(
    scalar_ref,
    norm_ref,
    mean_ref,
    blur_hi,
    blur_lo,
    wide_hi,
    wide_lo,
    col_hi,
    col_lo,
    *,
    columns,
):
    def column_step(step, carry):
        at = pl.multiple_of(step * 16, 16)
        l = iota((16, columns), 0) + at
        c = iota((16, columns), 1) - scalar_ref[COLUMN : COLUMN + 1, :].astype(jnp.int32)
        x = turn_fraction((2 * l + 1) * c)
        high, low = halves(cos_turn(x))
        col_hi[pl.ds(at, 16), :] = high
        col_lo[pl.ds(at, 16), :] = low
        high, low = halves(sin_turn(x))
        col_hi[pl.ds(HALF + at, 16), :] = high
        col_lo[pl.ds(HALF + at, 16), :] = low
        return carry

    lax.fori_loop(0, HALF // 16, column_step, 0)

    jitter = scalar_ref[JITTER : JITTER + 1, : columns // 2]
    falloff = 0.5 / (jitter * jitter)
    falloff = jnp.concatenate([falloff] * 3, 1)

    half = columns // 2

    def blur_step(step, carry):
        total, wide_total = carry
        at = pl.multiple_of(step * 16, 16)
        d = (iota((16, 3 * half), 0) + at - iota((16, 3 * half), 1) + half).astype(f32)
        exponent = d * d * falloff
        value = jnp.exp(-exponent)
        wide = value * (exponent + exponent)
        high, low = halves(value)
        blur_hi[pl.ds(at, 16), :] = high
        blur_lo[pl.ds(at, 16), :] = low
        high, low = halves(wide)
        wide_hi[pl.ds(at, 16), :] = high
        wide_lo[pl.ds(at, 16), :] = low
        return total + value, wide_total + wide

    zero = jnp.zeros((16, 3 * half), f32)
    total, wide_total = lax.fori_loop(0, half // 16, blur_step, (zero, zero))
    total = jnp.sum(total, 0, keepdims=True)
    wide_total = jnp.sum(wide_total, 0, keepdims=True)
    norm = 1.0 / (total[:, half:] + total[:, : 2 * half])
    mean = (wide_total[:, half:] + wide_total[:, : 2 * half]) * norm
    norm_ref[...] = jnp.broadcast_to(norm, (8, columns))
    mean_ref[...] = jnp.broadcast_to(mean, (8, columns))


def field_kernel(
    scalar_ref,
    observed_any,
    mask_any,
    count_any,
    fold_hi,
    fold_lo,
    norm_ref,
    mean_ref,
    blur_hi,
    blur_lo,
    wide_hi,
    wide_lo,
    col_hi,
    col_lo,
    observed_ref,
    weight_ref,
    image_ref,
    width_ref,
    field_ref,
    observed_in,
    mask_in,
    count_in,
    sems,
    *,
    rows,
    columns,
    all_frames,
):
    spread_rows = rows + GUARD
    copies = [
        pltpu.make_async_copy(source, target, sems.at[k])
        for k, (source, target) in enumerate(
            ((observed_any, observed_in), (mask_any, mask_in), (count_any, count_in))
        )
    ]
    for copy in copies:
        copy.start()
    norm, wide_mean = norm_ref[0:1, :], mean_ref[0:1, :]
    i = iota((spread_rows, HALF), 0)
    i = jnp.where(i < rows + 4, i, i - spread_rows)
    n = i + scalar_ref[ROW_START : ROW_START + 1, :HALF].astype(jnp.int32)
    x = turn_fraction((2 * iota((spread_rows, HALF), 1) + 1) * n)
    left = jnp.concatenate([cos_turn(x), sin_turn(x)], 1)
    mid = dot_split(left, fold_hi[...], fold_lo[...])
    er, ei, odd_r, odd_i = (mid[:, k * HALF : (k + 1) * HALF] for k in range(4))
    mid = jnp.concatenate(
        [jnp.concatenate([er, odd_i], 1), jnp.concatenate([ei, -odd_r], 1)], 0
    )
    field = dot_split(mid, col_hi[...], col_lo[...])
    field_ref[...] = field
    real, imag = field[:spread_rows], field[spread_rows:]
    intensity = (real * real + imag * imag) * FIELD_SCALE
    blurred = dot_blur(intensity, blur_hi, blur_lo)
    widened = dot_blur(intensity, wide_hi, wide_lo)
    image_ref[...] = blurred * norm + scalar_ref[SKY : SKY + 1, :]
    width_ref[...] = (widened - blurred * wide_mean) * (norm / scalar_ref[JITTER : JITTER + 1, :])
    for copy in copies:
        copy.wait()
    observed_ref[...] = observed_in[0]
    scale = 1.0 / (NR * math.sqrt(all_frames))
    weight_ref[...] = (mask_in[0] * count_in[0]).astype(f32) * scale


def bfe_weights():
    table = np.zeros((5, 5))
    for i in range(5):
        for j in range(5):
            distance = (i - 2) ** 2 + (j - 2) ** 2
            if distance > 0:
                table[i, j] = 1.0 / distance
    total = table.sum()
    return {d: float(np.float32(1.0 / d / total)) for d in (1, 2, 4, 5, 8)}


BFE = bfe_weights()


def gradient_kernel(
    near_ref,
    beside_ref,
    scalar_ref,
    turned_ref,
    observed_ref,
    weight_ref,
    image_ref,
    width_ref,
    field_ref,
    norm_ref,
    pupil_ref,
    blur_hi,
    blur_lo,
    col_hi,
    col_lo,
    maps_ref,
    pay_ref,
    fold_ref,
    *,
    rows,
    columns,
):
    spread_rows = rows + GUARD
    lane = iota((spread_rows, columns), 1)

    def across(x, k):
        moved = pltpu.roll(x, (-k) % columns, 1)
        return jnp.where(lane < columns - k if k > 0 else lane >= -k, moved, 0.0)

    def down(x, k):
        return pltpu.roll(x, (-k) % spread_rows, 0)

    def curve(x):
        one = across(x, 1) + across(x, -1)
        two = across(x, 2) + across(x, -2)
        near = BFE[1] * x + BFE[2] * one + BFE[5] * two
        far = BFE[4] * x + BFE[5] * one + BFE[8] * two
        own = BFE[1] * one + BFE[4] * two - x
        return own + (down(near, 1) + down(near, -1)) + (down(far, 2) + down(far, -2))

    kappa = [
        [scalar_ref[KAPPA + 3 * i + j : KAPPA + 3 * i + j + 1, :] for j in range(3)]
        for i in range(3)
    ]
    row8 = iota((GUARD, columns), 0)
    beside = beside_ref[...]
    guard = jnp.where((row8 == 3) | (row8 == 4), 0.0, beside)
    flat = jnp.concatenate([near_ref[0], guard], 0)
    guard = jnp.where((row8 == 0) | (row8 == 7), pltpu.roll(beside, 4, 0), 0.0)
    bfe = jnp.concatenate([near_ref[1], guard], 0)
    image = image_ref[...]
    charge = flat * image
    curvature = curve(charge)
    factor = 1.0 + bfe * curvature
    spread = charge * factor
    taps = (across(spread, -1), spread, across(spread, 1))
    lines = [sum(kappa[i][j] * taps[j] for j in range(3)) for i in range(3)]
    detected = down(lines[0], -1) + lines[1] + down(lines[2], 1)
    resid = weight_ref[...] * (detected[:rows] - observed_ref[...])
    resid = jnp.concatenate([resid, jnp.zeros((GUARD, columns), f32)], 0)
    back = (across(resid, 1), resid, across(resid, -1))
    lines = [sum(kappa[i][j] * back[j] for j in range(3)) for i in range(3)]
    spread_grad = down(lines[0], 1) + lines[1] + down(lines[2], -1)
    shifted = (down(resid, 1), resid, down(resid, -1))
    sums = []
    for i in range(3):
        for j in range(3):
            sums.append(jnp.sum(shifted[i] * taps[j], 0, keepdims=True))
    charge_curve = spread_grad * charge
    charge_grad = spread_grad * factor + curve(charge_curve * bfe)
    bfe_grad = charge_curve * curvature
    flat_grad = charge_grad * image
    image_grad = charge_grad * flat
    sums.append(jnp.sum(image_grad * width_ref[...], 0, keepdims=True))
    maps_ref[0] = flat_grad[:rows]
    maps_ref[1] = bfe_grad[:rows]
    guard = jnp.where(
        (row8 == 3) | (row8 == 4), pltpu.roll(bfe_grad[rows:], 4, 0), flat_grad[rows:]
    )
    pay_ref[:, :columns] = guard

    scaled = image_grad * norm_ref[0:1, :] * (2.0 * FIELD_SCALE)
    light = dot_blur(scaled, blur_hi, blur_lo)
    field = field_ref[...] * jnp.concatenate([light, light], 0)
    mid = dot_split(field, col_hi[...], col_lo[...], mm_nt)
    even_r, odd_i = mid[:spread_rows, :HALF], mid[:spread_rows, HALF:]
    even_i, odd_r = mid[spread_rows:, :HALF], -mid[spread_rows:, HALF:]
    mid = jnp.concatenate([even_r, even_i, odd_r, odd_i], 1)
    top = mid.astype(bf16).astype(f32)
    pad = jnp.zeros((HALF - 3 * spread_rows, 4 * HALF), f32)
    stacked = jnp.concatenate([top, top, mid - top, pad], 0).astype(bf16)
    fold_ref[...] = mm(turned_ref[...], stacked)

    v = (2 * iota((8, HALF), 1) + 1).astype(f32) * (1.0 / NP)

    def moment_step(step, carry):
        at = pl.multiple_of(step * 8, 8)
        u = (2 * (iota((8, HALF), 0) + at) + 1).astype(f32) * (1.0 / NP)

        def fold(first, k):
            return fold_ref[pl.ds(first + at, 8), k * HALF : (k + 1) * HALF]

        def unfold(ee, eo, oe, oo):
            a, b, c, d = ee + eo, oe + oo, ee - eo, oe - oo
            return a + b, a - b, c + d, c - d

        real = unfold(fold(0, 0), fold(0, 2), -fold(HALF, 1), -fold(HALF, 3))
        imag = unfold(fold(0, 1), fold(0, 3), fold(HALF, 0), fold(HALF, 2))
        g = [
            pupil_ref[q, pl.ds(at, 8), :] * imag[q] - pupil_ref[4 + q, pl.ds(at, 8), :] * real[q]
            for q in range(4)
        ]
        a, b, c, d = g[0] + g[1], g[0] - g[1], g[2] + g[3], g[2] - g[3]
        by_parity = ((a + c, a - c), (b + d, b - d))
        out = []
        power = None
        for p in range(6):
            power = jnp.ones_like(u) if p == 0 else power * u
            for q in range(2):
                term = by_parity[p % 2][q]
                out.append(carry[2 * p + q] + (term if p == 0 else term * power))
        return tuple(out)

    start = tuple(jnp.zeros((8, HALF), f32) for _ in range(12))
    moments = lax.fori_loop(0, HALF // 8, moment_step, start)
    moments = [jnp.sum(m, 0, keepdims=True) for m in moments]
    powers = [jnp.ones((1, HALF), f32)]
    for _ in range(5):
        powers.append(powers[-1] * v[0:1])
    zern = [moments[2 * p + q % 2] * powers[q] for p, q in MODES]
    for line in sums:
        total = line[:, :HALF]
        for k in range(1, columns // HALF):
            total = total + line[:, k * HALF : (k + 1) * HALF]
        zern.append(total)
    stack = jnp.concatenate(zern + [jnp.zeros((32 - len(zern), HALF), f32)], 0)
    totals = jnp.sum(stack, 1, keepdims=True)
    lane8 = iota((8, HALF), 1)
    small = jnp.zeros((8, HALF), f32)
    places = [ZERN_LANE + k for k in range(21)] + [IPC_LANE + k for k in range(9)] + [JITTER_LANE]
    for k, place in enumerate(places):
        small = jnp.where(lane8 == place, totals[k : k + 1, :], small)
    pay_ref[:, columns:] = small


def vmem(count):
    return [pl.BlockSpec(memory_space=pltpu.VMEM)] * count


def xor_pairs(count, mask):
    return [(i, i ^ mask) for i in range(count)]


def guard_tile(top, bottom, columns):
    parts = [top[0, :3], bottom[1, -1:], top[1, :1], bottom[0, -3:]]
    return jnp.concatenate(parts, 0).reshape(GUARD, columns)


def gather_maps(flat_map, bfe_map, rows, pupil_beside):
    own, columns = flat_map.shape[1:]
    frames = lax.axis_size("frame")
    blocks = lax.axis_size(("map", "psf"))
    held = jnp.concatenate([flat_map, bfe_map], 0)[:, None]
    index = lax.axis_index("frame")
    step = frames // 2
    while step:
        if step == 1:
            held = pupil_beside(held)
        other = lax.ppermute(held, "frame", xor_pairs(frames, step))
        before = held
        held = jnp.where(
            (index & step) == 0,
            jnp.stack([held, other], 2),
            jnp.stack([other, held], 2),
        ).reshape((2, -1, own, columns))
        step //= 2
    maps = held.reshape(2, rows, columns)
    row = iota((GUARD, columns), 0)
    first = (row < 3) | (row == 4)
    everywhere = ("frame", "map", "psf")
    if own == GUARD and frames == 4:
        tile = guard_tile(before[:, 0], before[:, 1], columns)
        tile = jnp.where(first == ((index & 1) == 0), tile, 0.0)
        tiles = []
        for odd in (0, 1):
            pairs = []
            for f in range(frames):
                for b in range(blocks):
                    to = (b + 1 if f % 2 else b - 1) % blocks
                    pairs.append((f * blocks + b, (f ^ odd) * blocks + to))
            tiles.append(lax.ppermute(tile, everywhere, pairs))
        block = lax.axis_index(("map", "psf"))
        inside = jnp.where(first, block + 1 < blocks, block > 0)
        return maps, jnp.where(inside, tiles[0] + tiles[1], 0.0)
    tile = guard_tile(maps, maps, columns)
    after = lax.ppermute(tile, ("map", "psf"), [(b + 1, b) for b in range(blocks - 1)])
    ahead = lax.ppermute(tile, ("map", "psf"), [(b, b + 1) for b in range(blocks - 1)])
    return maps, jnp.where(first, after, ahead)


def edge_kernel(grads_ref, *refs):
    *got_refs, out_ref = refs
    rows, columns = grads_ref.shape[1:]
    block = lax.axis_index(("map", "psf"))
    upper = jnp.zeros((GUARD, columns), f32)
    lower = jnp.zeros((GUARD, columns), f32)
    for k, got_ref in enumerate(got_refs):
        partner = block ^ (2 ** (k + 1) - 1)
        edge = got_ref[:, :columns]
        upper = jnp.where(partner == block - 1, edge, upper)
        lower = jnp.where(partner == block + 1, edge, lower)
    row = iota((GUARD, columns), 0)
    out_ref[...] = grads_ref[...]
    out_ref[0, :GUARD] += jnp.where(row < 3, upper, 0.0)
    out_ref[0, rows - GUARD :] += jnp.where(row >= 5, lower, 0.0)
    out_ref[1, :GUARD] += jnp.where(row < 1, pltpu.roll(upper, 4, 0), 0.0)
    out_ref[1, rows - GUARD :] += jnp.where(row >= 7, pltpu.roll(lower, 4, 0), 0.0)


def finish_kernel(
    mine_ref, one_ref, two_ref, three_ref, small_ref, flat_ref, bfe_ref, ipc_ref, zern_ref, jitter_ref
):
    columns = flat_ref.shape[2]
    total = (mine_ref[...] + one_ref[...]) + (two_ref[...] + three_ref[...])
    flat_ref[0] = total[:, :columns]
    bfe_ref[0] = total[:, columns : 2 * columns]
    totals = total[:, 2 * columns :]
    zern_ref[...] = totals[0, ZERN_LANE : ZERN_LANE + 21]
    for i in range(3):
        first = IPC_LANE + 3 * i
        ipc_ref[i : i + 1, :] = totals[0:1, first : first + 3]
    jitter_ref[...] = small_ref[0, JITTER_LANE : JITTER_LANE + 1]


def local(
    observed,
    pixel_mask,
    ramp_counts,
    flat_map,
    bfe_map,
    ipc_kernel,
    zernike,
    jitter,
    sky_level,
    dither,
):
    _, rows, columns = observed.shape
    frames = lax.axis_size("frame")
    blocks = lax.axis_size(("map", "psf"))
    own = rows // frames
    spread_rows = rows + GUARD
    frame = lax.axis_index("frame")

    def array(shape, dtype=f32):
        return jax.ShapeDtypeStruct(shape, dtype)

    params = pltpu.CompilerParams(vmem_limit_bytes=16 * 2**20)
    little = pltpu.CompilerParams(vmem_limit_bytes=2 * 2**20)
    scalars, turned, pupil, *fold = pl.pallas_call(
        lambda *refs: pupil_kernel(*refs, rows=rows, columns=columns),
        out_shape=[
            array((16, columns)),
            array((NP, HALF), bf16),
            array((8, HALF, HALF)),
            array((NP, 4 * HALF), bf16),
            array((NP, 4 * HALF), bf16),
        ],
        in_specs=[pl.BlockSpec(memory_space=pltpu.SMEM)] * 4,
        out_specs=vmem(5),
        compiler_params=params,
        name="pupil",
    )(zernike, jnp.stack([jitter, sky_level], 1), dither, ipc_kernel)
    tables = pl.pallas_call(
        lambda *refs: table_kernel(*refs, columns=columns),
        out_shape=[array((8, columns))] * 2
        + [array((columns // 2, 3 * columns // 2), bf16)] * 4
        + [array((NP, columns), bf16)] * 2,
        in_specs=vmem(1),
        out_specs=vmem(8),
        compiler_params=params,
        name="tables",
    )(scalars)

    def pupil_beside(sent):
        nonlocal scalars
        sent, scalars = lax.optimization_barrier((sent, scalars))
        return sent

    maps, beside = gather_maps(flat_map, bfe_map, rows, pupil_beside)

    seen = pl.pallas_call(
        lambda *refs: field_kernel(*refs, rows=rows, columns=columns, all_frames=frames),
        out_shape=[
            array((rows, columns)),
            array((rows, columns)),
            array((spread_rows, columns)),
            array((spread_rows, columns)),
            array((2 * spread_rows, columns)),
        ],
        in_specs=vmem(1) + [pl.BlockSpec(memory_space=pltpu.HBM)] * 3 + vmem(10),
        out_specs=vmem(5),
        scratch_shapes=[
            pltpu.VMEM((1, rows, columns), f32),
            pltpu.VMEM((1, rows, columns), jnp.int32),
            pltpu.VMEM((1, rows, columns), jnp.int32),
            pltpu.SemaphoreType.DMA((3,)),
        ],
        compiler_params=params,
        name="field",
    )(scalars, observed, pixel_mask, ramp_counts, *fold, *tables)
    norm, _, blur_hi, blur_lo, _, _, col_hi, col_lo = tables

    grads, pay = pl.pallas_call(
        lambda *refs: gradient_kernel(*refs, rows=rows, columns=columns),
        out_shape=[array((2, rows, columns)), array((8, columns + HALF))],
        in_specs=vmem(15),
        out_specs=vmem(2),
        scratch_shapes=[pltpu.VMEM((NP, 4 * HALF), f32)],
        compiler_params=params,
        name="gradient",
    )(maps, beside, scalars, turned, *seen, norm, pupil, blur_hi, blur_lo, col_hi, col_lo)

    lane = iota(pay.shape, 1)
    gots = []
    step = 1
    while step < blocks:
        got = lax.ppermute(pay, ("map", "psf"), xor_pairs(blocks, 2 * step - 1))
        gots.append(got)
        pay = jnp.where(lane >= columns, pay + got, pay)
        step *= 2
    small = pay[:, columns:]
    grads = pl.pallas_call(
        edge_kernel,
        out_shape=array((2, rows, columns)),
        in_specs=vmem(1 + len(gots)),
        out_specs=pl.BlockSpec(memory_space=pltpu.VMEM),
        compiler_params=little,
        name="edges",
    )(grads, *gots)

    held = grads.reshape(2, frames, own, columns)
    wide = small[:own]

    def joined(piece, wide):
        return jnp.concatenate([*piece.reshape(-1, own, columns), wide], 1)

    step = 1
    while 4 * step < frames:
        bit = (frame & step) != 0
        pieces = held.reshape((2, -1, 2) + held.shape[2:])
        mine = jnp.where(bit, pieces[:, :, 1], pieces[:, :, 0])
        theirs = jnp.where(bit, pieces[:, :, 0], pieces[:, :, 1])
        got = lax.ppermute(joined(theirs, wide), "frame", xor_pairs(frames, step))
        step *= 2
        count = 2 * mine.shape[1]
        other = jnp.stack([got[:, k * columns : (k + 1) * columns] for k in range(count)])
        held = mine + other.reshape(mine.shape)
        wide = wide + got[:, count * columns :]
    place = frame // step
    gots = []
    for other in (1, 2, 3):
        piece = lax.dynamic_index_in_dim(held, place ^ other, 1, keepdims=False)
        gots.append(
            lax.ppermute(joined(piece, wide), "frame", xor_pairs(frames, other * step))
        )
    mine = joined(lax.dynamic_index_in_dim(held, place, 1, keepdims=False), wide)
    return pl.pallas_call(
        finish_kernel,
        out_shape=[
            array((1, own, columns)),
            array((1, own, columns)),
            array((3, 3)),
            array((21,)),
            array((1,)),
        ],
        in_specs=vmem(5),
        out_specs=vmem(5),
        compiler_params=little,
        name="finish",
    )(mine, *gots, small)


def solution(mesh):
    in_specs = (
        P(("groups", "frame"), ("map", "psf"), None),
        P(("groups", "frame"), ("map", "psf"), None),
        P(("groups", "frame"), ("map", "psf"), None),
        P(("groups", "map", "psf"), "frame", None),
        P(("groups", "map", "psf"), "frame", None),
        P("groups", None),
        P("groups"),
        P(("groups", "frame")),
        P(("groups", "frame")),
        P(("groups", "frame"), None),
    )
    out_specs = (
        P(("groups", "map", "psf"), "frame", None),
        P(("groups", "map", "psf"), "frame", None),
        P("groups", None),
        P("groups"),
        P(("groups", "frame")),
    )
    return jax.shard_map(local, mesh=mesh, in_specs=in_specs, out_specs=out_specs, check_vma=False)
```

```python
import math

import jax
import jax.numpy as jnp
import numpy as np
from jax import lax
from jax.experimental import pallas as pl
from jax.experimental.pallas import tpu as pltpu
from jax.sharding import PartitionSpec as P

NP = 256
HALF = NP // 2
NR = 16
OVERSAMPLE = 32
AMPLITUDE = 2.0
IPC_CENTER = 0.8
TURN = 2 * NP * OVERSAMPLE
FIELD_SCALE = (AMPLITUDE / NP**2) ** 2
GUARD = 8
ZERN_LANE, IPC_LANE, JITTER_LANE = 0, 32, 48
JITTER, SKY, ROW_START, COLUMN, KAPPA = range(5)

f32, bf16 = jnp.float32, jnp.bfloat16
MODES = [(p, d - p) for d in range(6) for p in range(d + 1)]


def sine_table():
    nodes = 0.125 + 0.125 * np.cos(np.pi * (np.arange(200) + 0.5) / 200)
    powers = np.stack([nodes ** (2 * k + 1) for k in range(5)], 1)
    return [float(c) for c in np.linalg.lstsq(powers, np.sin(2 * np.pi * nodes), rcond=None)[0]]


SINE = sine_table()


def sin_quarter(y):
    t = y * y
    poly = SINE[4]
    for c in SINE[3::-1]:
        poly = poly * t + c
    return poly * y


def cos_turn(x):
    return sin_quarter(0.25 - jnp.abs(x))


def sin_turn(x):
    return sin_quarter(jnp.minimum(jnp.maximum(x, -0.5 - x), 0.5 - x))


def turn_fraction(k):
    return (((k + TURN // 2) & (TURN - 1)) - TURN // 2).astype(f32) * (1.0 / TURN)


def iota(shape, axis):
    return lax.broadcasted_iota(jnp.int32, shape, axis)


def mm(a, b):
    return jnp.dot(a, b, preferred_element_type=f32)


def mm_nt(a, b):
    return lax.dot_general(a, b, (((1,), (1,)), ((), ())), preferred_element_type=f32)


def halves(x):
    high = x.astype(bf16)
    return high, (x - high.astype(f32)).astype(bf16)


def dot_blur(x, high, low):
    half = high.shape[0]
    left, right = x[:, :half], x[:, half:]
    rows = x.shape[0]
    both = dot_split(jnp.concatenate([left, right], 0), high[:, half : 2 * half], low[:, half : 2 * half])
    first = both[:rows] + dot_split(right, high[:, :half], low[:, :half])
    last = both[rows:] + dot_split(left, high[:, 2 * half :], low[:, 2 * half :])
    return jnp.concatenate([first, last], 1)


def dot_split(x, high, low, product=mm):
    rows = x.shape[0]
    top = x.astype(bf16)
    both = jnp.concatenate([top.astype(f32), x - top.astype(f32)], 0).astype(bf16)
    first = product(both, high)
    return first[:rows] + first[rows:] + product(top, low)


def pupil_kernel(
    zern_ref,
    level_ref,
    dither_ref,
    ipc_ref,
    scalar_ref,
    turned_ref,
    pupil_ref,
    fold_hi,
    fold_lo,
    *,
    rows,
    columns,
):
    spread_rows = rows + GUARD
    blocks = lax.axis_size(("map", "psf"))
    row_start = lax.axis_index(("map", "psf")) * rows - rows * blocks // 2 - dither_ref[:, 0:1]
    column = columns // 2 + dither_ref[:, 1:2]
    values = [level_ref[:, 0:1], level_ref[:, 1:2], row_start.astype(f32), column.astype(f32)]
    values += [
        ipc_ref[i : i + 1, j : j + 1] + (IPC_CENTER if i == j == 1 else 0.0)
        for i in range(3)
        for j in range(3)
    ]
    for k, value in enumerate(values):
        scalar_ref[k : k + 1, :] = jnp.broadcast_to(value, (1, columns))
    z = {
        mode: jnp.broadcast_to(zern_ref[:, k : k + 1], (16, HALF)) for k, mode in enumerate(MODES)
    }

    def pupil_step(step, carry):
        at = pl.multiple_of(step * 16, 16)
        j = iota((16, HALF), 0) + at
        l = iota((16, HALF), 1)
        u = (2 * j + 1).astype(f32) * (1.0 / NP)
        v = (2 * l + 1).astype(f32) * (1.0 / NP)
        uu, vv = u * u, v * v
        ee = (
            z[0, 0]
            + vv * (z[0, 2] + vv * z[0, 4])
            + uu * (z[2, 0] + vv * z[2, 2] + uu * z[4, 0])
        )
        oe = u * (
            z[1, 0]
            + vv * (z[1, 2] + vv * z[1, 4])
            + uu * (z[3, 0] + vv * z[3, 2] + uu * z[5, 0])
        )
        eo = v * (
            z[0, 1]
            + vv * (z[0, 3] + vv * z[0, 5])
            + uu * (z[2, 1] + vv * z[2, 3] + uu * z[4, 1])
        )
        oo = u * v * (z[1, 1] + vv * z[1, 3] + uu * z[3, 1])
        radius = uu + vv
        open_ = jnp.where((radius <= 1.0) & (radius >= 0.09), 1.0, 0.0).astype(f32)
        even, odd = (ee + eo, oe + oo), (ee - eo, oe - oo)
        phases = (even[0] + even[1], even[0] - even[1], odd[0] + odd[1], odd[0] - odd[1])
        real, imag = [], []
        for quadrant, phase in enumerate(phases):
            turns = phase * (0.5 / math.pi)
            turns = turns - jnp.floor(turns + 0.5)
            real.append(open_ * cos_turn(turns))
            imag.append(open_ * sin_turn(turns))
            pupil_ref[quadrant, pl.ds(at, 16), :] = real[-1]
            pupil_ref[4 + quadrant, pl.ds(at, 16), :] = imag[-1]

        def folds(x):
            a, b, c, d = x[0] + x[1], x[0] - x[1], x[2] + x[3], x[2] - x[3]
            return a + c, a - c, b + d, b - d

        ree, reo, roe, roo = folds(real)
        iee, ieo, ioe, ioo = folds(imag)
        for first, parts in ((0, (ree, iee, reo, ieo)), (HALF, (ioe, -roe, ioo, -roo))):
            for k, part in enumerate(parts):
                high, low = halves(part)
                fold_hi[pl.ds(first + at, 16), k * HALF : (k + 1) * HALF] = high
                fold_lo[pl.ds(first + at, 16), k * HALF : (k + 1) * HALF] = low
        return carry

    lax.fori_loop(0, HALF // 16, pupil_step, 0)

    at = iota((HALF, HALF), 1)
    part = (at >= spread_rows).astype(jnp.int32) + (at >= 2 * spread_rows).astype(jnp.int32)
    i = at - part * spread_rows
    i = jnp.where(i < rows + 4, i, i - spread_rows)
    x = turn_fraction((2 * iota((HALF, HALF), 0) + 1) * (i + row_start))
    for first, value in ((0, cos_turn(x)), (HALF, sin_turn(x))):
        high = value.astype(bf16).astype(f32)
        value = jnp.where(part == 1, value - high, high)
        turned_ref[first : first + HALF, :] = value.astype(bf16)


def field_kernel(
    scalar_ref,
    observed_any,
    mask_any,
    count_any,
    fold_hi,
    fold_lo,
    observed_ref,
    weight_ref,
    image_ref,
    width_ref,
    field_ref,
    norm_ref,
    blur_hi,
    blur_lo,
    col_hi,
    col_lo,
    wide_hi,
    wide_lo,
    observed_in,
    mask_in,
    count_in,
    sems,
    *,
    rows,
    columns,
    all_frames,
):
    spread_rows = rows + GUARD
    copies = [
        pltpu.make_async_copy(source, target, sems.at[k])
        for k, (source, target) in enumerate(
            ((observed_any, observed_in), (mask_any, mask_in), (count_any, count_in))
        )
    ]
    for copy in copies:
        copy.start()

    def column_step(step, carry):
        at = pl.multiple_of(step * 16, 16)
        l = iota((16, columns), 0) + at
        c = iota((16, columns), 1) - scalar_ref[COLUMN : COLUMN + 1, :].astype(jnp.int32)
        x = turn_fraction((2 * l + 1) * c)
        high, low = halves(cos_turn(x))
        col_hi[pl.ds(at, 16), :] = high
        col_lo[pl.ds(at, 16), :] = low
        high, low = halves(sin_turn(x))
        col_hi[pl.ds(HALF + at, 16), :] = high
        col_lo[pl.ds(HALF + at, 16), :] = low
        return carry

    lax.fori_loop(0, HALF // 16, column_step, 0)

    jitter = scalar_ref[JITTER : JITTER + 1, : columns // 2]
    falloff = 0.5 / (jitter * jitter)
    falloff = jnp.concatenate([falloff] * 3, 1)

    half = columns // 2

    def blur_step(step, carry):
        total, wide_total = carry
        at = pl.multiple_of(step * 16, 16)
        d = (iota((16, 3 * half), 0) + at - iota((16, 3 * half), 1) + half).astype(f32)
        exponent = d * d * falloff
        value = jnp.exp(-exponent)
        wide = value * (exponent + exponent)
        high, low = halves(value)
        blur_hi[pl.ds(at, 16), :] = high
        blur_lo[pl.ds(at, 16), :] = low
        high, low = halves(wide)
        wide_hi[pl.ds(at, 16), :] = high
        wide_lo[pl.ds(at, 16), :] = low
        return total + value, wide_total + wide

    zero = jnp.zeros((16, 3 * half), f32)
    total, wide_total = lax.fori_loop(0, half // 16, blur_step, (zero, zero))
    total = jnp.sum(total, 0, keepdims=True)
    wide_total = jnp.sum(wide_total, 0, keepdims=True)
    norm = 1.0 / (total[:, half:] + total[:, : 2 * half])
    mean = (wide_total[:, half:] + wide_total[:, : 2 * half]) * norm
    norm_ref[...] = jnp.broadcast_to(norm, (8, columns))

    i = iota((spread_rows, HALF), 0)
    i = jnp.where(i < rows + 4, i, i - spread_rows)
    n = i + scalar_ref[ROW_START : ROW_START + 1, :HALF].astype(jnp.int32)
    x = turn_fraction((2 * iota((spread_rows, HALF), 1) + 1) * n)
    left = jnp.concatenate([cos_turn(x), sin_turn(x)], 1)
    mid = dot_split(left, fold_hi[...], fold_lo[...])
    er, ei, odd_r, odd_i = (mid[:, k * HALF : (k + 1) * HALF] for k in range(4))
    mid = jnp.concatenate(
        [jnp.concatenate([er, odd_i], 1), jnp.concatenate([ei, -odd_r], 1)], 0
    )
    field = dot_split(mid, col_hi[...], col_lo[...])
    field_ref[...] = field
    real, imag = field[:spread_rows], field[spread_rows:]
    intensity = (real * real + imag * imag) * FIELD_SCALE
    blurred = dot_blur(intensity, blur_hi, blur_lo)
    widened = dot_blur(intensity, wide_hi, wide_lo)
    image_ref[...] = blurred * norm + scalar_ref[SKY : SKY + 1, :]
    width_ref[...] = (widened - blurred * mean) * (norm / scalar_ref[JITTER : JITTER + 1, :])
    for copy in copies:
        copy.wait()
    observed_ref[...] = observed_in[0]
    scale = 1.0 / (NR * math.sqrt(all_frames))
    weight_ref[...] = (mask_in[0] * count_in[0]).astype(f32) * scale


def bfe_weights():
    table = np.zeros((5, 5))
    for i in range(5):
        for j in range(5):
            distance = (i - 2) ** 2 + (j - 2) ** 2
            if distance > 0:
                table[i, j] = 1.0 / distance
    total = table.sum()
    return {d: float(np.float32(1.0 / d / total)) for d in (1, 2, 4, 5, 8)}


BFE = bfe_weights()


def gradient_kernel(
    near_ref,
    beside_one,
    beside_two,
    scalar_ref,
    turned_ref,
    observed_ref,
    weight_ref,
    image_ref,
    width_ref,
    field_ref,
    norm_ref,
    pupil_ref,
    blur_hi,
    blur_lo,
    col_hi,
    col_lo,
    maps_ref,
    pay_ref,
    fold_ref,
    *,
    rows,
    columns,
):
    spread_rows = rows + GUARD
    lane = iota((spread_rows, columns), 1)

    def across(x, k):
        moved = pltpu.roll(x, (-k) % columns, 1)
        return jnp.where(lane < columns - k if k > 0 else lane >= -k, moved, 0.0)

    def down(x, k):
        return pltpu.roll(x, (-k) % spread_rows, 0)

    def curve(x):
        one = across(x, 1) + across(x, -1)
        two = across(x, 2) + across(x, -2)
        near = BFE[1] * x + BFE[2] * one + BFE[5] * two
        far = BFE[4] * x + BFE[5] * one + BFE[8] * two
        own = BFE[1] * one + BFE[4] * two - x
        return own + (down(near, 1) + down(near, -1)) + (down(far, 2) + down(far, -2))

    kappa = [
        [scalar_ref[KAPPA + 3 * i + j : KAPPA + 3 * i + j + 1, :] for j in range(3)]
        for i in range(3)
    ]
    row8 = iota((GUARD, columns), 0)
    block = lax.axis_index(("map", "psf"))
    after = jnp.where(block + 1 < lax.axis_size(("map", "psf")), 1.0, 0.0)
    ahead = jnp.where(block > 0, 1.0, 0.0)
    beside = beside_one[...] + beside_two[...]
    beside = beside * jnp.where((row8 < 3) | (row8 == 4), after, ahead)
    guard = jnp.where((row8 == 3) | (row8 == 4), 0.0, beside)
    flat = jnp.concatenate([near_ref[0], guard], 0)
    guard = jnp.where((row8 == 0) | (row8 == 7), pltpu.roll(beside, 4, 0), 0.0)
    bfe = jnp.concatenate([near_ref[1], guard], 0)
    image = image_ref[...]
    charge = flat * image
    curvature = curve(charge)
    factor = 1.0 + bfe * curvature
    spread = charge * factor
    taps = (across(spread, -1), spread, across(spread, 1))
    lines = [sum(kappa[i][j] * taps[j] for j in range(3)) for i in range(3)]
    detected = down(lines[0], -1) + lines[1] + down(lines[2], 1)
    resid = weight_ref[...] * (detected[:rows] - observed_ref[...])
    resid = jnp.concatenate([resid, jnp.zeros((GUARD, columns), f32)], 0)
    back = (across(resid, 1), resid, across(resid, -1))
    lines = [sum(kappa[i][j] * back[j] for j in range(3)) for i in range(3)]
    spread_grad = down(lines[0], 1) + lines[1] + down(lines[2], -1)
    shifted = (down(resid, 1), resid, down(resid, -1))
    sums = []
    for i in range(3):
        for j in range(3):
            sums.append(jnp.sum(shifted[i] * taps[j], 0, keepdims=True))
    charge_curve = spread_grad * charge
    charge_grad = spread_grad * factor + curve(charge_curve * bfe)
    bfe_grad = charge_curve * curvature
    flat_grad = charge_grad * image
    image_grad = charge_grad * flat
    sums.append(jnp.sum(image_grad * width_ref[...], 0, keepdims=True))
    maps_ref[0] = flat_grad[:rows]
    maps_ref[1] = bfe_grad[:rows]
    guard = jnp.where(
        (row8 == 3) | (row8 == 4), pltpu.roll(bfe_grad[rows:], 4, 0), flat_grad[rows:]
    )
    pay_ref[:, :columns] = guard

    scaled = image_grad * norm_ref[0:1, :] * (2.0 * FIELD_SCALE)
    light = dot_blur(scaled, blur_hi, blur_lo)
    field = field_ref[...] * jnp.concatenate([light, light], 0)
    mid = dot_split(field, col_hi[...], col_lo[...], mm_nt)
    even_r, odd_i = mid[:spread_rows, :HALF], mid[:spread_rows, HALF:]
    even_i, odd_r = mid[spread_rows:, :HALF], -mid[spread_rows:, HALF:]
    mid = jnp.concatenate([even_r, even_i, odd_r, odd_i], 1)
    top = mid.astype(bf16).astype(f32)
    pad = jnp.zeros((HALF - 3 * spread_rows, 4 * HALF), f32)
    stacked = jnp.concatenate([top, top, mid - top, pad], 0).astype(bf16)
    fold_ref[...] = mm(turned_ref[...], stacked)

    v = (2 * iota((8, HALF), 1) + 1).astype(f32) * (1.0 / NP)

    def moment_step(step, carry):
        at = pl.multiple_of(step * 8, 8)
        u = (2 * (iota((8, HALF), 0) + at) + 1).astype(f32) * (1.0 / NP)

        def fold(first, k):
            return fold_ref[pl.ds(first + at, 8), k * HALF : (k + 1) * HALF]

        def unfold(ee, eo, oe, oo):
            a, b, c, d = ee + eo, oe + oo, ee - eo, oe - oo
            return a + b, a - b, c + d, c - d

        real = unfold(fold(0, 0), fold(0, 2), -fold(HALF, 1), -fold(HALF, 3))
        imag = unfold(fold(0, 1), fold(0, 3), fold(HALF, 0), fold(HALF, 2))
        g = [
            pupil_ref[q, pl.ds(at, 8), :] * imag[q] - pupil_ref[4 + q, pl.ds(at, 8), :] * real[q]
            for q in range(4)
        ]
        a, b, c, d = g[0] + g[1], g[0] - g[1], g[2] + g[3], g[2] - g[3]
        by_parity = ((a + c, a - c), (b + d, b - d))
        out = []
        power = None
        for p in range(6):
            power = jnp.ones_like(u) if p == 0 else power * u
            for q in range(2):
                term = by_parity[p % 2][q]
                out.append(carry[2 * p + q] + (term if p == 0 else term * power))
        return tuple(out)

    start = tuple(jnp.zeros((8, HALF), f32) for _ in range(12))
    moments = lax.fori_loop(0, HALF // 8, moment_step, start)
    moments = [jnp.sum(m, 0, keepdims=True) for m in moments]
    powers = [jnp.ones((1, HALF), f32)]
    for _ in range(5):
        powers.append(powers[-1] * v[0:1])
    zern = [moments[2 * p + q % 2] * powers[q] for p, q in MODES]
    for line in sums:
        total = line[:, :HALF]
        for k in range(1, columns // HALF):
            total = total + line[:, k * HALF : (k + 1) * HALF]
        zern.append(total)
    stack = jnp.concatenate(zern + [jnp.zeros((32 - len(zern), HALF), f32)], 0)
    totals = jnp.sum(stack, 1, keepdims=True)
    lane8 = iota((8, HALF), 1)
    small = jnp.zeros((8, HALF), f32)
    places = [ZERN_LANE + k for k in range(21)] + [IPC_LANE + k for k in range(9)] + [JITTER_LANE]
    for k, place in enumerate(places):
        small = jnp.where(lane8 == place, totals[k : k + 1, :], small)
    pay_ref[:, columns:] = small


def vmem(count):
    return [pl.BlockSpec(memory_space=pltpu.VMEM)] * count


def xor_pairs(count, mask):
    return [(i, i ^ mask) for i in range(count)]


def guard_tile(top, bottom, columns):
    parts = [top[0, :3], bottom[1, -1:], top[1, :1], bottom[0, -3:]]
    return jnp.concatenate(parts, 0).reshape(GUARD, columns)


def gather_maps(flat_map, bfe_map, rows, pupil_beside):
    own, columns = flat_map.shape[1:]
    frames = lax.axis_size("frame")
    blocks = lax.axis_size(("map", "psf"))
    held = jnp.concatenate([flat_map, bfe_map], 0)[:, None]
    index = lax.axis_index("frame")
    step = frames // 2
    while step:
        if step == 1:
            held = pupil_beside(held)
        other = lax.ppermute(held, "frame", xor_pairs(frames, step))
        before = held
        held = jnp.where(
            (index & step) == 0,
            jnp.stack([held, other], 2),
            jnp.stack([other, held], 2),
        ).reshape((2, -1, own, columns))
        step //= 2
    maps = held.reshape(2, rows, columns)
    row = iota((GUARD, columns), 0)
    first = (row < 3) | (row == 4)
    everywhere = ("frame", "map", "psf")
    if own == GUARD and frames == 4:
        tile = guard_tile(before[:, 0], before[:, 1], columns)
        tile = jnp.where(first == ((index & 1) == 0), tile, 0.0)
        tiles = []
        for odd in (0, 1):
            pairs = []
            for f in range(frames):
                for b in range(blocks):
                    to = (b + 1 if f % 2 else b - 1) % blocks
                    pairs.append((f * blocks + b, (f ^ odd) * blocks + to))
            tiles.append(lax.ppermute(tile, everywhere, pairs))
        return maps, tiles
    tile = guard_tile(maps, maps, columns)
    after = lax.ppermute(tile, ("map", "psf"), [(b + 1, b) for b in range(blocks - 1)])
    ahead = lax.ppermute(tile, ("map", "psf"), [(b, b + 1) for b in range(blocks - 1)])
    return maps, [jnp.where(first, after, 0.0), jnp.where(first, 0.0, ahead)]


def edge_kernel(grads_ref, *refs):
    *got_refs, out_ref = refs
    rows, columns = grads_ref.shape[1:]
    block = lax.axis_index(("map", "psf"))
    upper = jnp.zeros((GUARD, columns), f32)
    lower = jnp.zeros((GUARD, columns), f32)
    for k, got_ref in enumerate(got_refs):
        partner = block ^ (2 ** (k + 1) - 1)
        edge = got_ref[:, :columns]
        upper = jnp.where(partner == block - 1, edge, upper)
        lower = jnp.where(partner == block + 1, edge, lower)
    row = iota((GUARD, columns), 0)
    out_ref[...] = grads_ref[...]
    out_ref[0, :GUARD] += jnp.where(row < 3, upper, 0.0)
    out_ref[0, rows - GUARD :] += jnp.where(row >= 5, lower, 0.0)
    out_ref[1, :GUARD] += jnp.where(row < 1, pltpu.roll(upper, 4, 0), 0.0)
    out_ref[1, rows - GUARD :] += jnp.where(row >= 7, pltpu.roll(lower, 4, 0), 0.0)


def finish_kernel(
    mine_ref, one_ref, two_ref, three_ref, small_ref, flat_ref, bfe_ref, ipc_ref, zern_ref, jitter_ref
):
    columns = flat_ref.shape[2]
    total = (mine_ref[...] + one_ref[...]) + (two_ref[...] + three_ref[...])
    flat_ref[0] = total[:, :columns]
    bfe_ref[0] = total[:, columns : 2 * columns]
    totals = total[:, 2 * columns :]
    zern_ref[...] = totals[0, ZERN_LANE : ZERN_LANE + 21]
    for i in range(3):
        first = IPC_LANE + 3 * i
        ipc_ref[i : i + 1, :] = totals[0:1, first : first + 3]
    jitter_ref[...] = small_ref[0, JITTER_LANE : JITTER_LANE + 1]


def local(
    observed,
    pixel_mask,
    ramp_counts,
    flat_map,
    bfe_map,
    ipc_kernel,
    zernike,
    jitter,
    sky_level,
    dither,
):
    _, rows, columns = observed.shape
    frames = lax.axis_size("frame")
    blocks = lax.axis_size(("map", "psf"))
    own = rows // frames
    spread_rows = rows + GUARD
    frame = lax.axis_index("frame")

    def array(shape, dtype=f32):
        return jax.ShapeDtypeStruct(shape, dtype)

    params = pltpu.CompilerParams(vmem_limit_bytes=16 * 2**20)
    little = pltpu.CompilerParams(vmem_limit_bytes=2 * 2**20)
    scalars, turned, pupil, *fold = pl.pallas_call(
        lambda *refs: pupil_kernel(*refs, rows=rows, columns=columns),
        out_shape=[
            array((16, columns)),
            array((NP, HALF), bf16),
            array((8, HALF, HALF)),
            array((NP, 4 * HALF), bf16),
            array((NP, 4 * HALF), bf16),
        ],
        in_specs=vmem(4),
        out_specs=vmem(5),
        compiler_params=params,
        name="pupil",
    )(zernike[None], jnp.stack([jitter, sky_level], 1), dither, ipc_kernel)
    def pupil_beside(sent):
        nonlocal scalars
        sent, scalars = lax.optimization_barrier((sent, scalars))
        return sent

    maps, beside = gather_maps(flat_map, bfe_map, rows, pupil_beside)

    seen = pl.pallas_call(
        lambda *refs: field_kernel(*refs, rows=rows, columns=columns, all_frames=frames),
        out_shape=[
            array((rows, columns)),
            array((rows, columns)),
            array((spread_rows, columns)),
            array((spread_rows, columns)),
            array((2 * spread_rows, columns)),
            array((8, columns)),
            *[array((columns // 2, 3 * columns // 2), bf16)] * 2,
            *[array((NP, columns), bf16)] * 2,
        ],
        in_specs=vmem(1) + [pl.BlockSpec(memory_space=pltpu.HBM)] * 3 + vmem(2),
        out_specs=vmem(10),
        scratch_shapes=[
            pltpu.VMEM((columns // 2, 3 * columns // 2), bf16),
            pltpu.VMEM((columns // 2, 3 * columns // 2), bf16),
            pltpu.VMEM((1, rows, columns), f32),
            pltpu.VMEM((1, rows, columns), jnp.int32),
            pltpu.VMEM((1, rows, columns), jnp.int32),
            pltpu.SemaphoreType.DMA((3,)),
        ],
        compiler_params=params,
        name="field",
    )(scalars, observed, pixel_mask, ramp_counts, *fold)
    seen, tables = seen[:5], seen[5:]

    grads, pay = pl.pallas_call(
        lambda *refs: gradient_kernel(*refs, rows=rows, columns=columns),
        out_shape=[array((2, rows, columns)), array((8, columns + HALF))],
        in_specs=vmem(16),
        out_specs=vmem(2),
        scratch_shapes=[pltpu.VMEM((NP, 4 * HALF), f32)],
        compiler_params=params,
        name="gradient",
    )(maps, *beside, scalars, turned, *seen, tables[0], pupil, *tables[1:])

    lane = iota(pay.shape, 1)
    gots = []
    step = 1
    while step < blocks:
        got = lax.ppermute(pay, ("map", "psf"), xor_pairs(blocks, 2 * step - 1))
        gots.append(got)
        pay = jnp.where(lane >= columns, pay + got, pay)
        step *= 2
    small = pay[:, columns:]
    grads = pl.pallas_call(
        edge_kernel,
        out_shape=array((2, rows, columns)),
        in_specs=vmem(1 + len(gots)),
        out_specs=pl.BlockSpec(memory_space=pltpu.VMEM),
        compiler_params=little,
        name="edges",
    )(grads, *gots)

    held = grads.reshape(2, frames, own, columns)
    wide = small[:own]

    def joined(piece, wide):
        return jnp.concatenate([*piece.reshape(-1, own, columns), wide], 1)

    step = 1
    while 4 * step < frames:
        bit = (frame & step) != 0
        pieces = held.reshape((2, -1, 2) + held.shape[2:])
        mine = jnp.where(bit, pieces[:, :, 1], pieces[:, :, 0])
        theirs = jnp.where(bit, pieces[:, :, 0], pieces[:, :, 1])
        got = lax.ppermute(joined(theirs, wide), "frame", xor_pairs(frames, step))
        step *= 2
        count = 2 * mine.shape[1]
        other = jnp.stack([got[:, k * columns : (k + 1) * columns] for k in range(count)])
        held = mine + other.reshape(mine.shape)
        wide = wide + got[:, count * columns :]
    place = frame // step
    gots = []
    for other in (1, 2, 3):
        piece = lax.dynamic_index_in_dim(held, place ^ other, 1, keepdims=False)
        gots.append(
            lax.ppermute(joined(piece, wide), "frame", xor_pairs(frames, other * step))
        )
    mine = joined(lax.dynamic_index_in_dim(held, place, 1, keepdims=False), wide)
    return pl.pallas_call(
        finish_kernel,
        out_shape=[
            array((1, own, columns)),
            array((1, own, columns)),
            array((3, 3)),
            array((21,)),
            array((1,)),
        ],
        in_specs=vmem(5),
        out_specs=vmem(5),
        compiler_params=little,
        name="finish",
    )(mine, *gots, small)


def solution(mesh):
    in_specs = (
        P(("groups", "frame"), ("map", "psf"), None),
        P(("groups", "frame"), ("map", "psf"), None),
        P(("groups", "frame"), ("map", "psf"), None),
        P(("groups", "map", "psf"), "frame", None),
        P(("groups", "map", "psf"), "frame", None),
        P("groups", None),
        P("groups"),
        P(("groups", "frame")),
        P(("groups", "frame")),
        P(("groups", "frame"), None),
    )
    out_specs = (
        P(("groups", "map", "psf"), "frame", None),
        P(("groups", "map", "psf"), "frame", None),
        P("groups", None),
        P("groups"),
        P(("groups", "frame")),
    )
    return jax.shard_map(local, mesh=mesh, in_specs=in_specs, out_specs=out_specs, check_vma=False)
```

```python
import math

import jax
import jax.numpy as jnp
import numpy as np
from jax import lax
from jax.experimental import pallas as pl
from jax.experimental.pallas import tpu as pltpu
from jax.sharding import PartitionSpec as P

NP = 256
HALF = NP // 2
NR = 16
OVERSAMPLE = 32
AMPLITUDE = 2.0
IPC_CENTER = 0.8
TURN = 2 * NP * OVERSAMPLE
FIELD_SCALE = (AMPLITUDE / NP**2) ** 2
GUARD = 8
ZERN_LANE, IPC_LANE, JITTER_LANE = 0, 32, 48
JITTER, SKY, ROW_START, COLUMN, KAPPA = range(5)

f32, bf16 = jnp.float32, jnp.bfloat16
MODES = [(p, d - p) for d in range(6) for p in range(d + 1)]


def sine_table():
    nodes = 0.125 + 0.125 * np.cos(np.pi * (np.arange(200) + 0.5) / 200)
    powers = np.stack([nodes ** (2 * k + 1) for k in range(5)], 1)
    return [float(c) for c in np.linalg.lstsq(powers, np.sin(2 * np.pi * nodes), rcond=None)[0]]


SINE = sine_table()


def sin_quarter(y):
    t = y * y
    poly = SINE[4]
    for c in SINE[3::-1]:
        poly = poly * t + c
    return poly * y


def cos_turn(x):
    return sin_quarter(0.25 - jnp.abs(x))


def sin_turn(x):
    return sin_quarter(jnp.minimum(jnp.maximum(x, -0.5 - x), 0.5 - x))


def turn_fraction(k):
    return (((k + TURN // 2) & (TURN - 1)) - TURN // 2).astype(f32) * (1.0 / TURN)


def iota(shape, axis):
    return lax.broadcasted_iota(jnp.int32, shape, axis)


def mm(a, b):
    return jnp.dot(a, b, preferred_element_type=f32)


def mm_nt(a, b):
    return lax.dot_general(a, b, (((1,), (1,)), ((), ())), preferred_element_type=f32)


def halves(x):
    high = x.astype(bf16)
    return high, (x - high.astype(f32)).astype(bf16)


def dot_blur(x, high, low):
    half = high.shape[0]
    left, right = x[:, :half], x[:, half:]
    rows = x.shape[0]
    both = dot_split(jnp.concatenate([left, right], 0), high[:, half : 2 * half], low[:, half : 2 * half])
    first = both[:rows] + dot_split(right, high[:, :half], low[:, :half])
    last = both[rows:] + dot_split(left, high[:, 2 * half :], low[:, 2 * half :])
    return jnp.concatenate([first, last], 1)


def dot_split(x, high, low, product=mm):
    rows = x.shape[0]
    top = x.astype(bf16)
    both = jnp.concatenate([top.astype(f32), x - top.astype(f32)], 0).astype(bf16)
    first = product(both, high)
    return first[:rows] + first[rows:] + product(top, low)


def pupil_kernel(
    zern_ref,
    level_ref,
    dither_ref,
    ipc_ref,
    scalar_ref,
    turned_ref,
    pupil_ref,
    fold_hi,
    fold_lo,
    *,
    rows,
    columns,
):
    spread_rows = rows + GUARD
    blocks = lax.axis_size(("map", "psf"))
    row_start = lax.axis_index(("map", "psf")) * rows - rows * blocks // 2 - dither_ref[:, 0:1]
    column = columns // 2 + dither_ref[:, 1:2]
    values = [level_ref[:, 0:1], level_ref[:, 1:2], row_start.astype(f32), column.astype(f32)]
    values += [
        ipc_ref[i : i + 1, j : j + 1] + (IPC_CENTER if i == j == 1 else 0.0)
        for i in range(3)
        for j in range(3)
    ]
    for k, value in enumerate(values):
        scalar_ref[k : k + 1, :] = jnp.broadcast_to(value, (1, columns))
    z = {
        mode: jnp.broadcast_to(zern_ref[:, k : k + 1], (16, HALF)) for k, mode in enumerate(MODES)
    }

    def pupil_step(step, carry):
        at = pl.multiple_of(step * 16, 16)
        j = iota((16, HALF), 0) + at
        l = iota((16, HALF), 1)
        u = (2 * j + 1).astype(f32) * (1.0 / NP)
        v = (2 * l + 1).astype(f32) * (1.0 / NP)
        uu, vv = u * u, v * v
        ee = (
            z[0, 0]
            + vv * (z[0, 2] + vv * z[0, 4])
            + uu * (z[2, 0] + vv * z[2, 2] + uu * z[4, 0])
        )
        oe = u * (
            z[1, 0]
            + vv * (z[1, 2] + vv * z[1, 4])
            + uu * (z[3, 0] + vv * z[3, 2] + uu * z[5, 0])
        )
        eo = v * (
            z[0, 1]
            + vv * (z[0, 3] + vv * z[0, 5])
            + uu * (z[2, 1] + vv * z[2, 3] + uu * z[4, 1])
        )
        oo = u * v * (z[1, 1] + vv * z[1, 3] + uu * z[3, 1])
        radius = uu + vv
        open_ = jnp.where((radius <= 1.0) & (radius >= 0.09), 1.0, 0.0).astype(f32)
        even, odd = (ee + eo, oe + oo), (ee - eo, oe - oo)
        phases = (even[0] + even[1], even[0] - even[1], odd[0] + odd[1], odd[0] - odd[1])
        real, imag = [], []
        for quadrant, phase in enumerate(phases):
            turns = phase * (0.5 / math.pi)
            turns = turns - jnp.floor(turns + 0.5)
            real.append(open_ * cos_turn(turns))
            imag.append(open_ * sin_turn(turns))
            pupil_ref[quadrant, pl.ds(at, 16), :] = real[-1]
            pupil_ref[4 + quadrant, pl.ds(at, 16), :] = imag[-1]

        def folds(x):
            a, b, c, d = x[0] + x[1], x[0] - x[1], x[2] + x[3], x[2] - x[3]
            return a + c, a - c, b + d, b - d

        ree, reo, roe, roo = folds(real)
        iee, ieo, ioe, ioo = folds(imag)
        for first, parts in ((0, (ree, iee, reo, ieo)), (HALF, (ioe, -roe, ioo, -roo))):
            for k, part in enumerate(parts):
                high, low = halves(part)
                fold_hi[pl.ds(first + at, 16), k * HALF : (k + 1) * HALF] = high
                fold_lo[pl.ds(first + at, 16), k * HALF : (k + 1) * HALF] = low
        return carry

    lax.fori_loop(0, HALF // 16, pupil_step, 0, unroll=True)

    at = iota((HALF, HALF), 1)
    part = (at >= spread_rows).astype(jnp.int32) + (at >= 2 * spread_rows).astype(jnp.int32)
    i = at - part * spread_rows
    i = jnp.where(i < rows + 4, i, i - spread_rows)
    x = turn_fraction((2 * iota((HALF, HALF), 0) + 1) * (i + row_start))
    for first, value in ((0, cos_turn(x)), (HALF, sin_turn(x))):
        high = value.astype(bf16).astype(f32)
        value = jnp.where(part == 1, value - high, high)
        turned_ref[first : first + HALF, :] = value.astype(bf16)


def field_kernel(
    scalar_ref,
    observed_any,
    mask_any,
    count_any,
    fold_hi,
    fold_lo,
    observed_ref,
    weight_ref,
    image_ref,
    width_ref,
    field_ref,
    norm_ref,
    blur_hi,
    blur_lo,
    col_hi,
    col_lo,
    wide_hi,
    wide_lo,
    observed_in,
    mask_in,
    count_in,
    sems,
    *,
    rows,
    columns,
    all_frames,
):
    spread_rows = rows + GUARD
    copies = [
        pltpu.make_async_copy(source, target, sems.at[k])
        for k, (source, target) in enumerate(
            ((observed_any, observed_in), (mask_any, mask_in), (count_any, count_in))
        )
    ]
    for copy in copies:
        copy.start()

    def column_step(step, carry):
        at = pl.multiple_of(step * 16, 16)
        l = iota((16, columns), 0) + at
        c = iota((16, columns), 1) - scalar_ref[COLUMN : COLUMN + 1, :].astype(jnp.int32)
        x = turn_fraction((2 * l + 1) * c)
        high, low = halves(cos_turn(x))
        col_hi[pl.ds(at, 16), :] = high
        col_lo[pl.ds(at, 16), :] = low
        high, low = halves(sin_turn(x))
        col_hi[pl.ds(HALF + at, 16), :] = high
        col_lo[pl.ds(HALF + at, 16), :] = low
        return carry

    lax.fori_loop(0, HALF // 16, column_step, 0, unroll=True)

    jitter = scalar_ref[JITTER : JITTER + 1, :HALF]
    falloff = 0.5 / (jitter * jitter)
    falloff = jnp.concatenate([falloff] * (3 * columns // (2 * HALF) + 1), 1)

    half = columns // 2

    def blur_step(step, carry):
        total, wide_total = carry
        at = pl.multiple_of(step * 16, 16)
        shape = (16, 3 * half + HALF)
        d = (iota(shape, 0) + at - iota(shape, 1) + (half + HALF)).astype(f32)
        exponent = d * d * falloff
        value = jnp.exp(-exponent)
        wide = value * (exponent + exponent)
        for table, (high_ref, low_ref) in ((value, (blur_hi, blur_lo)), (wide, (wide_hi, wide_lo))):
            for ref, part in zip((high_ref, low_ref), halves(table)):
                ref[pl.ds(at, 16), :] = part[:, HALF:]
                ref[pl.ds(HALF + at, 16), :] = part[:, : 3 * half]
        return total + value, wide_total + wide

    zero = jnp.zeros((16, 3 * half + HALF), f32)
    total, wide_total = lax.fori_loop(0, HALF // 16, blur_step, (zero, zero), unroll=True)
    total = total[:, HALF:] + total[:, : 3 * half]
    wide_total = wide_total[:, HALF:] + wide_total[:, : 3 * half]
    total = jnp.sum(total, 0, keepdims=True)
    wide_total = jnp.sum(wide_total, 0, keepdims=True)
    norm = 1.0 / (total[:, half:] + total[:, : 2 * half])
    mean = (wide_total[:, half:] + wide_total[:, : 2 * half]) * norm
    norm_ref[...] = jnp.broadcast_to(norm, (8, columns))

    i = iota((spread_rows, HALF), 0)
    i = jnp.where(i < rows + 4, i, i - spread_rows)
    n = i + scalar_ref[ROW_START : ROW_START + 1, :HALF].astype(jnp.int32)
    x = turn_fraction((2 * iota((spread_rows, HALF), 1) + 1) * n)
    left = jnp.concatenate([cos_turn(x), sin_turn(x)], 1)
    mid = dot_split(left, fold_hi[...], fold_lo[...])
    er, ei, odd_r, odd_i = (mid[:, k * HALF : (k + 1) * HALF] for k in range(4))
    mid = jnp.concatenate(
        [jnp.concatenate([er, odd_i], 1), jnp.concatenate([ei, -odd_r], 1)], 0
    )
    field = dot_split(mid, col_hi[...], col_lo[...])
    field_ref[...] = field
    real, imag = field[:spread_rows], field[spread_rows:]
    intensity = (real * real + imag * imag) * FIELD_SCALE
    blurred = dot_blur(intensity, blur_hi, blur_lo)
    widened = dot_blur(intensity, wide_hi, wide_lo)
    image_ref[...] = blurred * norm + scalar_ref[SKY : SKY + 1, :]
    width_ref[...] = (widened - blurred * mean) * (norm / scalar_ref[JITTER : JITTER + 1, :])
    for copy in copies:
        copy.wait()
    observed_ref[...] = observed_in[0]
    scale = 1.0 / (NR * math.sqrt(all_frames))
    weight_ref[...] = (mask_in[0] * count_in[0]).astype(f32) * scale


def bfe_weights():
    table = np.zeros((5, 5))
    for i in range(5):
        for j in range(5):
            distance = (i - 2) ** 2 + (j - 2) ** 2
            if distance > 0:
                table[i, j] = 1.0 / distance
    total = table.sum()
    return {d: float(np.float32(1.0 / d / total)) for d in (1, 2, 4, 5, 8)}


BFE = bfe_weights()


def gradient_kernel(
    beside_two,
    beside_one,
    near_ref,
    scalar_ref,
    turned_ref,
    observed_ref,
    weight_ref,
    image_ref,
    width_ref,
    field_ref,
    norm_ref,
    pupil_ref,
    blur_hi,
    blur_lo,
    col_hi,
    col_lo,
    maps_ref,
    pay_ref,
    fold_ref,
    *,
    rows,
    columns,
):
    spread_rows = rows + GUARD
    lane = iota((spread_rows, columns), 1)

    def across(x, k):
        moved = pltpu.roll(x, (-k) % columns, 1)
        return jnp.where(lane < columns - k if k > 0 else lane >= -k, moved, 0.0)

    def down(x, k):
        return pltpu.roll(x, (-k) % spread_rows, 0)

    def curve(x):
        one = across(x, 1) + across(x, -1)
        two = across(x, 2) + across(x, -2)
        near = BFE[1] * x + BFE[2] * one + BFE[5] * two
        far = BFE[4] * x + BFE[5] * one + BFE[8] * two
        own = BFE[1] * one + BFE[4] * two - x
        return own + (down(near, 1) + down(near, -1)) + (down(far, 2) + down(far, -2))

    kappa = [
        [scalar_ref[KAPPA + 3 * i + j : KAPPA + 3 * i + j + 1, :] for j in range(3)]
        for i in range(3)
    ]
    row8 = iota((GUARD, columns), 0)
    block = lax.axis_index(("map", "psf"))
    after = jnp.where(block + 1 < lax.axis_size(("map", "psf")), 1.0, 0.0)
    ahead = jnp.where(block > 0, 1.0, 0.0)
    beside = beside_one[...] + beside_two[...]
    beside = beside * jnp.where((row8 < 3) | (row8 == 4), after, ahead)
    guard = jnp.where((row8 == 3) | (row8 == 4), 0.0, beside)
    flat = jnp.concatenate([near_ref[0], guard], 0)
    guard = jnp.where((row8 == 0) | (row8 == 7), pltpu.roll(beside, 4, 0), 0.0)
    bfe = jnp.concatenate([near_ref[1], guard], 0)
    image = image_ref[...]
    charge = flat * image
    curvature = curve(charge)
    factor = 1.0 + bfe * curvature
    spread = charge * factor
    taps = (across(spread, -1), spread, across(spread, 1))
    lines = [sum(kappa[i][j] * taps[j] for j in range(3)) for i in range(3)]
    detected = down(lines[0], -1) + lines[1] + down(lines[2], 1)
    resid = weight_ref[...] * (detected[:rows] - observed_ref[...])
    resid = jnp.concatenate([resid, jnp.zeros((GUARD, columns), f32)], 0)
    back = (across(resid, 1), resid, across(resid, -1))
    lines = [sum(kappa[i][j] * back[j] for j in range(3)) for i in range(3)]
    spread_grad = down(lines[0], 1) + lines[1] + down(lines[2], -1)
    shifted = (down(resid, 1), resid, down(resid, -1))
    sums = []
    for i in range(3):
        for j in range(3):
            sums.append(jnp.sum(shifted[i] * taps[j], 0, keepdims=True))
    charge_curve = spread_grad * charge
    charge_grad = spread_grad * factor + curve(charge_curve * bfe)
    bfe_grad = charge_curve * curvature
    flat_grad = charge_grad * image
    image_grad = charge_grad * flat
    sums.append(jnp.sum(image_grad * width_ref[...], 0, keepdims=True))
    maps_ref[0] = flat_grad[:rows]
    maps_ref[1] = bfe_grad[:rows]
    guard = jnp.where(
        (row8 == 3) | (row8 == 4), pltpu.roll(bfe_grad[rows:], 4, 0), flat_grad[rows:]
    )
    pay_ref[:, :columns] = guard

    scaled = image_grad * norm_ref[0:1, :] * (2.0 * FIELD_SCALE)
    light = dot_blur(scaled, blur_hi, blur_lo)
    field = field_ref[...] * jnp.concatenate([light, light], 0)
    mid = dot_split(field, col_hi[...], col_lo[...], mm_nt)
    even_r, odd_i = mid[:spread_rows, :HALF], mid[:spread_rows, HALF:]
    even_i, odd_r = mid[spread_rows:, :HALF], -mid[spread_rows:, HALF:]
    mid = jnp.concatenate([even_r, even_i, odd_r, odd_i], 1)
    top = mid.astype(bf16).astype(f32)
    pad = jnp.zeros((HALF - 3 * spread_rows, 4 * HALF), f32)
    stacked = jnp.concatenate([top, top, mid - top, pad], 0).astype(bf16)
    fold_ref[...] = mm(turned_ref[...], stacked)

    v = (2 * iota((8, HALF), 1) + 1).astype(f32) * (1.0 / NP)

    def moment_step(step, carry):
        at = pl.multiple_of(step * 8, 8)
        u = (2 * (iota((8, HALF), 0) + at) + 1).astype(f32) * (1.0 / NP)

        def fold(first, k):
            return fold_ref[pl.ds(first + at, 8), k * HALF : (k + 1) * HALF]

        def unfold(ee, eo, oe, oo):
            a, b, c, d = ee + eo, oe + oo, ee - eo, oe - oo
            return a + b, a - b, c + d, c - d

        real = unfold(fold(0, 0), fold(0, 2), -fold(HALF, 1), -fold(HALF, 3))
        imag = unfold(fold(0, 1), fold(0, 3), fold(HALF, 0), fold(HALF, 2))
        g = [
            pupil_ref[q, pl.ds(at, 8), :] * imag[q] - pupil_ref[4 + q, pl.ds(at, 8), :] * real[q]
            for q in range(4)
        ]
        a, b, c, d = g[0] + g[1], g[0] - g[1], g[2] + g[3], g[2] - g[3]
        by_parity = ((a + c, a - c), (b + d, b - d))
        out = []
        power = None
        for p in range(6):
            power = jnp.ones_like(u) if p == 0 else power * u
            for q in range(2):
                term = by_parity[p % 2][q]
                out.append(carry[2 * p + q] + (term if p == 0 else term * power))
        return tuple(out)

    start = tuple(jnp.zeros((8, HALF), f32) for _ in range(12))
    moments = lax.fori_loop(0, HALF // 8, moment_step, start, unroll=True)
    moments = [jnp.sum(m, 0, keepdims=True) for m in moments]
    powers = [jnp.ones((1, HALF), f32)]
    for _ in range(5):
        powers.append(powers[-1] * v[0:1])
    zern = [moments[2 * p + q % 2] * powers[q] for p, q in MODES]
    for line in sums:
        total = line[:, :HALF]
        for k in range(1, columns // HALF):
            total = total + line[:, k * HALF : (k + 1) * HALF]
        zern.append(total)
    stack = jnp.concatenate(zern + [jnp.zeros((32 - len(zern), HALF), f32)], 0)
    totals = jnp.sum(stack, 1, keepdims=True)
    lane8 = iota((8, HALF), 1)
    small = jnp.zeros((8, HALF), f32)
    places = [ZERN_LANE + k for k in range(21)] + [IPC_LANE + k for k in range(9)] + [JITTER_LANE]
    for k, place in enumerate(places):
        small = jnp.where(lane8 == place, totals[k : k + 1, :], small)
    pay_ref[:, columns:] = small


def vmem(count):
    return [pl.BlockSpec(memory_space=pltpu.VMEM)] * count


def xor_pairs(count, mask):
    return [(i, i ^ mask) for i in range(count)]


def guard_tile(top, bottom, columns):
    parts = [top[0, :3], bottom[1, -1:], top[1, :1], bottom[0, -3:]]
    return jnp.concatenate(parts, 0).reshape(GUARD, columns)


def gather_maps(flat_map, bfe_map, rows, pupil_beside):
    own, columns = flat_map.shape[1:]
    frames = lax.axis_size("frame")
    blocks = lax.axis_size(("map", "psf"))
    held = jnp.concatenate([flat_map, bfe_map], 0)[:, None]
    index = lax.axis_index("frame")
    step = frames // 2
    while step:
        if step == 1:
            held = pupil_beside(held)
        other = lax.ppermute(held, "frame", xor_pairs(frames, step))
        before = held
        held = jnp.where(
            (index & step) == 0,
            jnp.stack([held, other], 2),
            jnp.stack([other, held], 2),
        ).reshape((2, -1, own, columns))
        step //= 2
    maps = held.reshape(2, rows, columns)
    row = iota((GUARD, columns), 0)
    first = (row < 3) | (row == 4)
    everywhere = ("frame", "map", "psf")
    if own == GUARD and frames == 4:
        tile = guard_tile(before[:, 0], before[:, 1], columns)
        tile = jnp.where(first == ((index & 1) == 0), tile, 0.0)
        tiles = []
        for odd in (0, 1):
            pairs = []
            for f in range(frames):
                for b in range(blocks):
                    to = (b + 1 if f % 2 else b - 1) % blocks
                    pairs.append((f * blocks + b, (f ^ odd) * blocks + to))
            tiles.append(lax.ppermute(tile, everywhere, pairs))
        return maps, tiles
    tile = guard_tile(maps, maps, columns)
    after = lax.ppermute(tile, ("map", "psf"), [(b + 1, b) for b in range(blocks - 1)])
    ahead = lax.ppermute(tile, ("map", "psf"), [(b, b + 1) for b in range(blocks - 1)])
    return maps, [jnp.where(first, after, 0.0), jnp.where(first, 0.0, ahead)]


def edge_kernel(grads_ref, *refs):
    *got_refs, out_ref = refs
    rows, columns = grads_ref.shape[1:]
    block = lax.axis_index(("map", "psf"))
    upper = jnp.zeros((GUARD, columns), f32)
    lower = jnp.zeros((GUARD, columns), f32)
    for k, got_ref in enumerate(got_refs):
        partner = block ^ (2 ** (k + 1) - 1)
        edge = got_ref[:, :columns]
        upper = jnp.where(partner == block - 1, edge, upper)
        lower = jnp.where(partner == block + 1, edge, lower)
    row = iota((GUARD, columns), 0)
    out_ref[...] = grads_ref[...]
    out_ref[0, :GUARD] += jnp.where(row < 3, upper, 0.0)
    out_ref[0, rows - GUARD :] += jnp.where(row >= 5, lower, 0.0)
    out_ref[1, :GUARD] += jnp.where(row < 1, pltpu.roll(upper, 4, 0), 0.0)
    out_ref[1, rows - GUARD :] += jnp.where(row >= 7, pltpu.roll(lower, 4, 0), 0.0)


def finish_kernel(
    mine_ref, three_ref, two_ref, one_ref, small_ref, flat_ref, bfe_ref, ipc_ref, zern_ref, jitter_ref
):
    columns = flat_ref.shape[2]
    total = (mine_ref[...] + one_ref[...]) + (two_ref[...] + three_ref[...])
    flat_ref[0] = total[:, :columns]
    bfe_ref[0] = total[:, columns : 2 * columns]
    totals = total[:, 2 * columns :]
    zern_ref[...] = totals[0, ZERN_LANE : ZERN_LANE + 21]
    for i in range(3):
        first = IPC_LANE + 3 * i
        ipc_ref[i : i + 1, :] = totals[0:1, first : first + 3]
    jitter_ref[...] = small_ref[0, JITTER_LANE : JITTER_LANE + 1]


def local(
    observed,
    pixel_mask,
    ramp_counts,
    flat_map,
    bfe_map,
    ipc_kernel,
    zernike,
    jitter,
    sky_level,
    dither,
):
    _, rows, columns = observed.shape
    frames = lax.axis_size("frame")
    blocks = lax.axis_size(("map", "psf"))
    own = rows // frames
    spread_rows = rows + GUARD
    frame = lax.axis_index("frame")

    def array(shape, dtype=f32):
        return jax.ShapeDtypeStruct(shape, dtype)

    params = pltpu.CompilerParams(vmem_limit_bytes=16 * 2**20)
    little = pltpu.CompilerParams(vmem_limit_bytes=2 * 2**20)
    scalars, turned, pupil, *fold = pl.pallas_call(
        lambda *refs: pupil_kernel(*refs, rows=rows, columns=columns),
        out_shape=[
            array((16, columns)),
            array((NP, HALF), bf16),
            array((8, HALF, HALF)),
            array((NP, 4 * HALF), bf16),
            array((NP, 4 * HALF), bf16),
        ],
        in_specs=vmem(4),
        out_specs=vmem(5),
        compiler_params=params,
        name="pupil",
    )(zernike[None], jnp.stack([jitter, sky_level], 1), dither, ipc_kernel)
    def pupil_beside(sent):
        nonlocal scalars
        sent, scalars = lax.optimization_barrier((sent, scalars))
        return sent

    maps, beside = gather_maps(flat_map, bfe_map, rows, pupil_beside)

    seen = pl.pallas_call(
        lambda *refs: field_kernel(*refs, rows=rows, columns=columns, all_frames=frames),
        out_shape=[
            array((rows, columns)),
            array((rows, columns)),
            array((spread_rows, columns)),
            array((spread_rows, columns)),
            array((2 * spread_rows, columns)),
            array((8, columns)),
            *[array((columns // 2, 3 * columns // 2), bf16)] * 2,
            *[array((NP, columns), bf16)] * 2,
        ],
        in_specs=vmem(1) + [pl.BlockSpec(memory_space=pltpu.HBM)] * 3 + vmem(2),
        out_specs=vmem(10),
        scratch_shapes=[
            pltpu.VMEM((columns // 2, 3 * columns // 2), bf16),
            pltpu.VMEM((columns // 2, 3 * columns // 2), bf16),
            pltpu.VMEM((1, rows, columns), f32),
            pltpu.VMEM((1, rows, columns), jnp.int32),
            pltpu.VMEM((1, rows, columns), jnp.int32),
            pltpu.SemaphoreType.DMA((3,)),
        ],
        compiler_params=params,
        name="field",
    )(scalars, observed, pixel_mask, ramp_counts, *fold)
    seen, tables = seen[:5], seen[5:]

    grads, pay = pl.pallas_call(
        lambda *refs: gradient_kernel(*refs, rows=rows, columns=columns),
        out_shape=[array((2, rows, columns)), array((8, columns + HALF))],
        in_specs=vmem(16),
        out_specs=vmem(2),
        scratch_shapes=[pltpu.VMEM((NP, 4 * HALF), f32)],
        compiler_params=params,
        name="gradient",
    )(beside[1], beside[0], maps, scalars, turned, *seen, tables[0], pupil, *tables[1:])

    lane = iota(pay.shape, 1)
    gots = []
    step = 1
    while step < blocks:
        got = lax.ppermute(pay, ("map", "psf"), xor_pairs(blocks, 2 * step - 1))
        gots.append(got)
        pay = jnp.where(lane >= columns, pay + got, pay)
        step *= 2
    small = pay[:, columns:]
    grads = pl.pallas_call(
        edge_kernel,
        out_shape=array((2, rows, columns)),
        in_specs=vmem(1 + len(gots)),
        out_specs=pl.BlockSpec(memory_space=pltpu.VMEM),
        compiler_params=little,
        name="edges",
    )(grads, *gots)

    held = grads.reshape(2, frames, own, columns)
    wide = small[:own]

    def joined(piece, wide):
        return jnp.concatenate([*piece.reshape(-1, own, columns), wide], 1)

    step = 1
    while 4 * step < frames:
        bit = (frame & step) != 0
        pieces = held.reshape((2, -1, 2) + held.shape[2:])
        mine = jnp.where(bit, pieces[:, :, 1], pieces[:, :, 0])
        theirs = jnp.where(bit, pieces[:, :, 0], pieces[:, :, 1])
        got = lax.ppermute(joined(theirs, wide), "frame", xor_pairs(frames, step))
        step *= 2
        count = 2 * mine.shape[1]
        other = jnp.stack([got[:, k * columns : (k + 1) * columns] for k in range(count)])
        held = mine + other.reshape(mine.shape)
        wide = wide + got[:, count * columns :]
    place = frame // step
    gots = {}
    for other in (3, 2, 1):
        piece = lax.dynamic_index_in_dim(held, place ^ other, 1, keepdims=False)
        gots[other] = lax.ppermute(joined(piece, wide), "frame", xor_pairs(frames, other * step))
    mine = joined(lax.dynamic_index_in_dim(held, place, 1, keepdims=False), wide)
    return pl.pallas_call(
        finish_kernel,
        out_shape=[
            array((1, own, columns)),
            array((1, own, columns)),
            array((3, 3)),
            array((21,)),
            array((1,)),
        ],
        in_specs=vmem(5),
        out_specs=vmem(5),
        compiler_params=little,
        name="finish",
    )(mine, gots[3], gots[2], gots[1], small)


def solution(mesh):
    in_specs = (
        P(("groups", "frame"), ("map", "psf"), None),
        P(("groups", "frame"), ("map", "psf"), None),
        P(("groups", "frame"), ("map", "psf"), None),
        P(("groups", "map", "psf"), "frame", None),
        P(("groups", "map", "psf"), "frame", None),
        P("groups", None),
        P("groups"),
        P(("groups", "frame")),
        P(("groups", "frame")),
        P(("groups", "frame"), None),
    )
    out_specs = (
        P(("groups", "map", "psf"), "frame", None),
        P(("groups", "map", "psf"), "frame", None),
        P("groups", None),
        P("groups"),
        P(("groups", "frame")),
    )
    return jax.shard_map(local, mesh=mesh, in_specs=in_specs, out_specs=out_specs, check_vma=False)
```

```python
import math

import jax
import jax.numpy as jnp
import numpy as np
from jax import lax
from jax.experimental import pallas as pl
from jax.experimental.pallas import tpu as pltpu
from jax.sharding import PartitionSpec as P

NP = 256
HALF = NP // 2
NR = 16
OVERSAMPLE = 32
AMPLITUDE = 2.0
IPC_CENTER = 0.8
TURN = 2 * NP * OVERSAMPLE
FIELD_SCALE = (AMPLITUDE / NP**2) ** 2
GUARD = 8
ZERN_LANE, IPC_LANE, JITTER_LANE = 0, 32, 48
JITTER, SKY, ROW_START, COLUMN, KAPPA = range(5)

f32, bf16 = jnp.float32, jnp.bfloat16
MODES = [(p, d - p) for d in range(6) for p in range(d + 1)]


def sine_table():
    nodes = 0.125 + 0.125 * np.cos(np.pi * (np.arange(200) + 0.5) / 200)
    powers = np.stack([nodes ** (2 * k + 1) for k in range(5)], 1)
    return [float(c) for c in np.linalg.lstsq(powers, np.sin(2 * np.pi * nodes), rcond=None)[0]]


SINE = sine_table()


def sin_quarter(y):
    t = y * y
    poly = SINE[4]
    for c in SINE[3::-1]:
        poly = poly * t + c
    return poly * y


def cos_turn(x):
    return sin_quarter(0.25 - jnp.abs(x))


def sin_turn(x):
    return sin_quarter(jnp.minimum(jnp.maximum(x, -0.5 - x), 0.5 - x))


def turn_fraction(k):
    return (((k + TURN // 2) & (TURN - 1)) - TURN // 2).astype(f32) * (1.0 / TURN)


def iota(shape, axis):
    return lax.broadcasted_iota(jnp.int32, shape, axis)


def mm(a, b):
    return jnp.dot(a, b, preferred_element_type=f32)


def mm_nt(a, b):
    return lax.dot_general(a, b, (((1,), (1,)), ((), ())), preferred_element_type=f32)


def halves(x):
    high = x.astype(bf16)
    return high, (x - high.astype(f32)).astype(bf16)


def dot_blur(x, high, low):
    half = high.shape[0]
    left, right = x[:, :half], x[:, half:]
    rows = x.shape[0]
    both = dot_split(jnp.concatenate([left, right], 0), high[:, half : 2 * half], low[:, half : 2 * half])
    first = both[:rows] + dot_split(right, high[:, :half], low[:, :half])
    last = both[rows:] + dot_split(left, high[:, 2 * half :], low[:, 2 * half :])
    return jnp.concatenate([first, last], 1)


def dot_split(x, high, low, product=mm):
    rows = x.shape[0]
    top = x.astype(bf16)
    both = jnp.concatenate([top.astype(f32), x - top.astype(f32)], 0).astype(bf16)
    first = product(both, high)
    return first[:rows] + first[rows:] + product(top, low)


def pupil_kernel(
    zern_ref,
    level_ref,
    dither_ref,
    ipc_ref,
    scalar_ref,
    fold_hi,
    fold_lo,
    *,
    rows,
    columns,
):
    blocks = lax.axis_size(("map", "psf"))
    row_start = lax.axis_index(("map", "psf")) * rows - rows * blocks // 2 - dither_ref[:, 0:1]
    column = columns // 2 + dither_ref[:, 1:2]
    values = [level_ref[:, 0:1], level_ref[:, 1:2], row_start.astype(f32), column.astype(f32)]
    values += [
        ipc_ref[i : i + 1, j : j + 1] + (IPC_CENTER if i == j == 1 else 0.0)
        for i in range(3)
        for j in range(3)
    ]
    for k, value in enumerate(values):
        scalar_ref[k : k + 1, :] = jnp.broadcast_to(value, (1, columns))
    z = {
        mode: jnp.broadcast_to(zern_ref[:, k : k + 1], (16, HALF)) for k, mode in enumerate(MODES)
    }

    def pupil_step(step, carry):
        at = pl.multiple_of(step * 16, 16)
        j = iota((16, HALF), 0) + at
        l = iota((16, HALF), 1)
        u = (2 * j + 1).astype(f32) * (1.0 / NP)
        v = (2 * l + 1).astype(f32) * (1.0 / NP)
        uu, vv = u * u, v * v
        ee = (
            z[0, 0]
            + vv * (z[0, 2] + vv * z[0, 4])
            + uu * (z[2, 0] + vv * z[2, 2] + uu * z[4, 0])
        )
        oe = u * (
            z[1, 0]
            + vv * (z[1, 2] + vv * z[1, 4])
            + uu * (z[3, 0] + vv * z[3, 2] + uu * z[5, 0])
        )
        eo = v * (
            z[0, 1]
            + vv * (z[0, 3] + vv * z[0, 5])
            + uu * (z[2, 1] + vv * z[2, 3] + uu * z[4, 1])
        )
        oo = u * v * (z[1, 1] + vv * z[1, 3] + uu * z[3, 1])
        radius = uu + vv
        open_ = jnp.where((radius <= 1.0) & (radius >= 0.09), 1.0, 0.0).astype(f32)
        even, odd = (ee + eo, oe + oo), (ee - eo, oe - oo)
        phases = (even[0] + even[1], even[0] - even[1], odd[0] + odd[1], odd[0] - odd[1])
        real, imag = [], []
        for phase in phases:
            turns = phase * (0.5 / math.pi)
            turns = turns - jnp.floor(turns + 0.5)
            real.append(open_ * cos_turn(turns))
            imag.append(open_ * sin_turn(turns))

        def folds(x):
            a, b, c, d = x[0] + x[1], x[0] - x[1], x[2] + x[3], x[2] - x[3]
            return a + c, a - c, b + d, b - d

        ree, reo, roe, roo = folds(real)
        iee, ieo, ioe, ioo = folds(imag)
        for first, parts in ((0, (ree, iee, reo, ieo)), (HALF, (ioe, -roe, ioo, -roo))):
            for k, part in enumerate(parts):
                high, low = halves(part)
                fold_hi[pl.ds(first + at, 16), k * HALF : (k + 1) * HALF] = high
                fold_lo[pl.ds(first + at, 16), k * HALF : (k + 1) * HALF] = low
        return carry

    lax.fori_loop(0, HALF // 16, pupil_step, 0, unroll=True)


def field_kernel(
    scalar_ref,
    observed_any,
    mask_any,
    count_any,
    fold_hi,
    fold_lo,
    observed_ref,
    weight_ref,
    image_ref,
    width_ref,
    field_ref,
    power_ref,
    norm_ref,
    blur_hi,
    blur_lo,
    col_hi,
    col_lo,
    wide_hi,
    wide_lo,
    observed_in,
    mask_in,
    count_in,
    sems,
    *,
    rows,
    columns,
    all_frames,
):
    spread_rows = rows + GUARD
    copies = [
        pltpu.make_async_copy(source, target, sems.at[k])
        for k, (source, target) in enumerate(
            ((observed_any, observed_in), (mask_any, mask_in), (count_any, count_in))
        )
    ]
    for copy in copies:
        copy.start()

    def column_step(step, carry):
        at = pl.multiple_of(step * 16, 16)
        l = iota((16, columns), 0) + at
        c = iota((16, columns), 1) - scalar_ref[COLUMN : COLUMN + 1, :].astype(jnp.int32)
        x = turn_fraction((2 * l + 1) * c)
        high, low = halves(cos_turn(x))
        col_hi[pl.ds(at, 16), :] = high
        col_lo[pl.ds(at, 16), :] = low
        high, low = halves(sin_turn(x))
        col_hi[pl.ds(HALF + at, 16), :] = high
        col_lo[pl.ds(HALF + at, 16), :] = low
        return carry

    lax.fori_loop(0, HALF // 16, column_step, 0, unroll=True)

    jitter = scalar_ref[JITTER : JITTER + 1, :HALF]
    falloff = 0.5 / (jitter * jitter)
    falloff = jnp.concatenate([falloff] * (3 * columns // (2 * HALF) + 1), 1)

    half = columns // 2

    def blur_step(step, carry):
        total, wide_total = carry
        at = pl.multiple_of(step * 16, 16)
        shape = (16, 3 * half + HALF)
        d = (iota(shape, 0) + at - iota(shape, 1) + (half + HALF)).astype(f32)
        exponent = d * d * falloff
        value = jnp.exp(-exponent)
        wide = value * (exponent + exponent)
        for table, (high_ref, low_ref) in ((value, (blur_hi, blur_lo)), (wide, (wide_hi, wide_lo))):
            for ref, part in zip((high_ref, low_ref), halves(table)):
                ref[pl.ds(at, 16), :] = part[:, HALF:]
                ref[pl.ds(HALF + at, 16), :] = part[:, : 3 * half]
        return total + value, wide_total + wide

    zero = jnp.zeros((16, 3 * half + HALF), f32)
    total, wide_total = lax.fori_loop(0, HALF // 16, blur_step, (zero, zero), unroll=True)
    total = total[:, HALF:] + total[:, : 3 * half]
    wide_total = wide_total[:, HALF:] + wide_total[:, : 3 * half]
    total = jnp.sum(total, 0, keepdims=True)
    wide_total = jnp.sum(wide_total, 0, keepdims=True)
    norm = 1.0 / (total[:, half:] + total[:, : 2 * half])
    mean = (wide_total[:, half:] + wide_total[:, : 2 * half]) * norm
    norm_ref[...] = jnp.broadcast_to(norm, (8, columns))

    i = iota((spread_rows, HALF), 0)
    i = jnp.where(i < rows + 4, i, i - spread_rows)
    n = i + scalar_ref[ROW_START : ROW_START + 1, :HALF].astype(jnp.int32)
    x = turn_fraction((2 * iota((spread_rows, HALF), 1) + 1) * n)
    cosine, sine = cos_turn(x), sin_turn(x)
    u = (2 * iota((spread_rows, HALF), 1) + 1).astype(f32) * (1.0 / NP)
    left = []
    for p in range(6):
        left.append(jnp.concatenate([sine, -cosine] if p % 2 else [cosine, sine], 1))
        cosine, sine = cosine * u, sine * u
    mid = dot_split(jnp.concatenate(left, 0), fold_hi[...], fold_lo[...])
    power_ref[...] = mid
    er, ei, odd_r, odd_i = (mid[:spread_rows, k * HALF : (k + 1) * HALF] for k in range(4))
    mid = jnp.concatenate(
        [jnp.concatenate([er, odd_i], 1), jnp.concatenate([ei, -odd_r], 1)], 0
    )
    field = dot_split(mid, col_hi[...], col_lo[...])
    field_ref[...] = field
    real, imag = field[:spread_rows], field[spread_rows:]
    intensity = (real * real + imag * imag) * FIELD_SCALE
    blurred = dot_blur(intensity, blur_hi, blur_lo)
    widened = dot_blur(intensity, wide_hi, wide_lo)
    image_ref[...] = blurred * norm + scalar_ref[SKY : SKY + 1, :]
    width_ref[...] = (widened - blurred * mean) * (norm / scalar_ref[JITTER : JITTER + 1, :])
    for copy in copies:
        copy.wait()
    observed_ref[...] = observed_in[0]
    scale = 1.0 / (NR * math.sqrt(all_frames))
    weight_ref[...] = (mask_in[0] * count_in[0]).astype(f32) * scale


def bfe_weights():
    table = np.zeros((5, 5))
    for i in range(5):
        for j in range(5):
            distance = (i - 2) ** 2 + (j - 2) ** 2
            if distance > 0:
                table[i, j] = 1.0 / distance
    total = table.sum()
    return {d: float(np.float32(1.0 / d / total)) for d in (1, 2, 4, 5, 8)}


BFE = bfe_weights()


def gradient_kernel(
    beside_two,
    beside_one,
    near_ref,
    scalar_ref,
    observed_ref,
    weight_ref,
    image_ref,
    width_ref,
    field_ref,
    power_ref,
    norm_ref,
    blur_hi,
    blur_lo,
    col_hi,
    col_lo,
    maps_ref,
    pay_ref,
    *,
    rows,
    columns,
):
    spread_rows = rows + GUARD
    lane = iota((spread_rows, columns), 1)

    def across(x, k):
        moved = pltpu.roll(x, (-k) % columns, 1)
        return jnp.where(lane < columns - k if k > 0 else lane >= -k, moved, 0.0)

    def down(x, k):
        return pltpu.roll(x, (-k) % spread_rows, 0)

    def curve(x):
        one = across(x, 1) + across(x, -1)
        two = across(x, 2) + across(x, -2)
        near = BFE[1] * x + BFE[2] * one + BFE[5] * two
        far = BFE[4] * x + BFE[5] * one + BFE[8] * two
        own = BFE[1] * one + BFE[4] * two - x
        return own + (down(near, 1) + down(near, -1)) + (down(far, 2) + down(far, -2))

    kappa = [
        [scalar_ref[KAPPA + 3 * i + j : KAPPA + 3 * i + j + 1, :] for j in range(3)]
        for i in range(3)
    ]
    row8 = iota((GUARD, columns), 0)
    block = lax.axis_index(("map", "psf"))
    after = jnp.where(block + 1 < lax.axis_size(("map", "psf")), 1.0, 0.0)
    ahead = jnp.where(block > 0, 1.0, 0.0)
    beside = beside_one[...] + beside_two[...]
    beside = beside * jnp.where((row8 < 3) | (row8 == 4), after, ahead)
    guard = jnp.where((row8 == 3) | (row8 == 4), 0.0, beside)
    flat = jnp.concatenate([near_ref[0], guard], 0)
    guard = jnp.where((row8 == 0) | (row8 == 7), pltpu.roll(beside, 4, 0), 0.0)
    bfe = jnp.concatenate([near_ref[1], guard], 0)
    image = image_ref[...]
    charge = flat * image
    curvature = curve(charge)
    factor = 1.0 + bfe * curvature
    spread = charge * factor
    taps = (across(spread, -1), spread, across(spread, 1))
    lines = [sum(kappa[i][j] * taps[j] for j in range(3)) for i in range(3)]
    detected = down(lines[0], -1) + lines[1] + down(lines[2], 1)
    resid = weight_ref[...] * (detected[:rows] - observed_ref[...])
    resid = jnp.concatenate([resid, jnp.zeros((GUARD, columns), f32)], 0)
    back = (across(resid, 1), resid, across(resid, -1))
    lines = [sum(kappa[i][j] * back[j] for j in range(3)) for i in range(3)]
    spread_grad = down(lines[0], 1) + lines[1] + down(lines[2], -1)
    shifted = (down(resid, 1), resid, down(resid, -1))
    sums = []
    for i in range(3):
        for j in range(3):
            sums.append(jnp.sum(shifted[i] * taps[j], 0, keepdims=True))
    charge_curve = spread_grad * charge
    charge_grad = spread_grad * factor + curve(charge_curve * bfe)
    bfe_grad = charge_curve * curvature
    flat_grad = charge_grad * image
    image_grad = charge_grad * flat
    sums.append(jnp.sum(image_grad * width_ref[...], 0, keepdims=True))
    maps_ref[0] = flat_grad[:rows]
    maps_ref[1] = bfe_grad[:rows]
    guard = jnp.where(
        (row8 == 3) | (row8 == 4), pltpu.roll(bfe_grad[rows:], 4, 0), flat_grad[rows:]
    )
    pay_ref[:, :columns] = guard

    scaled = image_grad * norm_ref[0:1, :] * (2.0 * FIELD_SCALE)
    light = dot_blur(scaled, blur_hi, blur_lo)
    field = field_ref[...] * jnp.concatenate([light, light], 0)
    mid = dot_split(field, col_hi[...], col_lo[...], mm_nt)
    cos_r, sin_r = mid[:spread_rows, :HALF], mid[:spread_rows, HALF:]
    cos_i, sin_i = mid[spread_rows:, :HALF], mid[spread_rows:, HALF:]
    moments = []
    for p in range(6):
        blocks = [
            power_ref[p * spread_rows : (p + 1) * spread_rows, k * HALF : (k + 1) * HALF]
            for k in range(4)
        ]
        for q in range(2):
            one, two = blocks[2 * q : 2 * q + 2]
            three, four = blocks[2 - 2 * q : 4 - 2 * q]
            if p % 2:
                term = (cos_i * two + cos_r * one) + (sin_r * four - sin_i * three)
            else:
                term = (cos_i * one - cos_r * two) + (sin_r * three + sin_i * four)
            moments.append(jnp.sum(term, 0, keepdims=True))
    v = (2 * iota((1, HALF), 1) + 1).astype(f32) * (1.0 / NP)
    powers = [jnp.ones((1, HALF), f32)]
    for _ in range(5):
        powers.append(powers[-1] * v)
    zern = [moments[2 * p + q % 2] * powers[q] for p, q in MODES]
    for line in sums:
        total = line[:, :HALF]
        for k in range(1, columns // HALF):
            total = total + line[:, k * HALF : (k + 1) * HALF]
        zern.append(total)
    stack = jnp.concatenate(zern + [jnp.zeros((32 - len(zern), HALF), f32)], 0)
    totals = jnp.sum(stack, 1, keepdims=True)
    lane8 = iota((8, HALF), 1)
    small = jnp.zeros((8, HALF), f32)
    places = [ZERN_LANE + k for k in range(21)] + [IPC_LANE + k for k in range(9)] + [JITTER_LANE]
    for k, place in enumerate(places):
        small = jnp.where(lane8 == place, totals[k : k + 1, :], small)
    pay_ref[:, columns:] = small


def vmem(count):
    return [pl.BlockSpec(memory_space=pltpu.VMEM)] * count


def xor_pairs(count, mask):
    return [(i, i ^ mask) for i in range(count)]


def guard_tile(top, bottom, columns):
    parts = [top[0, :3], bottom[1, -1:], top[1, :1], bottom[0, -3:]]
    return jnp.concatenate(parts, 0).reshape(GUARD, columns)


def gather_maps(flat_map, bfe_map, rows, pupil_beside):
    own, columns = flat_map.shape[1:]
    frames = lax.axis_size("frame")
    blocks = lax.axis_size(("map", "psf"))
    held = jnp.concatenate([flat_map, bfe_map], 0)[:, None]
    index = lax.axis_index("frame")
    step = frames // 2
    while step:
        if step == 1:
            held = pupil_beside(held)
        other = lax.ppermute(held, "frame", xor_pairs(frames, step))
        before = held
        held = jnp.where(
            (index & step) == 0,
            jnp.stack([held, other], 2),
            jnp.stack([other, held], 2),
        ).reshape((2, -1, own, columns))
        step //= 2
    maps = held.reshape(2, rows, columns)
    row = iota((GUARD, columns), 0)
    first = (row < 3) | (row == 4)
    everywhere = ("frame", "map", "psf")
    if own == GUARD and frames == 4:
        tile = guard_tile(before[:, 0], before[:, 1], columns)
        tile = jnp.where(first == ((index & 1) == 0), tile, 0.0)
        tiles = []
        for odd in (0, 1):
            pairs = []
            for f in range(frames):
                for b in range(blocks):
                    to = (b + 1 if f % 2 else b - 1) % blocks
                    pairs.append((f * blocks + b, (f ^ odd) * blocks + to))
            tiles.append(lax.ppermute(tile, everywhere, pairs))
        return maps, tiles
    tile = guard_tile(maps, maps, columns)
    after = lax.ppermute(tile, ("map", "psf"), [(b + 1, b) for b in range(blocks - 1)])
    ahead = lax.ppermute(tile, ("map", "psf"), [(b, b + 1) for b in range(blocks - 1)])
    return maps, [jnp.where(first, after, 0.0), jnp.where(first, 0.0, ahead)]


def edge_kernel(grads_ref, *refs):
    *got_refs, out_ref = refs
    rows, columns = grads_ref.shape[1:]
    block = lax.axis_index(("map", "psf"))
    upper = jnp.zeros((GUARD, columns), f32)
    lower = jnp.zeros((GUARD, columns), f32)
    for k, got_ref in enumerate(got_refs):
        partner = block ^ (2 ** (k + 1) - 1)
        edge = got_ref[:, :columns]
        upper = jnp.where(partner == block - 1, edge, upper)
        lower = jnp.where(partner == block + 1, edge, lower)
    row = iota((GUARD, columns), 0)
    out_ref[...] = grads_ref[...]
    out_ref[0, :GUARD] += jnp.where(row < 3, upper, 0.0)
    out_ref[0, rows - GUARD :] += jnp.where(row >= 5, lower, 0.0)
    out_ref[1, :GUARD] += jnp.where(row < 1, pltpu.roll(upper, 4, 0), 0.0)
    out_ref[1, rows - GUARD :] += jnp.where(row >= 7, pltpu.roll(lower, 4, 0), 0.0)


def finish_kernel(
    mine_ref, three_ref, two_ref, one_ref, small_ref, flat_ref, bfe_ref, ipc_ref, zern_ref, jitter_ref
):
    columns = flat_ref.shape[2]
    total = (mine_ref[...] + one_ref[...]) + (two_ref[...] + three_ref[...])
    flat_ref[0] = total[:, :columns]
    bfe_ref[0] = total[:, columns : 2 * columns]
    totals = total[:, 2 * columns :]
    zern_ref[...] = totals[0, ZERN_LANE : ZERN_LANE + 21]
    for i in range(3):
        first = IPC_LANE + 3 * i
        ipc_ref[i : i + 1, :] = totals[0:1, first : first + 3]
    jitter_ref[...] = small_ref[0, JITTER_LANE : JITTER_LANE + 1]


def local(
    observed,
    pixel_mask,
    ramp_counts,
    flat_map,
    bfe_map,
    ipc_kernel,
    zernike,
    jitter,
    sky_level,
    dither,
):
    _, rows, columns = observed.shape
    frames = lax.axis_size("frame")
    blocks = lax.axis_size(("map", "psf"))
    own = rows // frames
    spread_rows = rows + GUARD
    frame = lax.axis_index("frame")

    def array(shape, dtype=f32):
        return jax.ShapeDtypeStruct(shape, dtype)

    params = pltpu.CompilerParams(vmem_limit_bytes=16 * 2**20)
    little = pltpu.CompilerParams(vmem_limit_bytes=2 * 2**20)
    scalars, *fold = pl.pallas_call(
        lambda *refs: pupil_kernel(*refs, rows=rows, columns=columns),
        out_shape=[
            array((16, columns)),
            array((NP, 4 * HALF), bf16),
            array((NP, 4 * HALF), bf16),
        ],
        in_specs=vmem(4),
        out_specs=vmem(3),
        compiler_params=params,
        name="pupil",
    )(zernike[None], jnp.stack([jitter, sky_level], 1), dither, ipc_kernel)
    def pupil_beside(sent):
        nonlocal scalars
        sent, scalars = lax.optimization_barrier((sent, scalars))
        return sent

    maps, beside = gather_maps(flat_map, bfe_map, rows, pupil_beside)

    seen = pl.pallas_call(
        lambda *refs: field_kernel(*refs, rows=rows, columns=columns, all_frames=frames),
        out_shape=[
            array((rows, columns)),
            array((rows, columns)),
            array((spread_rows, columns)),
            array((spread_rows, columns)),
            array((2 * spread_rows, columns)),
            array((6 * spread_rows, 4 * HALF)),
            array((8, columns)),
            *[array((columns // 2, 3 * columns // 2), bf16)] * 2,
            *[array((NP, columns), bf16)] * 2,
        ],
        in_specs=vmem(1) + [pl.BlockSpec(memory_space=pltpu.HBM)] * 3 + vmem(2),
        out_specs=vmem(11),
        scratch_shapes=[
            pltpu.VMEM((columns // 2, 3 * columns // 2), bf16),
            pltpu.VMEM((columns // 2, 3 * columns // 2), bf16),
            pltpu.VMEM((1, rows, columns), f32),
            pltpu.VMEM((1, rows, columns), jnp.int32),
            pltpu.VMEM((1, rows, columns), jnp.int32),
            pltpu.SemaphoreType.DMA((3,)),
        ],
        compiler_params=params,
        name="field",
    )(scalars, observed, pixel_mask, ramp_counts, *fold)

    grads, pay = pl.pallas_call(
        lambda *refs: gradient_kernel(*refs, rows=rows, columns=columns),
        out_shape=[array((2, rows, columns)), array((8, columns + HALF))],
        in_specs=vmem(15),
        out_specs=vmem(2),
        compiler_params=params,
        name="gradient",
    )(beside[1], beside[0], maps, scalars, *seen)

    lane = iota(pay.shape, 1)
    gots = []
    step = 1
    while step < blocks:
        got = lax.ppermute(pay, ("map", "psf"), xor_pairs(blocks, 2 * step - 1))
        gots.append(got)
        pay = jnp.where(lane >= columns, pay + got, pay)
        step *= 2
    small = pay[:, columns:]
    grads = pl.pallas_call(
        edge_kernel,
        out_shape=array((2, rows, columns)),
        in_specs=vmem(1 + len(gots)),
        out_specs=pl.BlockSpec(memory_space=pltpu.VMEM),
        compiler_params=little,
        name="edges",
    )(grads, *gots)

    held = grads.reshape(2, frames, own, columns)
    wide = small[:own]

    def joined(piece, wide):
        return jnp.concatenate([*piece.reshape(-1, own, columns), wide], 1)

    step = 1
    while 4 * step < frames:
        bit = (frame & step) != 0
        pieces = held.reshape((2, -1, 2) + held.shape[2:])
        mine = jnp.where(bit, pieces[:, :, 1], pieces[:, :, 0])
        theirs = jnp.where(bit, pieces[:, :, 0], pieces[:, :, 1])
        got = lax.ppermute(joined(theirs, wide), "frame", xor_pairs(frames, step))
        step *= 2
        count = 2 * mine.shape[1]
        other = jnp.stack([got[:, k * columns : (k + 1) * columns] for k in range(count)])
        held = mine + other.reshape(mine.shape)
        wide = wide + got[:, count * columns :]
    place = frame // step
    gots = {}
    for other in (3, 2, 1):
        piece = lax.dynamic_index_in_dim(held, place ^ other, 1, keepdims=False)
        gots[other] = lax.ppermute(joined(piece, wide), "frame", xor_pairs(frames, other * step))
    mine = joined(lax.dynamic_index_in_dim(held, place, 1, keepdims=False), wide)
    return pl.pallas_call(
        finish_kernel,
        out_shape=[
            array((1, own, columns)),
            array((1, own, columns)),
            array((3, 3)),
            array((21,)),
            array((1,)),
        ],
        in_specs=vmem(5),
        out_specs=vmem(5),
        compiler_params=little,
        name="finish",
    )(mine, gots[3], gots[2], gots[1], small)


def solution(mesh):
    in_specs = (
        P(("groups", "frame"), ("map", "psf"), None),
        P(("groups", "frame"), ("map", "psf"), None),
        P(("groups", "frame"), ("map", "psf"), None),
        P(("groups", "map", "psf"), "frame", None),
        P(("groups", "map", "psf"), "frame", None),
        P("groups", None),
        P("groups"),
        P(("groups", "frame")),
        P(("groups", "frame")),
        P(("groups", "frame"), None),
    )
    out_specs = (
        P(("groups", "map", "psf"), "frame", None),
        P(("groups", "map", "psf"), "frame", None),
        P("groups", None),
        P("groups"),
        P(("groups", "frame")),
    )
    return jax.shard_map(local, mesh=mesh, in_specs=in_specs, out_specs=out_specs, check_vma=False)
```

```python
import math

import jax
import jax.numpy as jnp
import numpy as np
from jax import lax
from jax.experimental import pallas as pl
from jax.experimental.pallas import tpu as pltpu
from jax.sharding import PartitionSpec as P

NP = 256
HALF = NP // 2
NR = 16
OVERSAMPLE = 32
AMPLITUDE = 2.0
IPC_CENTER = 0.8
TURN = 2 * NP * OVERSAMPLE
FIELD_SCALE = (AMPLITUDE / NP**2) ** 2
GUARD = 8
ZERN_LANE, IPC_LANE, JITTER_LANE = 0, 32, 48
JITTER, SKY, ROW_START, COLUMN, KAPPA = range(5)

f32, bf16 = jnp.float32, jnp.bfloat16
MODES = [(p, d - p) for d in range(6) for p in range(d + 1)]


def sine_table():
    nodes = 0.125 + 0.125 * np.cos(np.pi * (np.arange(200) + 0.5) / 200)
    powers = np.stack([nodes ** (2 * k + 1) for k in range(5)], 1)
    return [float(c) for c in np.linalg.lstsq(powers, np.sin(2 * np.pi * nodes), rcond=None)[0]]


SINE = sine_table()


def sin_quarter(y):
    t = y * y
    poly = SINE[4]
    for c in SINE[3::-1]:
        poly = poly * t + c
    return poly * y


def cos_turn(x):
    return sin_quarter(0.25 - jnp.abs(x))


def sin_turn(x):
    return sin_quarter(jnp.minimum(jnp.maximum(x, -0.5 - x), 0.5 - x))


def turn_fraction(k):
    return (((k + TURN // 2) & (TURN - 1)) - TURN // 2).astype(f32) * (1.0 / TURN)


def iota(shape, axis):
    return lax.broadcasted_iota(jnp.int32, shape, axis)


def mm(a, b):
    return jnp.dot(a, b, preferred_element_type=f32)


def mm_nt(a, b):
    return lax.dot_general(a, b, (((1,), (1,)), ((), ())), preferred_element_type=f32)


def halves(x):
    high = x.astype(bf16)
    return high, (x - high.astype(f32)).astype(bf16)


def dot_blur(x, high, low):
    half = high.shape[0]
    left, right = x[:, :half], x[:, half:]
    rows = x.shape[0]
    both = dot_split(jnp.concatenate([left, right], 0), high[:, half : 2 * half], low[:, half : 2 * half])
    first = both[:rows] + dot_split(right, high[:, :half], low[:, :half])
    last = both[rows:] + dot_split(left, high[:, 2 * half :], low[:, 2 * half :])
    return jnp.concatenate([first, last], 1)


def dot_split(x, high, low, product=mm):
    rows = x.shape[0]
    top = x.astype(bf16)
    both = jnp.concatenate([top.astype(f32), x - top.astype(f32)], 0).astype(bf16)
    first = product(both, high)
    return first[:rows] + first[rows:] + product(top, low)


def pupil_kernel(
    zern_ref,
    level_ref,
    dither_ref,
    ipc_ref,
    scalar_ref,
    fold_hi,
    fold_lo,
    *,
    rows,
    columns,
):
    blocks = lax.axis_size(("map", "psf"))
    row_start = lax.axis_index(("map", "psf")) * rows - rows * blocks // 2 - dither_ref[:, 0:1]
    column = columns // 2 + dither_ref[:, 1:2]
    values = [level_ref[:, 0:1], level_ref[:, 1:2], row_start.astype(f32), column.astype(f32)]
    values += [
        ipc_ref[i : i + 1, j : j + 1] + (IPC_CENTER if i == j == 1 else 0.0)
        for i in range(3)
        for j in range(3)
    ]
    for k, value in enumerate(values):
        scalar_ref[k : k + 1, :] = jnp.broadcast_to(value, (1, columns))
    z = {
        mode: jnp.broadcast_to(zern_ref[:, k : k + 1], (16, HALF)) for k, mode in enumerate(MODES)
    }

    def pupil_step(step, carry):
        at = pl.multiple_of(step * 16, 16)
        j = iota((16, HALF), 0) + at
        l = iota((16, HALF), 1)
        u = (2 * j + 1).astype(f32) * (1.0 / NP)
        v = (2 * l + 1).astype(f32) * (1.0 / NP)
        uu, vv = u * u, v * v
        ee = (
            z[0, 0]
            + vv * (z[0, 2] + vv * z[0, 4])
            + uu * (z[2, 0] + vv * z[2, 2] + uu * z[4, 0])
        )
        oe = u * (
            z[1, 0]
            + vv * (z[1, 2] + vv * z[1, 4])
            + uu * (z[3, 0] + vv * z[3, 2] + uu * z[5, 0])
        )
        eo = v * (
            z[0, 1]
            + vv * (z[0, 3] + vv * z[0, 5])
            + uu * (z[2, 1] + vv * z[2, 3] + uu * z[4, 1])
        )
        oo = u * v * (z[1, 1] + vv * z[1, 3] + uu * z[3, 1])
        radius = uu + vv
        open_ = jnp.where((radius <= 1.0) & (radius >= 0.09), 1.0, 0.0).astype(f32)
        even, odd = (ee + eo, oe + oo), (ee - eo, oe - oo)
        phases = (even[0] + even[1], even[0] - even[1], odd[0] + odd[1], odd[0] - odd[1])
        real, imag = [], []
        for phase in phases:
            turns = phase * (0.5 / math.pi)
            turns = turns - jnp.floor(turns + 0.5)
            real.append(open_ * cos_turn(turns))
            imag.append(open_ * sin_turn(turns))

        def folds(x):
            a, b, c, d = x[0] + x[1], x[0] - x[1], x[2] + x[3], x[2] - x[3]
            return a + c, a - c, b + d, b - d

        ree, reo, roe, roo = folds(real)
        iee, ieo, ioe, ioo = folds(imag)
        for first, parts in ((0, (ree, iee, reo, ieo)), (HALF, (ioe, -roe, ioo, -roo))):
            for k, part in enumerate(parts):
                high, low = halves(part)
                fold_hi[pl.ds(first + at, 16), k * HALF : (k + 1) * HALF] = high
                fold_lo[pl.ds(first + at, 16), k * HALF : (k + 1) * HALF] = low
        return carry

    lax.fori_loop(0, HALF // 16, pupil_step, 0, unroll=True)


def field_kernel(
    scalar_ref,
    observed_any,
    mask_any,
    count_any,
    fold_hi,
    fold_lo,
    observed_ref,
    weight_ref,
    image_ref,
    width_ref,
    field_ref,
    power_ref,
    norm_ref,
    blur_hi,
    blur_lo,
    col_hi,
    col_lo,
    wide_hi,
    wide_lo,
    observed_in,
    mask_in,
    count_in,
    sems,
    *,
    rows,
    columns,
    all_frames,
):
    spread_rows = rows + GUARD
    copies = [
        pltpu.make_async_copy(source, target, sems.at[k])
        for k, (source, target) in enumerate(
            ((observed_any, observed_in), (mask_any, mask_in), (count_any, count_in))
        )
    ]
    for copy in copies:
        copy.start()

    def column_step(step, carry):
        at = pl.multiple_of(step * 16, 16)
        l = iota((16, columns), 0) + at
        c = iota((16, columns), 1) - scalar_ref[COLUMN : COLUMN + 1, :].astype(jnp.int32)
        x = turn_fraction((2 * l + 1) * c)
        high, low = halves(cos_turn(x))
        col_hi[pl.ds(at, 16), :] = high
        col_lo[pl.ds(at, 16), :] = low
        high, low = halves(sin_turn(x))
        col_hi[pl.ds(HALF + at, 16), :] = high
        col_lo[pl.ds(HALF + at, 16), :] = low
        return carry

    lax.fori_loop(0, HALF // 16, column_step, 0, unroll=True)

    jitter = scalar_ref[JITTER : JITTER + 1, :HALF]
    falloff = 0.5 / (jitter * jitter)
    falloff = jnp.concatenate([falloff] * (3 * columns // (2 * HALF) + 1), 1)

    half = columns // 2

    def blur_step(step, carry):
        total, wide_total = carry
        at = pl.multiple_of(step * 16, 16)
        shape = (16, 3 * half + HALF)
        d = (iota(shape, 0) + at - iota(shape, 1) + (half + HALF)).astype(f32)
        exponent = d * d * falloff
        value = jnp.exp(-exponent)
        wide = value * (exponent + exponent)
        held = []
        for table, refs in ((value, (blur_hi, blur_lo)), (wide, (wide_hi, wide_lo))):
            parts = halves(table)
            for ref, part in zip(refs, parts):
                ref[pl.ds(at, 16), :] = part[:, HALF:]
                ref[pl.ds(HALF + at, 16), :] = part[:, : 3 * half]
            held.append(parts[0].astype(f32) + parts[1].astype(f32))
        return total + held[0], wide_total + held[1]

    zero = jnp.zeros((16, 3 * half + HALF), f32)
    total, wide_total = lax.fori_loop(0, HALF // 16, blur_step, (zero, zero), unroll=True)
    total = total[:, HALF:] + total[:, : 3 * half]
    wide_total = wide_total[:, HALF:] + wide_total[:, : 3 * half]
    total = jnp.sum(total, 0, keepdims=True)
    wide_total = jnp.sum(wide_total, 0, keepdims=True)
    norm = 1.0 / (total[:, half:] + total[:, : 2 * half])
    mean = (wide_total[:, half:] + wide_total[:, : 2 * half]) * norm
    norm_ref[...] = jnp.broadcast_to(norm, (8, columns))

    i = iota((spread_rows, HALF), 0)
    i = jnp.where(i < rows + 4, i, i - spread_rows)
    n = i + scalar_ref[ROW_START : ROW_START + 1, :HALF].astype(jnp.int32)
    x = turn_fraction((2 * iota((spread_rows, HALF), 1) + 1) * n)
    cosine, sine = cos_turn(x), sin_turn(x)
    u = (2 * iota((spread_rows, HALF), 1) + 1).astype(f32) * (1.0 / NP)
    left = []
    for p in range(6):
        left.append(jnp.concatenate([sine, -cosine] if p % 2 else [cosine, sine], 1))
        cosine, sine = cosine * u, sine * u
    mid = dot_split(jnp.concatenate(left, 0), fold_hi[...], fold_lo[...])
    power_ref[...] = mid
    er, ei, odd_r, odd_i = (mid[:spread_rows, k * HALF : (k + 1) * HALF] for k in range(4))
    mid = jnp.concatenate(
        [jnp.concatenate([er, odd_i], 1), jnp.concatenate([ei, -odd_r], 1)], 0
    )
    field = dot_split(mid, col_hi[...], col_lo[...])
    field_ref[...] = field
    real, imag = field[:spread_rows], field[spread_rows:]
    intensity = (real * real + imag * imag) * FIELD_SCALE
    blurred = dot_blur(intensity, blur_hi, blur_lo)
    widened = dot_blur(intensity, wide_hi, wide_lo)
    image_ref[...] = blurred * norm + scalar_ref[SKY : SKY + 1, :]
    width_ref[...] = (widened - blurred * mean) * (norm / scalar_ref[JITTER : JITTER + 1, :])
    for copy in copies:
        copy.wait()
    observed_ref[...] = observed_in[0]
    scale = 1.0 / (NR * math.sqrt(all_frames))
    weight_ref[...] = (mask_in[0] * count_in[0]).astype(f32) * scale


def bfe_weights():
    table = np.zeros((5, 5))
    for i in range(5):
        for j in range(5):
            distance = (i - 2) ** 2 + (j - 2) ** 2
            if distance > 0:
                table[i, j] = 1.0 / distance
    total = table.sum()
    return {d: float(np.float32(1.0 / d / total)) for d in (1, 2, 4, 5, 8)}


BFE = bfe_weights()


def gradient_kernel(
    beside_two,
    beside_one,
    near_ref,
    scalar_ref,
    observed_ref,
    weight_ref,
    image_ref,
    width_ref,
    field_ref,
    power_ref,
    norm_ref,
    blur_hi,
    blur_lo,
    col_hi,
    col_lo,
    maps_ref,
    pay_ref,
    *,
    rows,
    columns,
):
    spread_rows = rows + GUARD
    lane = iota((spread_rows, columns), 1)

    def across(x, k):
        moved = pltpu.roll(x, (-k) % columns, 1)
        return jnp.where(lane < columns - k if k > 0 else lane >= -k, moved, 0.0)

    def down(x, k):
        return pltpu.roll(x, (-k) % spread_rows, 0)

    def curve(x):
        one = across(x, 1) + across(x, -1)
        two = across(x, 2) + across(x, -2)
        near = BFE[1] * x + BFE[2] * one + BFE[5] * two
        far = BFE[4] * x + BFE[5] * one + BFE[8] * two
        own = BFE[1] * one + BFE[4] * two - x
        return own + (down(near, 1) + down(near, -1)) + (down(far, 2) + down(far, -2))

    kappa = [
        [scalar_ref[KAPPA + 3 * i + j : KAPPA + 3 * i + j + 1, :] for j in range(3)]
        for i in range(3)
    ]
    row8 = iota((GUARD, columns), 0)
    block = lax.axis_index(("map", "psf"))
    after = jnp.where(block + 1 < lax.axis_size(("map", "psf")), 1.0, 0.0)
    ahead = jnp.where(block > 0, 1.0, 0.0)
    beside = beside_one[...] + beside_two[...]
    beside = beside * jnp.where((row8 < 3) | (row8 == 4), after, ahead)
    guard = jnp.where((row8 == 3) | (row8 == 4), 0.0, beside)
    flat = jnp.concatenate([near_ref[0], guard], 0)
    guard = jnp.where((row8 == 0) | (row8 == 7), pltpu.roll(beside, 4, 0), 0.0)
    bfe = jnp.concatenate([near_ref[1], guard], 0)
    image = image_ref[...]
    charge = flat * image
    curvature = curve(charge)
    factor = 1.0 + bfe * curvature
    spread = charge * factor
    taps = (across(spread, -1), spread, across(spread, 1))
    lines = [sum(kappa[i][j] * taps[j] for j in range(3)) for i in range(3)]
    detected = down(lines[0], -1) + lines[1] + down(lines[2], 1)
    resid = weight_ref[...] * (detected[:rows] - observed_ref[...])
    resid = jnp.concatenate([resid, jnp.zeros((GUARD, columns), f32)], 0)
    back = (across(resid, 1), resid, across(resid, -1))
    lines = [sum(kappa[i][j] * back[j] for j in range(3)) for i in range(3)]
    spread_grad = down(lines[0], 1) + lines[1] + down(lines[2], -1)
    shifted = (down(resid, 1), resid, down(resid, -1))
    sums = []
    for i in range(3):
        for j in range(3):
            sums.append(jnp.sum(shifted[i] * taps[j], 0, keepdims=True))
    charge_curve = spread_grad * charge
    charge_grad = spread_grad * factor + curve(charge_curve * bfe)
    bfe_grad = charge_curve * curvature
    flat_grad = charge_grad * image
    image_grad = charge_grad * flat
    sums.append(jnp.sum(image_grad * width_ref[...], 0, keepdims=True))
    maps_ref[0] = flat_grad[:rows]
    maps_ref[1] = bfe_grad[:rows]
    guard = jnp.where(
        (row8 == 3) | (row8 == 4), pltpu.roll(bfe_grad[rows:], 4, 0), flat_grad[rows:]
    )
    pay_ref[:, :columns] = guard

    scaled = image_grad * norm_ref[0:1, :] * (2.0 * FIELD_SCALE)
    light = dot_blur(scaled, blur_hi, blur_lo)
    field = field_ref[...] * jnp.concatenate([light, light], 0)
    mid = dot_split(field, col_hi[...], col_lo[...], mm_nt)
    cos_r, sin_r = mid[:spread_rows, :HALF], mid[:spread_rows, HALF:]
    cos_i, sin_i = mid[spread_rows:, :HALF], mid[spread_rows:, HALF:]
    moments = []
    for p in range(6):
        blocks = [
            power_ref[p * spread_rows : (p + 1) * spread_rows, k * HALF : (k + 1) * HALF]
            for k in range(4)
        ]
        for q in range(2):
            one, two = blocks[2 * q : 2 * q + 2]
            three, four = blocks[2 - 2 * q : 4 - 2 * q]
            if p % 2:
                term = (cos_i * two + cos_r * one) + (sin_r * four - sin_i * three)
            else:
                term = (cos_i * one - cos_r * two) + (sin_r * three + sin_i * four)
            moments.append(jnp.sum(term, 0, keepdims=True))
    v = (2 * iota((1, HALF), 1) + 1).astype(f32) * (1.0 / NP)
    powers = [jnp.ones((1, HALF), f32)]
    for _ in range(5):
        powers.append(powers[-1] * v)
    zern = [moments[2 * p + q % 2] * powers[q] for p, q in MODES]
    for line in sums:
        total = line[:, :HALF]
        for k in range(1, columns // HALF):
            total = total + line[:, k * HALF : (k + 1) * HALF]
        zern.append(total)
    stack = jnp.concatenate(zern + [jnp.zeros((32 - len(zern), HALF), f32)], 0)
    totals = jnp.sum(stack, 1, keepdims=True)
    lane8 = iota((8, HALF), 1)
    small = jnp.zeros((8, HALF), f32)
    places = [ZERN_LANE + k for k in range(21)] + [IPC_LANE + k for k in range(9)] + [JITTER_LANE]
    for k, place in enumerate(places):
        small = jnp.where(lane8 == place, totals[k : k + 1, :], small)
    pay_ref[:, columns:] = small


def vmem(count):
    return [pl.BlockSpec(memory_space=pltpu.VMEM)] * count


def xor_pairs(count, mask):
    return [(i, i ^ mask) for i in range(count)]


def guard_tile(top, bottom, columns):
    parts = [top[0, :3], bottom[1, -1:], top[1, :1], bottom[0, -3:]]
    return jnp.concatenate(parts, 0).reshape(GUARD, columns)


def gather_maps(flat_map, bfe_map, rows, pupil_beside):
    own, columns = flat_map.shape[1:]
    frames = lax.axis_size("frame")
    blocks = lax.axis_size(("map", "psf"))
    held = jnp.concatenate([flat_map, bfe_map], 0)[:, None]
    index = lax.axis_index("frame")
    step = frames // 2
    while step:
        if step == 1:
            held = pupil_beside(held)
        other = lax.ppermute(held, "frame", xor_pairs(frames, step))
        before = held
        held = jnp.where(
            (index & step) == 0,
            jnp.stack([held, other], 2),
            jnp.stack([other, held], 2),
        ).reshape((2, -1, own, columns))
        step //= 2
    maps = held.reshape(2, rows, columns)
    row = iota((GUARD, columns), 0)
    first = (row < 3) | (row == 4)
    everywhere = ("frame", "map", "psf")
    if own == GUARD and frames == 4:
        tile = guard_tile(before[:, 0], before[:, 1], columns)
        tile = jnp.where(first == ((index & 1) == 0), tile, 0.0)
        tiles = []
        for odd in (0, 1):
            pairs = []
            for f in range(frames):
                for b in range(blocks):
                    to = (b + 1 if f % 2 else b - 1) % blocks
                    pairs.append((f * blocks + b, (f ^ odd) * blocks + to))
            tiles.append(lax.ppermute(tile, everywhere, pairs))
        return maps, tiles
    tile = guard_tile(maps, maps, columns)
    after = lax.ppermute(tile, ("map", "psf"), [(b + 1, b) for b in range(blocks - 1)])
    ahead = lax.ppermute(tile, ("map", "psf"), [(b, b + 1) for b in range(blocks - 1)])
    return maps, [jnp.where(first, after, 0.0), jnp.where(first, 0.0, ahead)]


def edge_kernel(grads_ref, *refs):
    *got_refs, out_ref = refs
    rows, columns = grads_ref.shape[1:]
    block = lax.axis_index(("map", "psf"))
    upper = jnp.zeros((GUARD, columns), f32)
    lower = jnp.zeros((GUARD, columns), f32)
    for k, got_ref in enumerate(got_refs):
        partner = block ^ (2 ** (k + 1) - 1)
        edge = got_ref[:, :columns]
        upper = jnp.where(partner == block - 1, edge, upper)
        lower = jnp.where(partner == block + 1, edge, lower)
    row = iota((GUARD, columns), 0)
    out_ref[...] = grads_ref[...]
    out_ref[0, :GUARD] += jnp.where(row < 3, upper, 0.0)
    out_ref[0, rows - GUARD :] += jnp.where(row >= 5, lower, 0.0)
    out_ref[1, :GUARD] += jnp.where(row < 1, pltpu.roll(upper, 4, 0), 0.0)
    out_ref[1, rows - GUARD :] += jnp.where(row >= 7, pltpu.roll(lower, 4, 0), 0.0)


def finish_kernel(
    mine_ref, three_ref, two_ref, one_ref, small_ref, flat_ref, bfe_ref, ipc_ref, zern_ref, jitter_ref
):
    columns = flat_ref.shape[2]
    total = (mine_ref[...] + one_ref[...]) + (two_ref[...] + three_ref[...])
    flat_ref[0] = total[:, :columns]
    bfe_ref[0] = total[:, columns : 2 * columns]
    totals = total[:, 2 * columns :]
    zern_ref[...] = totals[0, ZERN_LANE : ZERN_LANE + 21]
    for i in range(3):
        first = IPC_LANE + 3 * i
        ipc_ref[i : i + 1, :] = totals[0:1, first : first + 3]
    jitter_ref[...] = small_ref[0, JITTER_LANE : JITTER_LANE + 1]


def local(
    observed,
    pixel_mask,
    ramp_counts,
    flat_map,
    bfe_map,
    ipc_kernel,
    zernike,
    jitter,
    sky_level,
    dither,
):
    _, rows, columns = observed.shape
    frames = lax.axis_size("frame")
    blocks = lax.axis_size(("map", "psf"))
    own = rows // frames
    spread_rows = rows + GUARD
    frame = lax.axis_index("frame")

    def array(shape, dtype=f32):
        return jax.ShapeDtypeStruct(shape, dtype)

    params = pltpu.CompilerParams(vmem_limit_bytes=16 * 2**20)
    little = pltpu.CompilerParams(vmem_limit_bytes=2 * 2**20)
    scalars, *fold = pl.pallas_call(
        lambda *refs: pupil_kernel(*refs, rows=rows, columns=columns),
        out_shape=[
            array((16, columns)),
            array((NP, 4 * HALF), bf16),
            array((NP, 4 * HALF), bf16),
        ],
        in_specs=vmem(4),
        out_specs=vmem(3),
        compiler_params=params,
        name="pupil",
    )(zernike[None], jnp.stack([jitter, sky_level], 1), dither, ipc_kernel)
    def pupil_beside(sent):
        nonlocal scalars
        sent, scalars = lax.optimization_barrier((sent, scalars))
        return sent

    maps, beside = gather_maps(flat_map, bfe_map, rows, pupil_beside)

    seen = pl.pallas_call(
        lambda *refs: field_kernel(*refs, rows=rows, columns=columns, all_frames=frames),
        out_shape=[
            array((rows, columns)),
            array((rows, columns)),
            array((spread_rows, columns)),
            array((spread_rows, columns)),
            array((2 * spread_rows, columns)),
            array((6 * spread_rows, 4 * HALF)),
            array((8, columns)),
            *[array((columns // 2, 3 * columns // 2), bf16)] * 2,
            *[array((NP, columns), bf16)] * 2,
        ],
        in_specs=vmem(1) + [pl.BlockSpec(memory_space=pltpu.HBM)] * 3 + vmem(2),
        out_specs=vmem(11),
        scratch_shapes=[
            pltpu.VMEM((columns // 2, 3 * columns // 2), bf16),
            pltpu.VMEM((columns // 2, 3 * columns // 2), bf16),
            pltpu.VMEM((1, rows, columns), f32),
            pltpu.VMEM((1, rows, columns), jnp.int32),
            pltpu.VMEM((1, rows, columns), jnp.int32),
            pltpu.SemaphoreType.DMA((3,)),
        ],
        compiler_params=params,
        name="field",
    )(scalars, observed, pixel_mask, ramp_counts, *fold)

    grads, pay = pl.pallas_call(
        lambda *refs: gradient_kernel(*refs, rows=rows, columns=columns),
        out_shape=[array((2, rows, columns)), array((8, columns + HALF))],
        in_specs=vmem(15),
        out_specs=vmem(2),
        compiler_params=params,
        name="gradient",
    )(beside[1], beside[0], maps, scalars, *seen)

    lane = iota(pay.shape, 1)
    gots = []
    step = 1
    while step < blocks:
        got = lax.ppermute(pay, ("map", "psf"), xor_pairs(blocks, 2 * step - 1))
        gots.append(got)
        pay = jnp.where(lane >= columns, pay + got, pay)
        step *= 2
    small = pay[:, columns:]
    grads = pl.pallas_call(
        edge_kernel,
        out_shape=array((2, rows, columns)),
        in_specs=vmem(1 + len(gots)),
        out_specs=pl.BlockSpec(memory_space=pltpu.VMEM),
        compiler_params=little,
        name="edges",
    )(grads, *gots)

    held = grads.reshape(2, frames, own, columns)
    wide = small[:own]

    def joined(piece, wide):
        return jnp.concatenate([*piece.reshape(-1, own, columns), wide], 1)

    step = 1
    while 4 * step < frames:
        bit = (frame & step) != 0
        pieces = held.reshape((2, -1, 2) + held.shape[2:])
        mine = jnp.where(bit, pieces[:, :, 1], pieces[:, :, 0])
        theirs = jnp.where(bit, pieces[:, :, 0], pieces[:, :, 1])
        got = lax.ppermute(joined(theirs, wide), "frame", xor_pairs(frames, step))
        step *= 2
        count = 2 * mine.shape[1]
        other = jnp.stack([got[:, k * columns : (k + 1) * columns] for k in range(count)])
        held = mine + other.reshape(mine.shape)
        wide = wide + got[:, count * columns :]
    place = frame // step
    gots = {}
    for other in (3, 2, 1):
        piece = lax.dynamic_index_in_dim(held, place ^ other, 1, keepdims=False)
        gots[other] = lax.ppermute(joined(piece, wide), "frame", xor_pairs(frames, other * step))
    mine = joined(lax.dynamic_index_in_dim(held, place, 1, keepdims=False), wide)
    return pl.pallas_call(
        finish_kernel,
        out_shape=[
            array((1, own, columns)),
            array((1, own, columns)),
            array((3, 3)),
            array((21,)),
            array((1,)),
        ],
        in_specs=vmem(5),
        out_specs=vmem(5),
        compiler_params=little,
        name="finish",
    )(mine, gots[3], gots[2], gots[1], small)


def solution(mesh):
    in_specs = (
        P(("groups", "frame"), ("map", "psf"), None),
        P(("groups", "frame"), ("map", "psf"), None),
        P(("groups", "frame"), ("map", "psf"), None),
        P(("groups", "map", "psf"), "frame", None),
        P(("groups", "map", "psf"), "frame", None),
        P("groups", None),
        P("groups"),
        P(("groups", "frame")),
        P(("groups", "frame")),
        P(("groups", "frame"), None),
    )
    out_specs = (
        P(("groups", "map", "psf"), "frame", None),
        P(("groups", "map", "psf"), "frame", None),
        P("groups", None),
        P("groups"),
        P(("groups", "frame")),
    )
    return jax.shard_map(local, mesh=mesh, in_specs=in_specs, out_specs=out_specs, check_vma=False)
```

```python
import math

import jax
import jax.numpy as jnp
import numpy as np
from jax import lax
from jax.experimental import pallas as pl
from jax.experimental.pallas import tpu as pltpu
from jax.sharding import PartitionSpec as P

NP = 256
HALF = NP // 2
NR = 16
OVERSAMPLE = 32
AMPLITUDE = 2.0
IPC_CENTER = 0.8
TURN = 2 * NP * OVERSAMPLE
FIELD_SCALE = (AMPLITUDE / NP**2) ** 2
GUARD = 8
ZERN_LANE, IPC_LANE, JITTER_LANE = 0, 32, 48
JITTER, SKY, ROW_START, COLUMN, KAPPA = range(5)

f32, bf16 = jnp.float32, jnp.bfloat16
MODES = [(p, d - p) for d in range(6) for p in range(d + 1)]


def sine_table():
    nodes = 0.125 + 0.125 * np.cos(np.pi * (np.arange(200) + 0.5) / 200)
    powers = np.stack([nodes ** (2 * k + 1) for k in range(5)], 1)
    return [float(c) for c in np.linalg.lstsq(powers, np.sin(2 * np.pi * nodes), rcond=None)[0]]


SINE = sine_table()


def sin_quarter(y):
    t = y * y
    poly = SINE[4]
    for c in SINE[3::-1]:
        poly = poly * t + c
    return poly * y


def cos_turn(x):
    return sin_quarter(0.25 - jnp.abs(x))


def sin_turn(x):
    return sin_quarter(jnp.minimum(jnp.maximum(x, -0.5 - x), 0.5 - x))


def turn_fraction(k):
    return (((k + TURN // 2) & (TURN - 1)) - TURN // 2).astype(f32) * (1.0 / TURN)


def iota(shape, axis):
    return lax.broadcasted_iota(jnp.int32, shape, axis)


def mm(a, b):
    return jnp.dot(a, b, preferred_element_type=f32)


def mm_nt(a, b):
    return lax.dot_general(a, b, (((1,), (1,)), ((), ())), preferred_element_type=f32)


def halves(x):
    high = x.astype(bf16)
    return high, (x - high.astype(f32)).astype(bf16)


def dot_blur(x, high, low):
    half = high.shape[0]
    left, right = x[:, :half], x[:, half:]
    rows = x.shape[0]
    both = dot_split(jnp.concatenate([left, right], 0), high[:, half : 2 * half], low[:, half : 2 * half])
    first = both[:rows] + dot_split(right, high[:, :half], low[:, :half])
    last = both[rows:] + dot_split(left, high[:, 2 * half :], low[:, 2 * half :])
    return jnp.concatenate([first, last], 1)


def dot_split(x, high, low, product=mm):
    rows = x.shape[0]
    top = x.astype(bf16)
    both = jnp.concatenate([top.astype(f32), x - top.astype(f32)], 0).astype(bf16)
    first = product(both, high)
    return first[:rows] + first[rows:] + product(top, low)


def pupil_kernel(
    zern_ref,
    level_ref,
    dither_ref,
    ipc_ref,
    scalar_ref,
    fold_hi,
    fold_lo,
    *,
    rows,
    columns,
):
    blocks = lax.axis_size(("map", "psf"))
    row_start = lax.axis_index(("map", "psf")) * rows - rows * blocks // 2 - dither_ref[:, 0:1]
    column = columns // 2 + dither_ref[:, 1:2]
    values = [level_ref[:, 0:1], level_ref[:, 1:2], row_start.astype(f32), column.astype(f32)]
    values += [
        ipc_ref[i : i + 1, j : j + 1] + (IPC_CENTER if i == j == 1 else 0.0)
        for i in range(3)
        for j in range(3)
    ]
    for k, value in enumerate(values):
        scalar_ref[k : k + 1, :] = jnp.broadcast_to(value, (1, columns))
    z = {
        mode: jnp.broadcast_to(zern_ref[:, k : k + 1], (16, HALF)) for k, mode in enumerate(MODES)
    }

    def pupil_step(step, carry):
        at = pl.multiple_of(step * 16, 16)
        j = iota((16, HALF), 0) + at
        l = iota((16, HALF), 1)
        u = (2 * j + 1).astype(f32) * (1.0 / NP)
        v = (2 * l + 1).astype(f32) * (1.0 / NP)
        uu, vv = u * u, v * v
        ee = (
            z[0, 0]
            + vv * (z[0, 2] + vv * z[0, 4])
            + uu * (z[2, 0] + vv * z[2, 2] + uu * z[4, 0])
        )
        oe = u * (
            z[1, 0]
            + vv * (z[1, 2] + vv * z[1, 4])
            + uu * (z[3, 0] + vv * z[3, 2] + uu * z[5, 0])
        )
        eo = v * (
            z[0, 1]
            + vv * (z[0, 3] + vv * z[0, 5])
            + uu * (z[2, 1] + vv * z[2, 3] + uu * z[4, 1])
        )
        oo = u * v * (z[1, 1] + vv * z[1, 3] + uu * z[3, 1])
        radius = uu + vv
        open_ = jnp.where((radius <= 1.0) & (radius >= 0.09), 1.0, 0.0).astype(f32)
        even, odd = (ee + eo, oe + oo), (ee - eo, oe - oo)
        phases = (even[0] + even[1], even[0] - even[1], odd[0] + odd[1], odd[0] - odd[1])
        real, imag = [], []
        for phase in phases:
            turns = phase * (0.5 / math.pi)
            turns = turns - jnp.floor(turns + 0.5)
            real.append(open_ * cos_turn(turns))
            imag.append(open_ * sin_turn(turns))

        def folds(x):
            a, b, c, d = x[0] + x[1], x[0] - x[1], x[2] + x[3], x[2] - x[3]
            return a + c, a - c, b + d, b - d

        ree, reo, roe, roo = folds(real)
        iee, ieo, ioe, ioo = folds(imag)
        for first, parts in ((0, (ree, iee, reo, ieo)), (HALF, (ioe, -roe, ioo, -roo))):
            for k, part in enumerate(parts):
                high, low = halves(part)
                fold_hi[pl.ds(first + at, 16), k * HALF : (k + 1) * HALF] = high
                fold_lo[pl.ds(first + at, 16), k * HALF : (k + 1) * HALF] = low
        return carry

    lax.fori_loop(0, HALF // 16, pupil_step, 0, unroll=True)


def field_kernel(
    scalar_ref,
    observed_any,
    mask_any,
    count_any,
    fold_hi,
    fold_lo,
    observed_ref,
    weight_ref,
    image_ref,
    width_ref,
    field_ref,
    power_ref,
    norm_ref,
    blur_hi,
    blur_lo,
    col_hi,
    col_lo,
    wide_hi,
    wide_lo,
    observed_in,
    mask_in,
    count_in,
    sems,
    *,
    rows,
    columns,
    all_frames,
):
    spread_rows = rows + GUARD
    copies = [
        pltpu.make_async_copy(source, target, sems.at[k])
        for k, (source, target) in enumerate(
            ((observed_any, observed_in), (mask_any, mask_in), (count_any, count_in))
        )
    ]
    for copy in copies:
        copy.start()

    def column_step(step, carry):
        at = pl.multiple_of(step * 16, 16)
        l = iota((16, columns), 0) + at
        c = iota((16, columns), 1) - scalar_ref[COLUMN : COLUMN + 1, :].astype(jnp.int32)
        x = turn_fraction((2 * l + 1) * c)
        high, low = halves(cos_turn(x))
        col_hi[pl.ds(at, 16), :] = high
        col_lo[pl.ds(at, 16), :] = low
        high, low = halves(sin_turn(x))
        col_hi[pl.ds(HALF + at, 16), :] = high
        col_lo[pl.ds(HALF + at, 16), :] = low
        return carry

    lax.fori_loop(0, HALF // 16, column_step, 0, unroll=True)

    jitter = scalar_ref[JITTER : JITTER + 1, :HALF]
    falloff = 0.5 / (jitter * jitter)
    falloff = jnp.concatenate([falloff] * (3 * columns // (2 * HALF) + 1), 1)

    half = columns // 2

    def blur_step(step, carry):
        total, wide_total = carry
        at = pl.multiple_of(step * 16, 16)
        shape = (16, 3 * half + HALF)
        d = (iota(shape, 0) + at - iota(shape, 1) + (half + HALF)).astype(f32)
        exponent = d * d * falloff
        value = jnp.exp(-exponent)
        wide = value * (exponent + exponent)
        held = []
        for table, refs in ((value, (blur_hi, blur_lo)), (wide, (wide_hi, wide_lo))):
            parts = halves(table)
            for ref, part in zip(refs, parts):
                ref[pl.ds(at, 16), :] = part[:, HALF:]
                ref[pl.ds(HALF + at, 16), :] = part[:, : 3 * half]
            held.append(parts[0].astype(f32) + parts[1].astype(f32))
        return total + held[0], wide_total + held[1]

    zero = jnp.zeros((16, 3 * half + HALF), f32)
    total, wide_total = lax.fori_loop(0, HALF // 16, blur_step, (zero, zero), unroll=True)
    total = total[:, HALF:] + total[:, : 3 * half]
    wide_total = wide_total[:, HALF:] + wide_total[:, : 3 * half]
    total = jnp.sum(total, 0, keepdims=True)
    wide_total = jnp.sum(wide_total, 0, keepdims=True)
    norm = 1.0 / (total[:, half:] + total[:, : 2 * half])
    mean = (wide_total[:, half:] + wide_total[:, : 2 * half]) * norm
    norm_ref[...] = jnp.broadcast_to(norm, (8, columns))

    i = iota((spread_rows, HALF), 0)
    i = jnp.where(i < rows + 4, i, i - spread_rows)
    n = i + scalar_ref[ROW_START : ROW_START + 1, :HALF].astype(jnp.int32)
    x = turn_fraction((2 * iota((spread_rows, HALF), 1) + 1) * n)
    cosine, sine = cos_turn(x), sin_turn(x)
    u = (2 * iota((spread_rows, HALF), 1) + 1).astype(f32) * (1.0 / NP)
    left = []
    for p in range(6):
        left.append(jnp.concatenate([sine, -cosine] if p % 2 else [cosine, sine], 1))
        cosine, sine = cosine * u, sine * u
    mid = dot_split(jnp.concatenate(left, 0), fold_hi[...], fold_lo[...])
    power_ref[...] = mid
    er, ei, odd_r, odd_i = (mid[:spread_rows, k * HALF : (k + 1) * HALF] for k in range(4))
    mid = jnp.concatenate(
        [jnp.concatenate([er, odd_i], 1), jnp.concatenate([ei, -odd_r], 1)], 0
    )
    field = dot_split(mid, col_hi[...], col_lo[...])
    field_ref[...] = field
    real, imag = field[:spread_rows], field[spread_rows:]
    intensity = (real * real + imag * imag) * FIELD_SCALE
    blurred = dot_blur(intensity, blur_hi, blur_lo)
    widened = dot_blur(intensity, wide_hi, wide_lo)
    image_ref[...] = blurred * norm + scalar_ref[SKY : SKY + 1, :]
    width_ref[...] = (widened - blurred * mean) * (norm / scalar_ref[JITTER : JITTER + 1, :])
    for copy in copies:
        copy.wait()
    observed_ref[...] = observed_in[0]
    scale = 1.0 / (NR * math.sqrt(all_frames))
    weight_ref[...] = (mask_in[0] * count_in[0]).astype(f32) * scale


def bfe_weights():
    table = np.zeros((5, 5))
    for i in range(5):
        for j in range(5):
            distance = (i - 2) ** 2 + (j - 2) ** 2
            if distance > 0:
                table[i, j] = 1.0 / distance
    total = table.sum()
    return {d: float(np.float32(1.0 / d / total)) for d in (1, 2, 4, 5, 8)}


BFE = bfe_weights()


def gradient_kernel(
    beside_two,
    beside_one,
    near_ref,
    scalar_ref,
    observed_ref,
    weight_ref,
    image_ref,
    width_ref,
    field_ref,
    power_ref,
    norm_ref,
    blur_hi,
    blur_lo,
    col_hi,
    col_lo,
    maps_ref,
    pay_ref,
    edge_ref,
    *,
    rows,
    columns,
):
    spread_rows = rows + GUARD
    lane = iota((spread_rows, columns), 1)

    def across(x, k):
        moved = pltpu.roll(x, (-k) % columns, 1)
        return jnp.where(lane < columns - k if k > 0 else lane >= -k, moved, 0.0)

    def down(x, k):
        return pltpu.roll(x, (-k) % spread_rows, 0)

    def curve(x):
        one = across(x, 1) + across(x, -1)
        two = across(x, 2) + across(x, -2)
        near = BFE[1] * x + BFE[2] * one + BFE[5] * two
        far = BFE[4] * x + BFE[5] * one + BFE[8] * two
        own = BFE[1] * one + BFE[4] * two - x
        return own + (down(near, 1) + down(near, -1)) + (down(far, 2) + down(far, -2))

    kappa = [
        [scalar_ref[KAPPA + 3 * i + j : KAPPA + 3 * i + j + 1, :] for j in range(3)]
        for i in range(3)
    ]
    row8 = iota((GUARD, columns), 0)
    block = lax.axis_index(("map", "psf"))
    after = jnp.where(block + 1 < lax.axis_size(("map", "psf")), 1.0, 0.0)
    ahead = jnp.where(block > 0, 1.0, 0.0)
    beside = beside_one[...] + beside_two[...]
    beside = beside * jnp.where((row8 < 3) | (row8 == 4), after, ahead)
    guard = jnp.where((row8 == 3) | (row8 == 4), 0.0, beside)
    flat = jnp.concatenate([near_ref[0], guard], 0)
    guard = jnp.where((row8 == 0) | (row8 == 7), pltpu.roll(beside, 4, 0), 0.0)
    bfe = jnp.concatenate([near_ref[1], guard], 0)
    image = image_ref[...]
    charge = flat * image
    curvature = curve(charge)
    factor = 1.0 + bfe * curvature
    spread = charge * factor
    taps = (across(spread, -1), spread, across(spread, 1))
    lines = [sum(kappa[i][j] * taps[j] for j in range(3)) for i in range(3)]
    detected = down(lines[0], -1) + lines[1] + down(lines[2], 1)
    resid = weight_ref[...] * (detected[:rows] - observed_ref[...])
    resid = jnp.concatenate([resid, jnp.zeros((GUARD, columns), f32)], 0)
    back = (across(resid, 1), resid, across(resid, -1))
    lines = [sum(kappa[i][j] * back[j] for j in range(3)) for i in range(3)]
    spread_grad = down(lines[0], 1) + lines[1] + down(lines[2], -1)
    shifted = (down(resid, 1), resid, down(resid, -1))
    sums = []
    for i in range(3):
        for j in range(3):
            sums.append(jnp.sum(shifted[i] * taps[j], 0, keepdims=True))
    charge_curve = spread_grad * charge
    charge_grad = spread_grad * factor + curve(charge_curve * bfe)
    bfe_grad = charge_curve * curvature
    flat_grad = charge_grad * image
    image_grad = charge_grad * flat
    sums.append(jnp.sum(image_grad * width_ref[...], 0, keepdims=True))
    lane8 = iota((8, HALF), 1)

    def placed(small, lines, places):
        pad = [jnp.zeros((-len(lines) % 8, HALF), f32)]
        totals = jnp.sum(jnp.concatenate(lines + pad, 0), 1, keepdims=True)
        for k, place in enumerate(places):
            small = jnp.where(lane8 == place, totals[k : k + 1, :], small)
        return small

    lines = []
    for line in sums:
        total = line[:, :HALF]
        for k in range(1, columns // HALF):
            total = total + line[:, k * HALF : (k + 1) * HALF]
        lines.append(total)
    places = [IPC_LANE + k for k in range(9)] + [JITTER_LANE]
    small = placed(jnp.zeros((8, HALF), f32), lines, places)
    maps_ref[0] = flat_grad[:rows]
    maps_ref[1] = bfe_grad[:rows]
    upper = jnp.concatenate([flat_grad[rows : rows + 3], bfe_grad[rows : rows + 1]], 0)
    lower = jnp.concatenate([flat_grad[rows + 5 :], bfe_grad[rows + 7 :]], 0)
    even = lax.rem(block, 2) == 0
    half = columns // 2
    for k, edge in enumerate((jnp.where(even, upper, lower), jnp.where(even, lower, upper))):
        edge = jnp.concatenate([edge[:, :half], edge[:, half:]], 0)
        if k:
            edge_ref[...] = edge
        else:
            pay_ref[:, :half] = edge

    scaled = image_grad * norm_ref[0:1, :] * (2.0 * FIELD_SCALE)
    light = dot_blur(scaled, blur_hi, blur_lo)
    field = field_ref[...] * jnp.concatenate([light, light], 0)
    mid = dot_split(field, col_hi[...], col_lo[...], mm_nt)
    cos_r, sin_r = mid[:spread_rows, :HALF], mid[:spread_rows, HALF:]
    cos_i, sin_i = mid[spread_rows:, :HALF], mid[spread_rows:, HALF:]
    moments = []
    for p in range(6):
        blocks = [
            power_ref[p * spread_rows : (p + 1) * spread_rows, k * HALF : (k + 1) * HALF]
            for k in range(4)
        ]
        for q in range(2):
            one, two = blocks[2 * q : 2 * q + 2]
            three, four = blocks[2 - 2 * q : 4 - 2 * q]
            if p % 2:
                term = (cos_i * two + cos_r * one) + (sin_r * four - sin_i * three)
            else:
                term = (cos_i * one - cos_r * two) + (sin_r * three + sin_i * four)
            moments.append(jnp.sum(term, 0, keepdims=True))
    v = (2 * iota((1, HALF), 1) + 1).astype(f32) * (1.0 / NP)
    powers = [jnp.ones((1, HALF), f32)]
    for _ in range(5):
        powers.append(powers[-1] * v)
    zern = [moments[2 * p + q % 2] * powers[q] for p, q in MODES]
    small = placed(small, zern, [ZERN_LANE + k for k in range(21)])
    pay_ref[:, half:] = small


def vmem(count):
    return [pl.BlockSpec(memory_space=pltpu.VMEM)] * count


def xor_pairs(count, mask):
    return [(i, i ^ mask) for i in range(count)]


def guard_tile(top, bottom, columns):
    parts = [top[0, :3], bottom[1, -1:], top[1, :1], bottom[0, -3:]]
    return jnp.concatenate(parts, 0).reshape(GUARD, columns)


def gather_maps(flat_map, bfe_map, rows, pupil_beside):
    own, columns = flat_map.shape[1:]
    frames = lax.axis_size("frame")
    blocks = lax.axis_size(("map", "psf"))
    held = jnp.concatenate([flat_map, bfe_map], 0)[:, None]
    index = lax.axis_index("frame")
    step = frames // 2
    while step:
        if step == 1:
            held = pupil_beside(held)
        other = lax.ppermute(held, "frame", xor_pairs(frames, step))
        before = held
        held = jnp.where(
            (index & step) == 0,
            jnp.stack([held, other], 2),
            jnp.stack([other, held], 2),
        ).reshape((2, -1, own, columns))
        step //= 2
    maps = held.reshape(2, rows, columns)
    row = iota((GUARD, columns), 0)
    first = (row < 3) | (row == 4)
    everywhere = ("frame", "map", "psf")
    if own == GUARD and frames == 4:
        tile = guard_tile(before[:, 0], before[:, 1], columns)
        tile = jnp.where(first == ((index & 1) == 0), tile, 0.0)
        tiles = []
        for odd in (0, 1):
            pairs = []
            for f in range(frames):
                for b in range(blocks):
                    to = (b + 1 if f % 2 else b - 1) % blocks
                    pairs.append((f * blocks + b, (f ^ odd) * blocks + to))
            tiles.append(lax.ppermute(tile, everywhere, pairs))
        return maps, tiles
    tile = guard_tile(maps, maps, columns)
    after = lax.ppermute(tile, ("map", "psf"), [(b + 1, b) for b in range(blocks - 1)])
    ahead = lax.ppermute(tile, ("map", "psf"), [(b, b + 1) for b in range(blocks - 1)])
    return maps, [jnp.where(first, after, 0.0), jnp.where(first, 0.0, ahead)]


def edge_kernel(grads_ref, *refs):
    *got_refs, out_ref = refs
    rows, columns = grads_ref.shape[1:]
    block = lax.axis_index(("map", "psf"))
    half = columns // 2
    before = jnp.zeros((GUARD, half), f32)
    after = jnp.zeros((GUARD, half), f32)
    for k, got_ref in enumerate(got_refs):
        partner = block ^ (2 ** (k + 1) - 1)
        edge = got_ref[:, :half]
        before = jnp.where(partner == block - 1, edge, before)
        after = jnp.where(partner == block + 1, edge, after)
    before = jnp.concatenate([before[:4], before[4:]], 1)
    after = jnp.concatenate([after[:4], after[4:]], 1)
    out_ref[...] = grads_ref[...]
    out_ref[0, :3] += before[:3]
    out_ref[1, :1] += before[3:]
    out_ref[0, rows - 3 :] += after[:3]
    out_ref[1, rows - 1 :] += after[3:]


def finish_kernel(
    mine_ref, three_ref, two_ref, one_ref, small_ref, flat_ref, bfe_ref, ipc_ref, zern_ref, jitter_ref
):
    columns = flat_ref.shape[2]
    total = (mine_ref[...] + one_ref[...]) + (two_ref[...] + three_ref[...])
    flat_ref[0] = total[:, :columns]
    bfe_ref[0] = total[:, columns : 2 * columns]
    totals = total[:, 2 * columns :]
    zern_ref[...] = totals[0, ZERN_LANE : ZERN_LANE + 21]
    for i in range(3):
        first = IPC_LANE + 3 * i
        ipc_ref[i : i + 1, :] = totals[0:1, first : first + 3]
    jitter_ref[...] = small_ref[0, JITTER_LANE : JITTER_LANE + 1]


def local(
    observed,
    pixel_mask,
    ramp_counts,
    flat_map,
    bfe_map,
    ipc_kernel,
    zernike,
    jitter,
    sky_level,
    dither,
):
    _, rows, columns = observed.shape
    frames = lax.axis_size("frame")
    blocks = lax.axis_size(("map", "psf"))
    own = rows // frames
    spread_rows = rows + GUARD
    frame = lax.axis_index("frame")

    def array(shape, dtype=f32):
        return jax.ShapeDtypeStruct(shape, dtype)

    params = pltpu.CompilerParams(vmem_limit_bytes=16 * 2**20)
    little = pltpu.CompilerParams(vmem_limit_bytes=2 * 2**20)
    scalars, *fold = pl.pallas_call(
        lambda *refs: pupil_kernel(*refs, rows=rows, columns=columns),
        out_shape=[
            array((16, columns)),
            array((NP, 4 * HALF), bf16),
            array((NP, 4 * HALF), bf16),
        ],
        in_specs=vmem(4),
        out_specs=vmem(3),
        compiler_params=params,
        name="pupil",
    )(zernike[None], jnp.stack([jitter, sky_level], 1), dither, ipc_kernel)
    def pupil_beside(sent):
        nonlocal scalars
        sent, scalars = lax.optimization_barrier((sent, scalars))
        return sent

    maps, beside = gather_maps(flat_map, bfe_map, rows, pupil_beside)

    seen = pl.pallas_call(
        lambda *refs: field_kernel(*refs, rows=rows, columns=columns, all_frames=frames),
        out_shape=[
            array((rows, columns)),
            array((rows, columns)),
            array((spread_rows, columns)),
            array((spread_rows, columns)),
            array((2 * spread_rows, columns)),
            array((6 * spread_rows, 4 * HALF)),
            array((8, columns)),
            *[array((columns // 2, 3 * columns // 2), bf16)] * 2,
            *[array((NP, columns), bf16)] * 2,
        ],
        in_specs=vmem(1) + [pl.BlockSpec(memory_space=pltpu.HBM)] * 3 + vmem(2),
        out_specs=vmem(11),
        scratch_shapes=[
            pltpu.VMEM((columns // 2, 3 * columns // 2), bf16),
            pltpu.VMEM((columns // 2, 3 * columns // 2), bf16),
            pltpu.VMEM((1, rows, columns), f32),
            pltpu.VMEM((1, rows, columns), jnp.int32),
            pltpu.VMEM((1, rows, columns), jnp.int32),
            pltpu.SemaphoreType.DMA((3,)),
        ],
        compiler_params=params,
        name="field",
    )(scalars, observed, pixel_mask, ramp_counts, *fold)

    grads, pay, edge = pl.pallas_call(
        lambda *refs: gradient_kernel(*refs, rows=rows, columns=columns),
        out_shape=[
            array((2, rows, columns)),
            array((8, columns // 2 + HALF)),
            array((8, columns // 2)),
        ],
        in_specs=vmem(15),
        out_specs=vmem(3),
        compiler_params=params,
        name="gradient",
    )(beside[1], beside[0], maps, scalars, *seen)

    gots = []
    small = pay[:, columns // 2 :]
    step = 1
    while step < blocks:
        if gots:
            pay = jnp.concatenate([edge, small], 1)
        got = lax.ppermute(pay, ("map", "psf"), xor_pairs(blocks, 2 * step - 1))
        gots.append(got)
        small = small + got[:, columns // 2 :]
        step *= 2
    grads = pl.pallas_call(
        edge_kernel,
        out_shape=array((2, rows, columns)),
        in_specs=vmem(1 + len(gots)),
        out_specs=pl.BlockSpec(memory_space=pltpu.VMEM),
        compiler_params=little,
        name="edges",
    )(grads, *gots)

    held = grads.reshape(2, frames, own, columns)
    wide = small[:own]

    def joined(piece, wide):
        return jnp.concatenate([*piece.reshape(-1, own, columns), wide], 1)

    step = 1
    while 4 * step < frames:
        bit = (frame & step) != 0
        pieces = held.reshape((2, -1, 2) + held.shape[2:])
        mine = jnp.where(bit, pieces[:, :, 1], pieces[:, :, 0])
        theirs = jnp.where(bit, pieces[:, :, 0], pieces[:, :, 1])
        got = lax.ppermute(joined(theirs, wide), "frame", xor_pairs(frames, step))
        step *= 2
        count = 2 * mine.shape[1]
        other = jnp.stack([got[:, k * columns : (k + 1) * columns] for k in range(count)])
        held = mine + other.reshape(mine.shape)
        wide = wide + got[:, count * columns :]
    place = frame // step
    gots = {}
    for other in (3, 2, 1):
        piece = lax.dynamic_index_in_dim(held, place ^ other, 1, keepdims=False)
        gots[other] = lax.ppermute(joined(piece, wide), "frame", xor_pairs(frames, other * step))
    mine = joined(lax.dynamic_index_in_dim(held, place, 1, keepdims=False), wide)
    return pl.pallas_call(
        finish_kernel,
        out_shape=[
            array((1, own, columns)),
            array((1, own, columns)),
            array((3, 3)),
            array((21,)),
            array((1,)),
        ],
        in_specs=vmem(5),
        out_specs=vmem(5),
        compiler_params=little,
        name="finish",
    )(mine, gots[3], gots[2], gots[1], small)


def solution(mesh):
    in_specs = (
        P(("groups", "frame"), ("map", "psf"), None),
        P(("groups", "frame"), ("map", "psf"), None),
        P(("groups", "frame"), ("map", "psf"), None),
        P(("groups", "map", "psf"), "frame", None),
        P(("groups", "map", "psf"), "frame", None),
        P("groups", None),
        P("groups"),
        P(("groups", "frame")),
        P(("groups", "frame")),
        P(("groups", "frame"), None),
    )
    out_specs = (
        P(("groups", "map", "psf"), "frame", None),
        P(("groups", "map", "psf"), "frame", None),
        P("groups", None),
        P("groups"),
        P(("groups", "frame")),
    )
    return jax.shard_map(local, mesh=mesh, in_specs=in_specs, out_specs=out_specs, check_vma=False)
```

```python
import math

import jax
import jax.numpy as jnp
import numpy as np
from jax import lax
from jax.experimental import pallas as pl
from jax.experimental.pallas import tpu as pltpu
from jax.sharding import PartitionSpec as P

NP = 256
HALF = NP // 2
NR = 16
OVERSAMPLE = 32
AMPLITUDE = 2.0
IPC_CENTER = 0.8
TURN = 2 * NP * OVERSAMPLE
FIELD_SCALE = (AMPLITUDE / NP**2) ** 2
GUARD = 8
ZERN_LANE, IPC_LANE, JITTER_LANE = 0, 32, 48
JITTER, SKY, ROW_START, COLUMN, KAPPA = range(5)

f32, bf16 = jnp.float32, jnp.bfloat16
MODES = [(p, d - p) for d in range(6) for p in range(d + 1)]


def sine_table():
    nodes = 0.125 + 0.125 * np.cos(np.pi * (np.arange(200) + 0.5) / 200)
    powers = np.stack([nodes ** (2 * k + 1) for k in range(5)], 1)
    return [float(c) for c in np.linalg.lstsq(powers, np.sin(2 * np.pi * nodes), rcond=None)[0]]


SINE = sine_table()


def sin_quarter(y):
    t = y * y
    poly = SINE[4]
    for c in SINE[3::-1]:
        poly = poly * t + c
    return poly * y


def cos_turn(x):
    return sin_quarter(0.25 - jnp.abs(x))


def sin_turn(x):
    return sin_quarter(jnp.minimum(jnp.maximum(x, -0.5 - x), 0.5 - x))


def turn_fraction(k):
    return (((k + TURN // 2) & (TURN - 1)) - TURN // 2).astype(f32) * (1.0 / TURN)


def iota(shape, axis):
    return lax.broadcasted_iota(jnp.int32, shape, axis)


def mm(a, b):
    return jnp.dot(a, b, preferred_element_type=f32)


def mm_nt(a, b):
    return lax.dot_general(a, b, (((1,), (1,)), ((), ())), preferred_element_type=f32)


def halves(x):
    high = x.astype(bf16)
    return high, (x - high.astype(f32)).astype(bf16)


def dot_blur(x, high, low):
    half = high.shape[0]
    left, right = x[:, :half], x[:, half:]
    rows = x.shape[0]
    both = dot_split(jnp.concatenate([left, right], 0), high[:, half : 2 * half], low[:, half : 2 * half])
    first = both[:rows] + dot_split(right, high[:, :half], low[:, :half])
    last = both[rows:] + dot_split(left, high[:, 2 * half :], low[:, 2 * half :])
    return jnp.concatenate([first, last], 1)


def dot_split(x, high, low, product=mm):
    rows = x.shape[0]
    top = x.astype(bf16)
    both = jnp.concatenate([top.astype(f32), x - top.astype(f32)], 0).astype(bf16)
    first = product(both, high)
    return first[:rows] + first[rows:] + product(top, low)


def pupil_kernel(
    zern_ref,
    level_ref,
    dither_ref,
    ipc_ref,
    scalar_ref,
    fold_hi,
    fold_lo,
    *,
    rows,
    columns,
):
    blocks = lax.axis_size(("map", "psf"))
    row_start = lax.axis_index(("map", "psf")) * rows - rows * blocks // 2 - dither_ref[:, 0:1]
    column = columns // 2 + dither_ref[:, 1:2]
    values = [level_ref[:, 0:1], level_ref[:, 1:2], row_start.astype(f32), column.astype(f32)]
    values += [
        ipc_ref[i : i + 1, j : j + 1] + (IPC_CENTER if i == j == 1 else 0.0)
        for i in range(3)
        for j in range(3)
    ]
    for k, value in enumerate(values):
        scalar_ref[k : k + 1, :] = jnp.broadcast_to(value, (1, columns))
    z = {
        mode: jnp.broadcast_to(zern_ref[:, k : k + 1], (16, HALF)) for k, mode in enumerate(MODES)
    }

    def pupil_step(step, carry):
        at = pl.multiple_of(step * 16, 16)
        j = iota((16, HALF), 0) + at
        l = iota((16, HALF), 1)
        u = (2 * j + 1).astype(f32) * (1.0 / NP)
        v = (2 * l + 1).astype(f32) * (1.0 / NP)
        uu, vv = u * u, v * v
        ee = (
            z[0, 0]
            + vv * (z[0, 2] + vv * z[0, 4])
            + uu * (z[2, 0] + vv * z[2, 2] + uu * z[4, 0])
        )
        oe = u * (
            z[1, 0]
            + vv * (z[1, 2] + vv * z[1, 4])
            + uu * (z[3, 0] + vv * z[3, 2] + uu * z[5, 0])
        )
        eo = v * (
            z[0, 1]
            + vv * (z[0, 3] + vv * z[0, 5])
            + uu * (z[2, 1] + vv * z[2, 3] + uu * z[4, 1])
        )
        oo = u * v * (z[1, 1] + vv * z[1, 3] + uu * z[3, 1])
        radius = uu + vv
        open_ = jnp.where((radius <= 1.0) & (radius >= 0.09), 1.0, 0.0).astype(f32)
        even, odd = (ee + eo, oe + oo), (ee - eo, oe - oo)
        phases = (even[0] + even[1], even[0] - even[1], odd[0] + odd[1], odd[0] - odd[1])
        real, imag = [], []
        for phase in phases:
            turns = phase * (0.5 / math.pi)
            turns = turns - jnp.floor(turns + 0.5)
            real.append(open_ * cos_turn(turns))
            imag.append(open_ * sin_turn(turns))

        def folds(x):
            a, b, c, d = x[0] + x[1], x[0] - x[1], x[2] + x[3], x[2] - x[3]
            return a + c, a - c, b + d, b - d

        ree, reo, roe, roo = folds(real)
        iee, ieo, ioe, ioo = folds(imag)
        for first, parts in ((0, (ree, iee, reo, ieo)), (HALF, (ioe, -roe, ioo, -roo))):
            for k, part in enumerate(parts):
                high, low = halves(part)
                fold_hi[pl.ds(first + at, 16), k * HALF : (k + 1) * HALF] = high
                fold_lo[pl.ds(first + at, 16), k * HALF : (k + 1) * HALF] = low
        return carry

    lax.fori_loop(0, HALF // 16, pupil_step, 0, unroll=True)


def field_kernel(
    scalar_ref,
    observed_any,
    mask_any,
    count_any,
    fold_hi,
    fold_lo,
    observed_ref,
    weight_ref,
    image_ref,
    width_ref,
    field_ref,
    power_ref,
    norm_ref,
    blur_hi,
    blur_lo,
    col_hi,
    col_lo,
    wide_hi,
    wide_lo,
    observed_in,
    mask_in,
    count_in,
    sems,
    *,
    rows,
    columns,
    all_frames,
):
    spread_rows = rows + GUARD
    copies = [
        pltpu.make_async_copy(source, target, sems.at[k])
        for k, (source, target) in enumerate(
            ((observed_any, observed_in), (mask_any, mask_in), (count_any, count_in))
        )
    ]
    for copy in copies:
        copy.start()

    def column_step(step, carry):
        at = pl.multiple_of(step * 16, 16)
        l = iota((16, columns), 0) + at
        c = iota((16, columns), 1) - scalar_ref[COLUMN : COLUMN + 1, :].astype(jnp.int32)
        x = turn_fraction((2 * l + 1) * c)
        high, low = halves(cos_turn(x))
        col_hi[pl.ds(at, 16), :] = high
        col_lo[pl.ds(at, 16), :] = low
        high, low = halves(sin_turn(x))
        col_hi[pl.ds(HALF + at, 16), :] = high
        col_lo[pl.ds(HALF + at, 16), :] = low
        return carry

    lax.fori_loop(0, HALF // 16, column_step, 0, unroll=True)

    jitter = scalar_ref[JITTER : JITTER + 1, :HALF]
    falloff = 0.5 / (jitter * jitter)
    falloff = jnp.concatenate([falloff] * (3 * columns // (2 * HALF) + 1), 1)

    half = columns // 2

    def blur_step(step, carry):
        total, wide_total = carry
        at = pl.multiple_of(step * 16, 16)
        shape = (16, 3 * half + HALF)
        d = (iota(shape, 0) + at - iota(shape, 1) + (half + HALF)).astype(f32)
        exponent = d * d * falloff
        value = jnp.exp(-exponent)
        wide = value * (exponent + exponent)
        held = []
        for table, refs in ((value, (blur_hi, blur_lo)), (wide, (wide_hi, wide_lo))):
            parts = halves(table)
            for ref, part in zip(refs, parts):
                ref[pl.ds(at, 16), :] = part[:, HALF:]
                ref[pl.ds(HALF + at, 16), :] = part[:, : 3 * half]
            held.append(parts[0].astype(f32) + parts[1].astype(f32))
        return total + held[0], wide_total + held[1]

    zero = jnp.zeros((16, 3 * half + HALF), f32)
    total, wide_total = lax.fori_loop(0, HALF // 16, blur_step, (zero, zero), unroll=True)
    total = total[:, HALF:] + total[:, : 3 * half]
    wide_total = wide_total[:, HALF:] + wide_total[:, : 3 * half]
    total = jnp.sum(total, 0, keepdims=True)
    wide_total = jnp.sum(wide_total, 0, keepdims=True)
    norm = 1.0 / (total[:, half:] + total[:, : 2 * half])
    mean = (wide_total[:, half:] + wide_total[:, : 2 * half]) * norm
    norm_ref[...] = jnp.broadcast_to(norm, (8, columns))

    i = iota((spread_rows, HALF), 0)
    i = jnp.where(i < rows + 4, i, i - spread_rows)
    n = i + scalar_ref[ROW_START : ROW_START + 1, :HALF].astype(jnp.int32)
    x = turn_fraction((2 * iota((spread_rows, HALF), 1) + 1) * n)
    cosine, sine = cos_turn(x), sin_turn(x)
    u = (2 * iota((spread_rows, HALF), 1) + 1).astype(f32) * (1.0 / NP)
    left = []
    for p in range(6):
        left.append(jnp.concatenate([sine, -cosine] if p % 2 else [cosine, sine], 1))
        cosine, sine = cosine * u, sine * u
    mid = dot_split(jnp.concatenate(left, 0), fold_hi[...], fold_lo[...])
    power_ref[...] = mid
    er, ei, odd_r, odd_i = (mid[:spread_rows, k * HALF : (k + 1) * HALF] for k in range(4))
    mid = jnp.concatenate(
        [jnp.concatenate([er, odd_i], 1), jnp.concatenate([ei, -odd_r], 1)], 0
    )
    field = dot_split(mid, col_hi[...], col_lo[...])
    field_ref[...] = field
    real, imag = field[:spread_rows], field[spread_rows:]
    intensity = (real * real + imag * imag) * FIELD_SCALE
    blurred = dot_blur(intensity, blur_hi, blur_lo)
    widened = dot_blur(intensity, wide_hi, wide_lo)
    image_ref[...] = blurred * norm + scalar_ref[SKY : SKY + 1, :]
    width_ref[...] = (widened - blurred * mean) * (norm / scalar_ref[JITTER : JITTER + 1, :])
    for copy in copies:
        copy.wait()
    observed_ref[...] = observed_in[0]
    scale = 1.0 / (NR * math.sqrt(all_frames))
    weight_ref[...] = (mask_in[0] * count_in[0]).astype(f32) * scale


def bfe_weights():
    table = np.zeros((5, 5))
    for i in range(5):
        for j in range(5):
            distance = (i - 2) ** 2 + (j - 2) ** 2
            if distance > 0:
                table[i, j] = 1.0 / distance
    total = table.sum()
    return {d: float(np.float32(1.0 / d / total)) for d in (1, 2, 4, 5, 8)}


BFE = bfe_weights()


def gradient_kernel(
    beside_two,
    beside_one,
    near_ref,
    scalar_ref,
    observed_ref,
    weight_ref,
    image_ref,
    width_ref,
    field_ref,
    power_ref,
    norm_ref,
    blur_hi,
    blur_lo,
    col_hi,
    col_lo,
    maps_ref,
    pay_ref,
    edge_ref,
    *,
    rows,
    columns,
):
    spread_rows = rows + GUARD
    lane = iota((spread_rows, columns), 1)

    def across(x, k):
        moved = pltpu.roll(x, (-k) % columns, 1)
        return jnp.where(lane < columns - k if k > 0 else lane >= -k, moved, 0.0)

    def down(x, k):
        return pltpu.roll(x, (-k) % spread_rows, 0)

    def curve(x):
        one = across(x, 1) + across(x, -1)
        two = across(x, 2) + across(x, -2)
        near = BFE[1] * x + BFE[2] * one + BFE[5] * two
        far = BFE[4] * x + BFE[5] * one + BFE[8] * two
        own = BFE[1] * one + BFE[4] * two - x
        return own + (down(near, 1) + down(near, -1)) + (down(far, 2) + down(far, -2))

    kappa = [
        [scalar_ref[KAPPA + 3 * i + j : KAPPA + 3 * i + j + 1, :] for j in range(3)]
        for i in range(3)
    ]
    block = lax.axis_index(("map", "psf"))
    after = jnp.where(block + 1 < lax.axis_size(("map", "psf")), 1.0, 0.0)
    ahead = jnp.where(block > 0, 1.0, 0.0)
    even = lax.rem(lax.axis_index("frame"), 2) == 0
    one, two = beside_one[...], beside_two[...]
    top = jnp.where(even, one, two) * after
    bottom = jnp.where(even, two, one) * ahead
    top = jnp.concatenate([top[:4], top[4:]], 1)
    bottom = jnp.concatenate([bottom[:4], bottom[4:]], 1)
    gap = jnp.zeros((6, columns), f32)
    flat = jnp.concatenate([near_ref[0], top[:3], gap[:2], bottom[:3]], 0)
    bfe = jnp.concatenate([near_ref[1], top[3:], gap, bottom[3:]], 0)
    image = image_ref[...]
    charge = flat * image
    curvature = curve(charge)
    factor = 1.0 + bfe * curvature
    spread = charge * factor
    taps = (across(spread, -1), spread, across(spread, 1))
    lines = [sum(kappa[i][j] * taps[j] for j in range(3)) for i in range(3)]
    detected = down(lines[0], -1) + lines[1] + down(lines[2], 1)
    resid = weight_ref[...] * (detected[:rows] - observed_ref[...])
    resid = jnp.concatenate([resid, jnp.zeros((GUARD, columns), f32)], 0)
    back = (across(resid, 1), resid, across(resid, -1))
    lines = [sum(kappa[i][j] * back[j] for j in range(3)) for i in range(3)]
    spread_grad = down(lines[0], 1) + lines[1] + down(lines[2], -1)
    shifted = (down(resid, 1), resid, down(resid, -1))
    sums = []
    for i in range(3):
        for j in range(3):
            sums.append(jnp.sum(shifted[i] * taps[j], 0, keepdims=True))
    charge_curve = spread_grad * charge
    charge_grad = spread_grad * factor + curve(charge_curve * bfe)
    bfe_grad = charge_curve * curvature
    flat_grad = charge_grad * image
    image_grad = charge_grad * flat
    sums.append(jnp.sum(image_grad * width_ref[...], 0, keepdims=True))
    lane8 = iota((8, HALF), 1)

    def placed(small, lines, places):
        pad = [jnp.zeros((-len(lines) % 8, HALF), f32)]
        totals = jnp.sum(jnp.concatenate(lines + pad, 0), 1, keepdims=True)
        for k, place in enumerate(places):
            small = jnp.where(lane8 == place, totals[k : k + 1, :], small)
        return small

    lines = []
    for line in sums:
        total = line[:, :HALF]
        for k in range(1, columns // HALF):
            total = total + line[:, k * HALF : (k + 1) * HALF]
        lines.append(total)
    places = [IPC_LANE + k for k in range(9)] + [JITTER_LANE]
    small = placed(jnp.zeros((8, HALF), f32), lines, places)
    maps_ref[0] = flat_grad[:rows]
    maps_ref[1] = bfe_grad[:rows]
    upper = jnp.concatenate([flat_grad[rows : rows + 3], bfe_grad[rows : rows + 1]], 0)
    lower = jnp.concatenate([flat_grad[rows + 5 :], bfe_grad[rows + 7 :]], 0)
    even = lax.rem(block, 2) == 0
    half = columns // 2
    for k, edge in enumerate((jnp.where(even, upper, lower), jnp.where(even, lower, upper))):
        edge = jnp.concatenate([edge[:, :half], edge[:, half:]], 0)
        if k:
            edge_ref[...] = edge
        else:
            pay_ref[:, :half] = edge

    scaled = image_grad * norm_ref[0:1, :] * (2.0 * FIELD_SCALE)
    light = dot_blur(scaled, blur_hi, blur_lo)
    field = field_ref[...] * jnp.concatenate([light, light], 0)
    mid = dot_split(field, col_hi[...], col_lo[...], mm_nt)
    cos_r, sin_r = mid[:spread_rows, :HALF], mid[:spread_rows, HALF:]
    cos_i, sin_i = mid[spread_rows:, :HALF], mid[spread_rows:, HALF:]
    moments = []
    for p in range(6):
        blocks = [
            power_ref[p * spread_rows : (p + 1) * spread_rows, k * HALF : (k + 1) * HALF]
            for k in range(4)
        ]
        for q in range(2):
            one, two = blocks[2 * q : 2 * q + 2]
            three, four = blocks[2 - 2 * q : 4 - 2 * q]
            if p % 2:
                term = (cos_i * two + cos_r * one) + (sin_r * four - sin_i * three)
            else:
                term = (cos_i * one - cos_r * two) + (sin_r * three + sin_i * four)
            moments.append(jnp.sum(term, 0, keepdims=True))
    v = (2 * iota((1, HALF), 1) + 1).astype(f32) * (1.0 / NP)
    powers = [jnp.ones((1, HALF), f32)]
    for _ in range(5):
        powers.append(powers[-1] * v)
    zern = [moments[2 * p + q % 2] * powers[q] for p, q in MODES]
    small = placed(small, zern, [ZERN_LANE + k for k in range(21)])
    pay_ref[:, half:] = small


def vmem(count):
    return [pl.BlockSpec(memory_space=pltpu.VMEM)] * count


def xor_pairs(count, mask):
    return [(i, i ^ mask) for i in range(count)]


def edge_rows(top, bottom):
    half = top.shape[-1] // 2
    edges = (
        jnp.concatenate([top[0, :3], top[1, :1]], 0),
        jnp.concatenate([bottom[0, -3:], bottom[1, -1:]], 0),
    )
    return [jnp.concatenate([edge[:, :half], edge[:, half:]], 0) for edge in edges]


def gather_maps(flat_map, bfe_map, rows, pupil_beside):
    own, columns = flat_map.shape[1:]
    frames = lax.axis_size("frame")
    blocks = lax.axis_size(("map", "psf"))
    held = jnp.concatenate([flat_map, bfe_map], 0)[:, None]
    index = lax.axis_index("frame")
    step = frames // 2
    while step:
        if step == 1:
            held = pupil_beside(held)
        other = lax.ppermute(held, "frame", xor_pairs(frames, step))
        before = held
        held = jnp.where(
            (index & step) == 0,
            jnp.stack([held, other], 2),
            jnp.stack([other, held], 2),
        ).reshape((2, -1, own, columns))
        step //= 2
    maps = held.reshape(2, rows, columns)
    even = (index & 1) == 0
    everywhere = ("frame", "map", "psf")
    if own == GUARD and frames == 4:
        first, last = edge_rows(before[:, 0], before[:, 1])
        tile = jnp.where(even, first, last)
        tiles = []
        for odd in (0, 1):
            pairs = []
            for f in range(frames):
                for b in range(blocks):
                    to = (b + 1 if f % 2 else b - 1) % blocks
                    pairs.append((f * blocks + b, (f ^ odd) * blocks + to))
            tiles.append(lax.ppermute(tile, everywhere, pairs))
        return maps, tiles
    first, last = edge_rows(maps, maps)
    after = lax.ppermute(first, ("map", "psf"), [(b + 1, b) for b in range(blocks - 1)])
    ahead = lax.ppermute(last, ("map", "psf"), [(b, b + 1) for b in range(blocks - 1)])
    return maps, [jnp.where(even, after, ahead), jnp.where(even, ahead, after)]


def edge_kernel(grads_ref, *refs):
    *got_refs, out_ref = refs
    rows, columns = grads_ref.shape[1:]
    block = lax.axis_index(("map", "psf"))
    half = columns // 2
    before = jnp.zeros((GUARD, half), f32)
    after = jnp.zeros((GUARD, half), f32)
    for k, got_ref in enumerate(got_refs):
        partner = block ^ (2 ** (k + 1) - 1)
        edge = got_ref[:, :half]
        before = jnp.where(partner == block - 1, edge, before)
        after = jnp.where(partner == block + 1, edge, after)
    before = jnp.concatenate([before[:4], before[4:]], 1)
    after = jnp.concatenate([after[:4], after[4:]], 1)
    out_ref[...] = grads_ref[...]
    out_ref[0, :3] += before[:3]
    out_ref[1, :1] += before[3:]
    out_ref[0, rows - 3 :] += after[:3]
    out_ref[1, rows - 1 :] += after[3:]


def finish_kernel(
    mine_ref, three_ref, two_ref, one_ref, small_ref, flat_ref, bfe_ref, ipc_ref, zern_ref, jitter_ref
):
    columns = flat_ref.shape[2]
    total = (mine_ref[...] + one_ref[...]) + (two_ref[...] + three_ref[...])
    flat_ref[0] = total[:, :columns]
    bfe_ref[0] = total[:, columns : 2 * columns]
    totals = total[:, 2 * columns :]
    zern_ref[...] = totals[0, ZERN_LANE : ZERN_LANE + 21]
    for i in range(3):
        first = IPC_LANE + 3 * i
        ipc_ref[i : i + 1, :] = totals[0:1, first : first + 3]
    jitter_ref[...] = small_ref[0, JITTER_LANE : JITTER_LANE + 1]


def local(
    observed,
    pixel_mask,
    ramp_counts,
    flat_map,
    bfe_map,
    ipc_kernel,
    zernike,
    jitter,
    sky_level,
    dither,
):
    _, rows, columns = observed.shape
    frames = lax.axis_size("frame")
    blocks = lax.axis_size(("map", "psf"))
    own = rows // frames
    spread_rows = rows + GUARD
    frame = lax.axis_index("frame")

    def array(shape, dtype=f32):
        return jax.ShapeDtypeStruct(shape, dtype)

    params = pltpu.CompilerParams(vmem_limit_bytes=16 * 2**20)
    little = pltpu.CompilerParams(vmem_limit_bytes=2 * 2**20)
    scalars, *fold = pl.pallas_call(
        lambda *refs: pupil_kernel(*refs, rows=rows, columns=columns),
        out_shape=[
            array((16, columns)),
            array((NP, 4 * HALF), bf16),
            array((NP, 4 * HALF), bf16),
        ],
        in_specs=vmem(4),
        out_specs=vmem(3),
        compiler_params=params,
        name="pupil",
    )(zernike[None], jnp.stack([jitter, sky_level], 1), dither, ipc_kernel)
    def pupil_beside(sent):
        nonlocal scalars
        sent, scalars = lax.optimization_barrier((sent, scalars))
        return sent

    maps, beside = gather_maps(flat_map, bfe_map, rows, pupil_beside)

    seen = pl.pallas_call(
        lambda *refs: field_kernel(*refs, rows=rows, columns=columns, all_frames=frames),
        out_shape=[
            array((rows, columns)),
            array((rows, columns)),
            array((spread_rows, columns)),
            array((spread_rows, columns)),
            array((2 * spread_rows, columns)),
            array((6 * spread_rows, 4 * HALF)),
            array((8, columns)),
            *[array((columns // 2, 3 * columns // 2), bf16)] * 2,
            *[array((NP, columns), bf16)] * 2,
        ],
        in_specs=vmem(1) + [pl.BlockSpec(memory_space=pltpu.HBM)] * 3 + vmem(2),
        out_specs=vmem(11),
        scratch_shapes=[
            pltpu.VMEM((columns // 2, 3 * columns // 2), bf16),
            pltpu.VMEM((columns // 2, 3 * columns // 2), bf16),
            pltpu.VMEM((1, rows, columns), f32),
            pltpu.VMEM((1, rows, columns), jnp.int32),
            pltpu.VMEM((1, rows, columns), jnp.int32),
            pltpu.SemaphoreType.DMA((3,)),
        ],
        compiler_params=params,
        name="field",
    )(scalars, observed, pixel_mask, ramp_counts, *fold)

    grads, pay, edge = pl.pallas_call(
        lambda *refs: gradient_kernel(*refs, rows=rows, columns=columns),
        out_shape=[
            array((2, rows, columns)),
            array((8, columns // 2 + HALF)),
            array((8, columns // 2)),
        ],
        in_specs=vmem(15),
        out_specs=vmem(3),
        compiler_params=params,
        name="gradient",
    )(beside[1], beside[0], maps, scalars, *seen)

    gots = []
    small = pay[:, columns // 2 :]
    step = 1
    while step < blocks:
        if gots:
            pay = jnp.concatenate([edge, small], 1)
        got = lax.ppermute(pay, ("map", "psf"), xor_pairs(blocks, 2 * step - 1))
        gots.append(got)
        small = small + got[:, columns // 2 :]
        step *= 2
    grads = pl.pallas_call(
        edge_kernel,
        out_shape=array((2, rows, columns)),
        in_specs=vmem(1 + len(gots)),
        out_specs=pl.BlockSpec(memory_space=pltpu.VMEM),
        compiler_params=little,
        name="edges",
    )(grads, *gots)

    held = grads.reshape(2, frames, own, columns)
    wide = small[:own]

    def joined(piece, wide):
        return jnp.concatenate([*piece.reshape(-1, own, columns), wide], 1)

    step = 1
    while 4 * step < frames:
        bit = (frame & step) != 0
        pieces = held.reshape((2, -1, 2) + held.shape[2:])
        mine = jnp.where(bit, pieces[:, :, 1], pieces[:, :, 0])
        theirs = jnp.where(bit, pieces[:, :, 0], pieces[:, :, 1])
        got = lax.ppermute(joined(theirs, wide), "frame", xor_pairs(frames, step))
        step *= 2
        count = 2 * mine.shape[1]
        other = jnp.stack([got[:, k * columns : (k + 1) * columns] for k in range(count)])
        held = mine + other.reshape(mine.shape)
        wide = wide + got[:, count * columns :]
    place = frame // step
    gots = {}
    for other in (3, 2, 1):
        piece = lax.dynamic_index_in_dim(held, place ^ other, 1, keepdims=False)
        gots[other] = lax.ppermute(joined(piece, wide), "frame", xor_pairs(frames, other * step))
    mine = joined(lax.dynamic_index_in_dim(held, place, 1, keepdims=False), wide)
    return pl.pallas_call(
        finish_kernel,
        out_shape=[
            array((1, own, columns)),
            array((1, own, columns)),
            array((3, 3)),
            array((21,)),
            array((1,)),
        ],
        in_specs=vmem(5),
        out_specs=vmem(5),
        compiler_params=little,
        name="finish",
    )(mine, gots[3], gots[2], gots[1], small)


def solution(mesh):
    in_specs = (
        P(("groups", "frame"), ("map", "psf"), None),
        P(("groups", "frame"), ("map", "psf"), None),
        P(("groups", "frame"), ("map", "psf"), None),
        P(("groups", "map", "psf"), "frame", None),
        P(("groups", "map", "psf"), "frame", None),
        P("groups", None),
        P("groups"),
        P(("groups", "frame")),
        P(("groups", "frame")),
        P(("groups", "frame"), None),
    )
    out_specs = (
        P(("groups", "map", "psf"), "frame", None),
        P(("groups", "map", "psf"), "frame", None),
        P("groups", None),
        P("groups"),
        P(("groups", "frame")),
    )
    return jax.shard_map(local, mesh=mesh, in_specs=in_specs, out_specs=out_specs, check_vma=False)
```

```python
import math

import jax
import jax.numpy as jnp
import numpy as np
from jax import lax
from jax.experimental import pallas as pl
from jax.experimental.pallas import tpu as pltpu
from jax.sharding import PartitionSpec as P

NP = 256
HALF = NP // 2
NR = 16
OVERSAMPLE = 32
AMPLITUDE = 2.0
IPC_CENTER = 0.8
TURN = 2 * NP * OVERSAMPLE
FIELD_SCALE = (AMPLITUDE / NP**2) ** 2
GUARD = 8
ZERN_LANE, IPC_LANE, JITTER_LANE = 0, 32, 48
JITTER, SKY, ROW_START, COLUMN, KAPPA = range(5)

f32, bf16 = jnp.float32, jnp.bfloat16
MODES = [(p, d - p) for d in range(6) for p in range(d + 1)]


def sine_table():
    nodes = 0.125 + 0.125 * np.cos(np.pi * (np.arange(200) + 0.5) / 200)
    powers = np.stack([nodes ** (2 * k + 1) for k in range(5)], 1)
    return [float(c) for c in np.linalg.lstsq(powers, np.sin(2 * np.pi * nodes), rcond=None)[0]]


SINE = sine_table()


def sin_quarter(y):
    t = y * y
    poly = SINE[4]
    for c in SINE[3::-1]:
        poly = poly * t + c
    return poly * y


def cos_turn(x):
    return sin_quarter(0.25 - jnp.abs(x))


def sin_turn(x):
    return sin_quarter(jnp.minimum(jnp.maximum(x, -0.5 - x), 0.5 - x))


def turn_fraction(k):
    return (((k + TURN // 2) & (TURN - 1)) - TURN // 2).astype(f32) * (1.0 / TURN)


def iota(shape, axis):
    return lax.broadcasted_iota(jnp.int32, shape, axis)


def mm(a, b):
    return jnp.dot(a, b, preferred_element_type=f32)


def mm_nt(a, b):
    return lax.dot_general(a, b, (((1,), (1,)), ((), ())), preferred_element_type=f32)


def halves(x):
    high = x.astype(bf16)
    return high, (x - high.astype(f32)).astype(bf16)


def dot_blur(x, high, low):
    half = high.shape[0]
    left, right = x[:, :half], x[:, half:]
    rows = x.shape[0]
    both = dot_split(jnp.concatenate([left, right], 0), high[:, half : 2 * half], low[:, half : 2 * half])
    first = both[:rows] + dot_split(right, high[:, :half], low[:, :half])
    last = both[rows:] + dot_split(left, high[:, 2 * half :], low[:, 2 * half :])
    return jnp.concatenate([first, last], 1)


def dot_split(x, high, low, product=mm):
    rows = x.shape[0]
    top = x.astype(bf16)
    both = jnp.concatenate([top.astype(f32), x - top.astype(f32)], 0).astype(bf16)
    first = product(both, high)
    return first[:rows] + first[rows:] + product(top, low)


def pupil_kernel(
    zern_ref,
    level_ref,
    dither_ref,
    ipc_ref,
    scalar_ref,
    fold_hi,
    fold_lo,
    *,
    rows,
    columns,
):
    blocks = lax.axis_size(("map", "psf"))
    row_start = lax.axis_index(("map", "psf")) * rows - rows * blocks // 2 - dither_ref[:, 0:1]
    column = columns // 2 + dither_ref[:, 1:2]
    values = [level_ref[:, 0:1], level_ref[:, 1:2], row_start.astype(f32), column.astype(f32)]
    values += [
        ipc_ref[i : i + 1, j : j + 1] + (IPC_CENTER if i == j == 1 else 0.0)
        for i in range(3)
        for j in range(3)
    ]
    for k, value in enumerate(values):
        scalar_ref[k : k + 1, :] = jnp.broadcast_to(value, (1, columns))
    z = {
        mode: jnp.broadcast_to(zern_ref[:, k : k + 1], (16, HALF)) for k, mode in enumerate(MODES)
    }

    def pupil_step(step, carry):
        at = pl.multiple_of(step * 16, 16)
        j = iota((16, HALF), 0) + at
        l = iota((16, HALF), 1)
        u = (2 * j + 1).astype(f32) * (1.0 / NP)
        v = (2 * l + 1).astype(f32) * (1.0 / NP)
        uu, vv = u * u, v * v
        ee = (
            z[0, 0]
            + vv * (z[0, 2] + vv * z[0, 4])
            + uu * (z[2, 0] + vv * z[2, 2] + uu * z[4, 0])
        )
        oe = u * (
            z[1, 0]
            + vv * (z[1, 2] + vv * z[1, 4])
            + uu * (z[3, 0] + vv * z[3, 2] + uu * z[5, 0])
        )
        eo = v * (
            z[0, 1]
            + vv * (z[0, 3] + vv * z[0, 5])
            + uu * (z[2, 1] + vv * z[2, 3] + uu * z[4, 1])
        )
        oo = u * v * (z[1, 1] + vv * z[1, 3] + uu * z[3, 1])
        radius = uu + vv
        open_ = jnp.where((radius <= 1.0) & (radius >= 0.09), 1.0, 0.0).astype(f32)
        even, odd = (ee + eo, oe + oo), (ee - eo, oe - oo)
        phases = (even[0] + even[1], even[0] - even[1], odd[0] + odd[1], odd[0] - odd[1])
        real, imag = [], []
        for phase in phases:
            turns = phase * (0.5 / math.pi)
            turns = turns - jnp.floor(turns + 0.5)
            real.append(open_ * cos_turn(turns))
            imag.append(open_ * sin_turn(turns))

        def folds(x):
            a, b, c, d = x[0] + x[1], x[0] - x[1], x[2] + x[3], x[2] - x[3]
            return a + c, a - c, b + d, b - d

        ree, reo, roe, roo = folds(real)
        iee, ieo, ioe, ioo = folds(imag)
        for first, parts in ((0, (ree, iee, reo, ieo)), (HALF, (ioe, -roe, ioo, -roo))):
            for k, part in enumerate(parts):
                high, low = halves(part)
                fold_hi[pl.ds(first + at, 16), k * HALF : (k + 1) * HALF] = high
                fold_lo[pl.ds(first + at, 16), k * HALF : (k + 1) * HALF] = low
        return carry

    lax.fori_loop(0, HALF // 16, pupil_step, 0, unroll=True)


def field_kernel(
    scalar_ref,
    observed_any,
    mask_any,
    count_any,
    fold_hi,
    fold_lo,
    observed_ref,
    weight_ref,
    image_ref,
    width_ref,
    field_ref,
    power_ref,
    norm_ref,
    blur_hi,
    blur_lo,
    col_hi,
    col_lo,
    wide_hi,
    wide_lo,
    observed_in,
    mask_in,
    count_in,
    sems,
    *,
    rows,
    columns,
    all_frames,
):
    spread_rows = rows + GUARD
    copies = [
        pltpu.make_async_copy(source, target, sems.at[k])
        for k, (source, target) in enumerate(
            ((observed_any, observed_in), (mask_any, mask_in), (count_any, count_in))
        )
    ]
    for copy in copies:
        copy.start()

    def column_step(step, carry):
        at = pl.multiple_of(step * 16, 16)
        l = iota((16, columns), 0) + at
        c = iota((16, columns), 1) - scalar_ref[COLUMN : COLUMN + 1, :].astype(jnp.int32)
        x = turn_fraction((2 * l + 1) * c)
        high, low = halves(cos_turn(x))
        col_hi[pl.ds(at, 16), :] = high
        col_lo[pl.ds(at, 16), :] = low
        high, low = halves(sin_turn(x))
        col_hi[pl.ds(HALF + at, 16), :] = high
        col_lo[pl.ds(HALF + at, 16), :] = low
        return carry

    lax.fori_loop(0, HALF // 16, column_step, 0, unroll=True)

    jitter = scalar_ref[JITTER : JITTER + 1, :HALF]
    falloff = 0.5 / (jitter * jitter)
    falloff = jnp.concatenate([falloff] * (3 * columns // (2 * HALF) + 1), 1)

    half = columns // 2

    def blur_step(step, carry):
        total, wide_total = carry
        at = pl.multiple_of(step * 16, 16)
        shape = (16, 3 * half + HALF)
        d = (iota(shape, 0) + at - iota(shape, 1) + (half + HALF)).astype(f32)
        exponent = d * d * falloff
        value = jnp.exp(-exponent)
        wide = value * (exponent + exponent)
        held = []
        for table, refs in ((value, (blur_hi, blur_lo)), (wide, (wide_hi, wide_lo))):
            parts = halves(table)
            for ref, part in zip(refs, parts):
                ref[pl.ds(at, 16), :] = part[:, HALF:]
                ref[pl.ds(HALF + at, 16), :] = part[:, : 3 * half]
            held.append(parts[0].astype(f32) + parts[1].astype(f32))
        return total + held[0], wide_total + held[1]

    zero = jnp.zeros((16, 3 * half + HALF), f32)
    total, wide_total = lax.fori_loop(0, HALF // 16, blur_step, (zero, zero), unroll=True)
    total = total[:, HALF:] + total[:, : 3 * half]
    wide_total = wide_total[:, HALF:] + wide_total[:, : 3 * half]
    total = jnp.sum(total, 0, keepdims=True)
    wide_total = jnp.sum(wide_total, 0, keepdims=True)
    norm = 1.0 / (total[:, half:] + total[:, : 2 * half])
    mean = (wide_total[:, half:] + wide_total[:, : 2 * half]) * norm
    norm_ref[...] = jnp.broadcast_to(norm, (8, columns))

    i = iota((spread_rows, HALF), 0)
    i = jnp.where(i < rows + 4, i, i - spread_rows)
    n = i + scalar_ref[ROW_START : ROW_START + 1, :HALF].astype(jnp.int32)
    x = turn_fraction((2 * iota((spread_rows, HALF), 1) + 1) * n)
    cosine, sine = cos_turn(x), sin_turn(x)
    u = (2 * iota((spread_rows, HALF), 1) + 1).astype(f32) * (1.0 / NP)
    left = []
    for p in range(6):
        left.append(jnp.concatenate([sine, -cosine] if p % 2 else [cosine, sine], 1))
        cosine, sine = cosine * u, sine * u
    mid = dot_split(jnp.concatenate(left, 0), fold_hi[...], fold_lo[...])
    power_ref[...] = mid
    er, ei, odd_r, odd_i = (mid[:spread_rows, k * HALF : (k + 1) * HALF] for k in range(4))
    mid = jnp.concatenate(
        [jnp.concatenate([er, odd_i], 1), jnp.concatenate([ei, -odd_r], 1)], 0
    )
    field = dot_split(mid, col_hi[...], col_lo[...])
    field_ref[...] = field
    real, imag = field[:spread_rows], field[spread_rows:]
    intensity = (real * real + imag * imag) * FIELD_SCALE
    blurred = dot_blur(intensity, blur_hi, blur_lo)
    widened = dot_blur(intensity, wide_hi, wide_lo)
    image_ref[...] = blurred * norm + scalar_ref[SKY : SKY + 1, :]
    width_ref[...] = (widened - blurred * mean) * (norm / scalar_ref[JITTER : JITTER + 1, :])
    for copy in copies:
        copy.wait()
    observed_ref[...] = observed_in[0]
    scale = 1.0 / (NR * math.sqrt(all_frames))
    weight_ref[...] = (mask_in[0] * count_in[0]).astype(f32) * scale


def bfe_weights():
    table = np.zeros((5, 5))
    for i in range(5):
        for j in range(5):
            distance = (i - 2) ** 2 + (j - 2) ** 2
            if distance > 0:
                table[i, j] = 1.0 / distance
    total = table.sum()
    return {d: float(np.float32(1.0 / d / total)) for d in (1, 2, 4, 5, 8)}


BFE = bfe_weights()


def gradient_kernel(
    near_ref,
    beside_two,
    beside_one,
    scalar_ref,
    observed_ref,
    weight_ref,
    image_ref,
    width_ref,
    field_ref,
    power_ref,
    norm_ref,
    blur_hi,
    blur_lo,
    col_hi,
    col_lo,
    maps_ref,
    pay_ref,
    edge_ref,
    *,
    rows,
    columns,
):
    spread_rows = rows + GUARD
    lane = iota((spread_rows, columns), 1)

    def across(x, k):
        moved = pltpu.roll(x, (-k) % columns, 1)
        return jnp.where(lane < columns - k if k > 0 else lane >= -k, moved, 0.0)

    def down(x, k):
        return pltpu.roll(x, (-k) % spread_rows, 0)

    def curve(x):
        one = across(x, 1) + across(x, -1)
        two = across(x, 2) + across(x, -2)
        near = BFE[1] * x + BFE[2] * one + BFE[5] * two
        far = BFE[4] * x + BFE[5] * one + BFE[8] * two
        own = BFE[1] * one + BFE[4] * two - x
        return own + (down(near, 1) + down(near, -1)) + (down(far, 2) + down(far, -2))

    kappa = [
        [scalar_ref[KAPPA + 3 * i + j : KAPPA + 3 * i + j + 1, :] for j in range(3)]
        for i in range(3)
    ]
    block = lax.axis_index(("map", "psf"))
    after = jnp.where(block + 1 < lax.axis_size(("map", "psf")), 1.0, 0.0)
    ahead = jnp.where(block > 0, 1.0, 0.0)
    even = lax.rem(lax.axis_index("frame"), 2) == 0
    one, two = beside_one[...], beside_two[...]
    top = jnp.where(even, one, two) * after
    bottom = jnp.where(even, two, one) * ahead
    top = jnp.concatenate([top[:4], top[4:]], 1)
    bottom = jnp.concatenate([bottom[:4], bottom[4:]], 1)
    gap = jnp.zeros((6, columns), f32)
    flat = jnp.concatenate([near_ref[0], top[:3], gap[:2], bottom[:3]], 0)
    bfe = jnp.concatenate([near_ref[1], top[3:], gap, bottom[3:]], 0)
    image = image_ref[...]
    charge = flat * image
    curvature = curve(charge)
    factor = 1.0 + bfe * curvature
    spread = charge * factor
    taps = (across(spread, -1), spread, across(spread, 1))
    lines = [sum(kappa[i][j] * taps[j] for j in range(3)) for i in range(3)]
    detected = down(lines[0], -1) + lines[1] + down(lines[2], 1)
    resid = weight_ref[...] * (detected[:rows] - observed_ref[...])
    resid = jnp.concatenate([resid, jnp.zeros((GUARD, columns), f32)], 0)
    back = (across(resid, 1), resid, across(resid, -1))
    lines = [sum(kappa[i][j] * back[j] for j in range(3)) for i in range(3)]
    spread_grad = down(lines[0], 1) + lines[1] + down(lines[2], -1)
    shifted = (down(resid, 1), resid, down(resid, -1))
    sums = []
    for i in range(3):
        for j in range(3):
            sums.append(jnp.sum(shifted[i] * taps[j], 0, keepdims=True))
    charge_curve = spread_grad * charge
    charge_grad = spread_grad * factor + curve(charge_curve * bfe)
    bfe_grad = charge_curve * curvature
    flat_grad = charge_grad * image
    image_grad = charge_grad * flat
    sums.append(jnp.sum(image_grad * width_ref[...], 0, keepdims=True))
    lane8 = iota((8, HALF), 1)

    def placed(small, lines, places):
        pad = [jnp.zeros((-len(lines) % 8, HALF), f32)]
        totals = jnp.sum(jnp.concatenate(lines + pad, 0), 1, keepdims=True)
        for k, place in enumerate(places):
            small = jnp.where(lane8 == place, totals[k : k + 1, :], small)
        return small

    lines = []
    for line in sums:
        total = line[:, :HALF]
        for k in range(1, columns // HALF):
            total = total + line[:, k * HALF : (k + 1) * HALF]
        lines.append(total)
    places = [IPC_LANE + k for k in range(9)] + [JITTER_LANE]
    small = placed(jnp.zeros((8, HALF), f32), lines, places)
    maps_ref[0] = flat_grad[:rows]
    maps_ref[1] = bfe_grad[:rows]
    upper = jnp.concatenate([flat_grad[rows : rows + 3], bfe_grad[rows : rows + 1]], 0)
    lower = jnp.concatenate([flat_grad[rows + 5 :], bfe_grad[rows + 7 :]], 0)
    even = lax.rem(block, 2) == 0
    half = columns // 2
    for k, edge in enumerate((jnp.where(even, upper, lower), jnp.where(even, lower, upper))):
        edge = jnp.concatenate([edge[:, :half], edge[:, half:]], 0)
        if k:
            edge_ref[...] = edge
        else:
            pay_ref[:, :half] = edge

    scaled = image_grad * norm_ref[0:1, :] * (2.0 * FIELD_SCALE)
    light = dot_blur(scaled, blur_hi, blur_lo)
    field = field_ref[...] * jnp.concatenate([light, light], 0)
    mid = dot_split(field, col_hi[...], col_lo[...], mm_nt)
    cos_r, sin_r = mid[:spread_rows, :HALF], mid[:spread_rows, HALF:]
    cos_i, sin_i = mid[spread_rows:, :HALF], mid[spread_rows:, HALF:]
    moments = []
    for p in range(6):
        blocks = [
            power_ref[p * spread_rows : (p + 1) * spread_rows, k * HALF : (k + 1) * HALF]
            for k in range(4)
        ]
        for q in range(2):
            one, two = blocks[2 * q : 2 * q + 2]
            three, four = blocks[2 - 2 * q : 4 - 2 * q]
            if p % 2:
                term = (cos_i * two + cos_r * one) + (sin_r * four - sin_i * three)
            else:
                term = (cos_i * one - cos_r * two) + (sin_r * three + sin_i * four)
            moments.append(jnp.sum(term, 0, keepdims=True))
    v = (2 * iota((1, HALF), 1) + 1).astype(f32) * (1.0 / NP)
    powers = [jnp.ones((1, HALF), f32)]
    for _ in range(5):
        powers.append(powers[-1] * v)
    zern = [moments[2 * p + q % 2] * powers[q] for p, q in MODES]
    small = placed(small, zern, [ZERN_LANE + k for k in range(21)])
    pay_ref[:, half:] = small


def vmem(count):
    return [pl.BlockSpec(memory_space=pltpu.VMEM)] * count


def xor_pairs(count, mask):
    return [(i, i ^ mask) for i in range(count)]


def edge_rows(top, bottom):
    half = top.shape[-1] // 2
    edges = (
        jnp.concatenate([top[0, :3], top[1, :1]], 0),
        jnp.concatenate([bottom[0, -3:], bottom[1, -1:]], 0),
    )
    return [jnp.concatenate([edge[:, :half], edge[:, half:]], 0) for edge in edges]


def gather_maps(flat_map, bfe_map, rows, pupil_beside):
    own, columns = flat_map.shape[1:]
    frames = lax.axis_size("frame")
    blocks = lax.axis_size(("map", "psf"))
    held = jnp.concatenate([flat_map, bfe_map], 0)[:, None]
    index = lax.axis_index("frame")
    step = frames // 2
    while step:
        if step == 1:
            held = pupil_beside(held)
        other = lax.ppermute(held, "frame", xor_pairs(frames, step))
        before = held
        held = jnp.where(
            (index & step) == 0,
            jnp.stack([held, other], 2),
            jnp.stack([other, held], 2),
        ).reshape((2, -1, own, columns))
        step //= 2
    maps = held.reshape(2, rows, columns)
    even = (index & 1) == 0
    everywhere = ("frame", "map", "psf")
    if own == GUARD and frames == 4:
        first, last = edge_rows(before[:, 0], before[:, 1])
        tile = jnp.where(even, first, last)
        tiles = []
        for odd in (0, 1):
            pairs = []
            for f in range(frames):
                for b in range(blocks):
                    to = (b + 1 if f % 2 else b - 1) % blocks
                    pairs.append((f * blocks + b, (f ^ odd) * blocks + to))
            tiles.append(lax.ppermute(tile, everywhere, pairs))
        return maps, tiles
    first, last = edge_rows(maps, maps)
    after = lax.ppermute(first, ("map", "psf"), [(b + 1, b) for b in range(blocks - 1)])
    ahead = lax.ppermute(last, ("map", "psf"), [(b, b + 1) for b in range(blocks - 1)])
    return maps, [jnp.where(even, after, ahead), jnp.where(even, ahead, after)]


def edge_kernel(grads_ref, *refs):
    *got_refs, out_ref = refs
    rows, columns = grads_ref.shape[1:]
    block = lax.axis_index(("map", "psf"))
    half = columns // 2
    before = jnp.zeros((GUARD, half), f32)
    after = jnp.zeros((GUARD, half), f32)
    for k, got_ref in enumerate(got_refs):
        partner = block ^ (2 ** (k + 1) - 1)
        edge = got_ref[:, :half]
        before = jnp.where(partner == block - 1, edge, before)
        after = jnp.where(partner == block + 1, edge, after)
    before = jnp.concatenate([before[:4], before[4:]], 1)
    after = jnp.concatenate([after[:4], after[4:]], 1)
    out_ref[...] = grads_ref[...]
    out_ref[0, :3] += before[:3]
    out_ref[1, :1] += before[3:]
    out_ref[0, rows - 3 :] += after[:3]
    out_ref[1, rows - 1 :] += after[3:]


def finish_kernel(
    mine_ref, three_ref, two_ref, one_ref, small_ref, flat_ref, bfe_ref, ipc_ref, zern_ref, jitter_ref
):
    columns = flat_ref.shape[2]
    total = (mine_ref[...] + one_ref[...]) + (two_ref[...] + three_ref[...])
    flat_ref[0] = total[:, :columns]
    bfe_ref[0] = total[:, columns : 2 * columns]
    totals = total[:, 2 * columns :]
    zern_ref[...] = totals[0, ZERN_LANE : ZERN_LANE + 21]
    for i in range(3):
        first = IPC_LANE + 3 * i
        ipc_ref[i : i + 1, :] = totals[0:1, first : first + 3]
    jitter_ref[...] = small_ref[0, JITTER_LANE : JITTER_LANE + 1]


def local(
    observed,
    pixel_mask,
    ramp_counts,
    flat_map,
    bfe_map,
    ipc_kernel,
    zernike,
    jitter,
    sky_level,
    dither,
):
    _, rows, columns = observed.shape
    frames = lax.axis_size("frame")
    blocks = lax.axis_size(("map", "psf"))
    own = rows // frames
    spread_rows = rows + GUARD
    frame = lax.axis_index("frame")

    def array(shape, dtype=f32):
        return jax.ShapeDtypeStruct(shape, dtype)

    params = pltpu.CompilerParams(vmem_limit_bytes=16 * 2**20)
    little = pltpu.CompilerParams(vmem_limit_bytes=2 * 2**20)
    scalars, *fold = pl.pallas_call(
        lambda *refs: pupil_kernel(*refs, rows=rows, columns=columns),
        out_shape=[
            array((16, columns)),
            array((NP, 4 * HALF), bf16),
            array((NP, 4 * HALF), bf16),
        ],
        in_specs=vmem(4),
        out_specs=vmem(3),
        compiler_params=params,
        name="pupil",
    )(zernike[None], jnp.stack([jitter, sky_level], 1), dither, ipc_kernel)
    def pupil_beside(sent):
        nonlocal scalars
        sent, scalars = lax.optimization_barrier((sent, scalars))
        return sent

    maps, beside = gather_maps(flat_map, bfe_map, rows, pupil_beside)

    seen = pl.pallas_call(
        lambda *refs: field_kernel(*refs, rows=rows, columns=columns, all_frames=frames),
        out_shape=[
            array((rows, columns)),
            array((rows, columns)),
            array((spread_rows, columns)),
            array((spread_rows, columns)),
            array((2 * spread_rows, columns)),
            array((6 * spread_rows, 4 * HALF)),
            array((8, columns)),
            *[array((columns // 2, 3 * columns // 2), bf16)] * 2,
            *[array((NP, columns), bf16)] * 2,
        ],
        in_specs=vmem(1) + [pl.BlockSpec(memory_space=pltpu.HBM)] * 3 + vmem(2),
        out_specs=vmem(11),
        scratch_shapes=[
            pltpu.VMEM((columns // 2, 3 * columns // 2), bf16),
            pltpu.VMEM((columns // 2, 3 * columns // 2), bf16),
            pltpu.VMEM((1, rows, columns), f32),
            pltpu.VMEM((1, rows, columns), jnp.int32),
            pltpu.VMEM((1, rows, columns), jnp.int32),
            pltpu.SemaphoreType.DMA((3,)),
        ],
        compiler_params=params,
        name="field",
    )(scalars, observed, pixel_mask, ramp_counts, *fold)

    grads, pay, edge = pl.pallas_call(
        lambda *refs: gradient_kernel(*refs, rows=rows, columns=columns),
        out_shape=[
            array((2, rows, columns)),
            array((8, columns // 2 + HALF)),
            array((8, columns // 2)),
        ],
        in_specs=vmem(15),
        out_specs=vmem(3),
        compiler_params=params,
        name="gradient",
    )(maps, beside[1], beside[0], scalars, *seen)

    gots = []
    small = pay[:, columns // 2 :]
    step = 1
    while step < blocks:
        if gots:
            pay = jnp.concatenate([edge, small], 1)
        got = lax.ppermute(pay, ("map", "psf"), xor_pairs(blocks, 2 * step - 1))
        gots.append(got)
        small = small + got[:, columns // 2 :]
        step *= 2
    grads = pl.pallas_call(
        edge_kernel,
        out_shape=array((2, rows, columns)),
        in_specs=vmem(1 + len(gots)),
        out_specs=pl.BlockSpec(memory_space=pltpu.VMEM),
        compiler_params=little,
        name="edges",
    )(grads, *gots)

    held = grads.reshape(2, frames, own, columns)
    wide = small[:own]

    def joined(piece, wide):
        return jnp.concatenate([*piece.reshape(-1, own, columns), wide], 1)

    step = 1
    while 4 * step < frames:
        bit = (frame & step) != 0
        pieces = held.reshape((2, -1, 2) + held.shape[2:])
        mine = jnp.where(bit, pieces[:, :, 1], pieces[:, :, 0])
        theirs = jnp.where(bit, pieces[:, :, 0], pieces[:, :, 1])
        got = lax.ppermute(joined(theirs, wide), "frame", xor_pairs(frames, step))
        step *= 2
        count = 2 * mine.shape[1]
        other = jnp.stack([got[:, k * columns : (k + 1) * columns] for k in range(count)])
        held = mine + other.reshape(mine.shape)
        wide = wide + got[:, count * columns :]
    place = frame // step
    gots = {}
    for other in (3, 2, 1):
        piece = lax.dynamic_index_in_dim(held, place ^ other, 1, keepdims=False)
        gots[other] = lax.ppermute(joined(piece, wide), "frame", xor_pairs(frames, other * step))
    mine = joined(lax.dynamic_index_in_dim(held, place, 1, keepdims=False), wide)
    return pl.pallas_call(
        finish_kernel,
        out_shape=[
            array((1, own, columns)),
            array((1, own, columns)),
            array((3, 3)),
            array((21,)),
            array((1,)),
        ],
        in_specs=vmem(5),
        out_specs=vmem(5),
        compiler_params=little,
        name="finish",
    )(mine, gots[3], gots[2], gots[1], small)


def solution(mesh):
    in_specs = (
        P(("groups", "frame"), ("map", "psf"), None),
        P(("groups", "frame"), ("map", "psf"), None),
        P(("groups", "frame"), ("map", "psf"), None),
        P(("groups", "map", "psf"), "frame", None),
        P(("groups", "map", "psf"), "frame", None),
        P("groups", None),
        P("groups"),
        P(("groups", "frame")),
        P(("groups", "frame")),
        P(("groups", "frame"), None),
    )
    out_specs = (
        P(("groups", "map", "psf"), "frame", None),
        P(("groups", "map", "psf"), "frame", None),
        P("groups", None),
        P("groups"),
        P(("groups", "frame")),
    )
    return jax.shard_map(local, mesh=mesh, in_specs=in_specs, out_specs=out_specs, check_vma=False)
```
